32 devices in a mesh: dp: 8 (over z, x), expert: 4 (over y, core).
Axes of the slice: x: 2, y: 2, z: 4, core: 2. Of those that a mesh axis runs over, the one named last changes fastest.
Arguments:
- tokens: bfloat16 [32768, 512], P(('dp', 'expert')), may hold values from -6 to 6
- doc_lengths: int32 [32, 4], P(('dp', 'expert')), may hold values from 1 to 512, 1024 in all within a row
- group_order: int32 [32, 1024], P(('dp', 'expert')), may hold values from 0 to 1023, each once within a row
- ln1_gain: float32 [512], replicated, may hold values from 0.5 to 1.5
- w_query: bfloat16 [512, 512], replicated, may hold values from -0.25 to 0.25
- w_key: bfloat16 [512, 512], replicated, may hold values from -0.25 to 0.25
- w_value: bfloat16 [512, 512], replicated, may hold values from -0.25 to 0.25
- w_out: bfloat16 [512, 512], replicated, may hold values from -1 to 1
- ln2_gain: float32 [512], replicated, may hold values from 0.5 to 1.5
- w_control: bfloat16 [512, 8], replicated, may hold values from -0.1875 to 0.1875
- w_up: bfloat16 [8, 512, 2048], P('expert'), may hold values from -1.5 to 1.5
- w_down: bfloat16 [8, 2048, 512], P('expert'), may hold values from -2 to 2
- cotangent: bfloat16 [32768, 512], P(('dp', 'expert')), may hold values from -6 to 6
Outputs:
- output: bfloat16 [32768, 512], P(('dp', 'expert'))
- grad_tokens: bfloat16 [32768, 512], P(('dp', 'expert'))
- grad_ln1_gain: float32 [512], replicated
- grad_w_query: float32 [512, 512], replicated
- grad_w_key: float32 [512, 512], replicated
- grad_w_value: float32 [512, 512], replicated
- grad_w_out: float32 [512, 512], replicated
- grad_ln2_gain: float32 [512], replicated
- grad_w_control: float32 [512, 8], replicated
- grad_w_up: float32 [8, 512, 2048], P('expert', 'dp')
- grad_w_down: float32 [8, 2048, 512], P('expert', 'dp')
The draws below stay inside these ranges and needn't reach their ends.
Inputs may be any that keep to these rules, and one draw needn't show every extreme that they name: `doc_lengths`: each row holds the lengths of the 4 documents packed in order into one device's 1024 tokens; they sum to 1024 and the longest is exactly 512. `group_order`: each row is a permutation of one device's 1024 token places.
All inputs are finite; a program needn't handle non-finite values.
Results may differ from the reference program's by a relative error of at most 0.02.
Values may be sent and summed in bfloat16 or wider, within the bound.
No kernel may reach another device: no remote copies, remote signals or barrier semaphores. Data moves between devices by JAX's collectives and lax.ppermute only.
A program may use at most 256 MiB of HBM per device.

```python
import math
import jax
import jax.numpy as jnp
import numpy as np
from jax import lax

D = 512
HEADS = 8
HEAD_DIM = 64
FF = 2048
GROUP = 32
TOK_DEV = 1024
DOCS = 4
LONGEST = 512
EXPERTS = 8
TOKENS = 32768
N_DP = 8
N_EXPERT = 4


def levels(key, extent, cuts, least, largest):
    loudness, own = 1.0, jax.random.fold_in(key, 6)
    for position, parts in cuts:
        heights = jnp.exp(jax.random.uniform(jax.random.fold_in(own, position), (parts,), jnp.float32, least / len(cuts), largest / len(cuts)))
        loudness = loudness * jnp.repeat(heights, extent[position] // parts).reshape([-1 if axis == position else 1 for axis in range(len(extent))])
    return loudness


def profile(number_of, total, reach, slope):
    loads = [(1 << 20) // math.isqrt(standing ** slope) + 1 for standing in range(2, number_of + 1)]
    rest, holding = total - reach - (number_of - 1), [1] * (number_of - 1)
    while rest > 0:
        movable = [i for i in range(number_of - 1) if holding[i] < reach]
        whole, budget = sum([loads[i] for i in movable]), rest
        for i in movable:
            more = min(reach - holding[i], max(1, budget * loads[i] // whole), rest)
            holding[i] = holding[i] + more
            rest = rest - more
    return np.array([reach] + holding)


def uneven_parts(rng, amount, total, limit, skew):
    if amount == 2:
        one = jax.random.randint(rng, (), max(1, total - limit), min(limit, total - 1) + 1)
        return jnp.stack([one, total - one])
    tallies = jnp.asarray(profile(amount, total, limit, skew), jnp.int32)
    twos = (amount - 1) // 2
    source_of, receiver = tallies[1:1 + 2 * twos:2], tallies[2:2 + 2 * twos:2]
    slack = jnp.minimum(source_of - 1, limit - receiver)
    passed = jax.random.randint(jax.random.fold_in(rng, 1), (twos,), 0, 1 << 20) % (slack + 1)
    tallies = tallies.at[1:1 + 2 * twos:2].set(source_of - passed).at[2:2 + 2 * twos:2].set(receiver + passed)
    return tallies[jax.random.permutation(jax.random.fold_in(rng, 2), amount)]


def centred(rng, shape, scale, limit, split=(), kind=jnp.bfloat16):
    drawn = scale * jax.random.normal(rng, shape, jnp.float32)
    if split:
        drawn = drawn * levels(rng, shape, split, -0.22, 0.18)
    return jnp.clip(drawn, -limit, limit).astype(kind)


def setup_inputs(seed: int = 0) -> dict:
    key_list = jax.random.split(jax.random.key(seed), 14)
    return {
        "tokens": centred(key_list[0], (TOKENS, D), 1.0, 6.0, ((0, 32),)),
        "doc_lengths": jax.vmap(lambda own: uneven_parts(own, DOCS, TOK_DEV, LONGEST, 2))(jax.random.split(key_list[1], (N_DP * N_EXPERT))).reshape((N_DP * N_EXPERT, DOCS)).astype(jnp.int32),
        "group_order": jax.vmap(lambda own: jax.random.permutation(own, TOK_DEV))(jax.random.split(key_list[2], (N_DP * N_EXPERT))).reshape((N_DP * N_EXPERT, TOK_DEV)).astype(jnp.int32),
        "ln1_gain": jnp.clip(1.0 + 0.1 * jax.random.normal(key_list[3], (D,), jnp.float32), 0.5, 1.5),
        "w_query": centred(key_list[4], (D, D), D ** -0.5, 0.25),
        "w_key": centred(key_list[5], (D, D), D ** -0.5, 0.25),
        "w_value": centred(key_list[6], (D, D), D ** -0.5, 0.25),
        "w_out": centred(key_list[7], (D, D), (D // 16) ** -0.5, 1.0),
        "ln2_gain": jnp.clip(1.0 + 0.1 * jax.random.normal(key_list[8], (D,), jnp.float32), 0.5, 1.5),
        "w_control": centred(key_list[9], (D, EXPERTS), (2 * D) ** -0.5, 0.1875),
        "w_up": centred(key_list[10], (EXPERTS, D, FF), (D // GROUP) ** -0.5, 1.5, ((0, 4),)),
        "w_down": centred(key_list[11], (EXPERTS, FF, D), (max(FF * EXPERTS // (2 * GROUP * GROUP), 1)) ** -0.5, 2.0, ((0, 4),)),
        "cotangent": centred(key_list[12], (TOKENS, D), 1.0, 6.0, ((0, 32),)),
    }


HIGH = lax.Precision.HIGHEST
EPSILON = 1e-05
NEGATIVE = -1e+30

@jax.custom_vjp
def low(v):
    return lax.optimization_barrier(v.astype(jnp.bfloat16)).astype(jnp.float32)

@jax.custom_vjp
def low_back(v):
    return v

def low_keep(v):
    return (low(v), None)

def low_pass(kept, grad):
    return (grad,)

def back_keep(v):
    return (v, None)

def back_low(kept, grad):
    return (low(grad),)
low.defvjp(low_keep, low_pass)
low_back.defvjp(back_keep, back_low)

def product(left, right):
    return jnp.matmul(left, right, precision=HIGH)

def rounded(values):
    return low_back(low(values))

def normalize(values, norm_gain):
    center = values - lax.optimization_barrier(jnp.mean(values, axis=-1, keepdims=True))
    spread = lax.optimization_barrier(jnp.mean(center * center, axis=-1, keepdims=True))
    return center * lax.rsqrt(spread + EPSILON) * norm_gain

def activation(values):
    return jax.nn.gelu(values, approximate=True)

def device_forward(inputs, lengths, token_order, params):
    ln1_gain, w_query, w_key, w_value, w_out, ln2_gain, w_control, w_up, w_down = params
    row_count = inputs.shape[0]
    positions = jnp.arange(row_count, dtype=jnp.int32)
    doc_ends = jnp.cumsum(lengths.astype(jnp.int32))
    document = lax.optimization_barrier(jnp.sum((positions[:, None] >= doc_ends[None, :]).astype(jnp.int32), axis=1))
    allowed = (document[:, None] == document[None, :]) & (positions[None, :] <= positions[:, None])
    normed = low(normalize(inputs, ln1_gain))
    query_heads = rounded(product(normed, w_query)).reshape(row_count, HEADS, HEAD_DIM)
    key_heads = rounded(product(normed, w_key)).reshape(row_count, HEADS, HEAD_DIM)
    value_heads = rounded(product(normed, w_value)).reshape(row_count, HEADS, HEAD_DIM)
    scores = low_back(jnp.einsum('qhd,khd->hqk', query_heads, key_heads, precision=HIGH) * HEAD_DIM ** (-0.5))
    scores = jnp.where(allowed[None], scores, NEGATIVE)
    prob_low = low(jax.nn.softmax(scores, axis=-1))
    attended = rounded(jnp.einsum('hqk,khd->qhd', prob_low, value_heads, precision=HIGH).reshape(row_count, HEADS * HEAD_DIM))
    hidden = inputs + low_back(product(attended, w_out))
    second = low(normalize(hidden, ln2_gain))
    logits = low_back(product(second, w_control))
    groups = row_count // GROUP
    order_index = token_order.astype(jnp.int32)
    mix_low = low(jax.nn.softmax(logits[order_index].reshape(groups, GROUP, -1), axis=1))
    grouped = second[order_index].reshape(groups, GROUP, -1)
    mixed = rounded(jnp.einsum('gte,gtd->ged', mix_low, grouped, precision=HIGH))
    pre_act = low_back(jnp.einsum('ged,edf->gef', mixed, w_up, precision=HIGH))
    act_low = low(activation(pre_act))
    expert_out = rounded(jnp.einsum('gef,efd->ged', act_low, w_down, precision=HIGH))
    token_mix = jnp.einsum('gte,ged->gtd', mix_low, expert_out, precision=HIGH).reshape(row_count, -1)
    placed = jnp.zeros_like(token_mix).at[order_index].set(token_mix)
    return hidden + placed

def reference(tokens, doc_lengths, group_order, ln1_gain, w_query, w_key, w_value, w_out, ln2_gain, w_control, w_up, w_down, cotangent):
    blocks = doc_lengths.shape[0]
    inputs = tokens.astype(jnp.float32).reshape(blocks, TOK_DEV, D)
    params = (ln1_gain.astype(jnp.float32), w_query.astype(jnp.float32), w_key.astype(jnp.float32), w_value.astype(jnp.float32), w_out.astype(jnp.float32), ln2_gain.astype(jnp.float32), w_control.astype(jnp.float32), w_up.astype(jnp.float32), w_down.astype(jnp.float32))

    def whole(inputs_all, params_all):

        def one_block(item):
            return jax.checkpoint(device_forward)(item[0], item[1], item[2], params_all)
        return lax.map(one_block, (inputs_all, doc_lengths, group_order))
    output, pull_back = jax.vjp(whole, inputs, params)
    grad_inputs, grads = pull_back(cotangent.astype(jnp.float32).reshape(blocks, TOK_DEV, D))
    return (output.reshape(-1, D).astype(jnp.bfloat16), grad_inputs.reshape(-1, D).astype(jnp.bfloat16), grads[0], grads[1], grads[2], grads[3], grads[4], grads[5], grads[6], grads[7], grads[8])
```

```python
import functools

import jax
import jax.numpy as jnp
from jax import lax
from jax.experimental import pallas as pl
from jax.experimental.pallas import tpu as pltpu
from jax.sharding import PartitionSpec as P

D = 512
HEADS = 8
HEAD_DIM = 64
PAIRS = 4
PAIR = 2 * HEAD_DIM
GROUP = 32
EXP_DEV = 2
LONGEST = 512
BLOCK = 256
FF_BLOCK = 512
EPSILON = 1e-05
NEGATIVE = -1e30
MIB = 1 << 20

F32 = jnp.float32
LOW = jnp.bfloat16


def product(left, right):
    return jnp.dot(left, right, preferred_element_type=F32)


def product_nt(left, right):
    return lax.dot_general(left, right, (((1,), (1,)), ((), ())), preferred_element_type=F32)


def product_tn(left, right):
    return lax.dot_general(left, right, (((0,), (0,)), ((), ())), preferred_element_type=F32)


def standard(values):
    center = values - jnp.mean(values, axis=-1, keepdims=True)
    inverse = lax.rsqrt(jnp.mean(center * center, axis=-1, keepdims=True) + EPSILON)
    return center * inverse, inverse


def standard_pull(norm, inverse, grad):
    return (
        grad
        - jnp.mean(grad, axis=-1, keepdims=True)
        - norm * jnp.mean(grad * norm, axis=-1, keepdims=True)
    ) * inverse


def gelu_parts(values):
    square = values * values
    tanh = jnp.tanh(0.7978845608028654 * values * (1.0 + 0.044715 * square))
    half = 0.5 + 0.5 * tanh
    slope = half + values * (0.5 - 0.5 * tanh * tanh) * (
        0.7978845608028654 + 0.10703222440890037 * square
    )
    return values * half, slope


def three_parts(values):
    high = values.astype(LOW).astype(F32)
    rest = values - high
    middle = rest.astype(LOW).astype(F32)
    return high, middle, rest - middle


def forward_kernel(
    lengths,
    place,
    tok,
    cot,
    order,
    gain1,
    w_query,
    w_key,
    w_value,
    w_out,
    gain2,
    w_wide,
    send0,
    send1,
    send2,
    send3,
    hidden,
    mix,
    normed,
    queries,
    keys,
    values,
    attended,
    second,
    spread,
    mixed,
    pulled,
):
    rows_all = tok.shape[0]
    groups = rows_all // GROUP
    width = mix.shape[1]
    blocks = [pl.ds(start, BLOCK) for start in range(0, rows_all, BLOCK)]
    lane = lax.broadcasted_iota(jnp.int32, (BLOCK, PAIR), 1)
    upper = lane >= HEAD_DIM
    slot = lane % HEAD_DIM
    end0 = lengths[0, 0]
    end1 = end0 + lengths[0, 1]
    end2 = end1 + lengths[0, 2]
    ones = (slot >= 4) & (slot < 7)
    for number, rows in enumerate(blocks):
        norm, _ = standard(tok[rows, :].astype(F32))
        low = (norm * gain1[...]).astype(LOW)
        normed[rows, :] = low
        places = number * BLOCK + lax.broadcasted_iota(jnp.int32, (BLOCK, PAIR), 0)
        document = (
            (places >= end0).astype(jnp.int32)
            + (places >= end1).astype(jnp.int32)
            + (places >= end2).astype(jnp.int32)
        )
        same = slot == document
        key_marks = jnp.where(same | ones, 1.0, 0.0)
        value_marks = jnp.where(ones, 1.0, 0.0)
        query_marks = jnp.where((slot < 4) & ~same, NEGATIVE, 0.0)
        query = product(low, w_query[...]) * (HEAD_DIM ** (-0.5))
        key = product(low, w_key[...])
        value = product(low, w_value[...])
        for pair in range(PAIRS):
            cols = slice(pair * PAIR, (pair + 1) * PAIR)
            for half in range(2):
                mine = upper if half else ~upper
                head = 2 * pair + half
                queries[head, rows, :] = jnp.where(mine, query[:, cols], query_marks).astype(LOW)
                keys[head, rows, :] = jnp.where(mine, key[:, cols], key_marks).astype(LOW)
                values[head, rows, :] = jnp.where(mine, value[:, cols], value_marks).astype(LOW)

    triangle = lax.broadcasted_iota(jnp.int32, (BLOCK, BLOCK), 1) <= lax.broadcasted_iota(
        jnp.int32, (BLOCK, BLOCK), 0
    )

    def attend(pair, carry):
        for number, rows in enumerate(blocks):
            start = number * BLOCK
            first = max(0, start - LONGEST)
            outs = []
            for half in range(2):
                head = 2 * pair + half
                query = queries[head, rows, :]
                near = product_nt(query, keys[head, rows, :])
                near = jnp.where(triangle, near, NEGATIVE)
                top = jnp.max(near, axis=1, keepdims=True)
                if start > first:
                    past = pl.ds(first, start - first)
                    far = product_nt(query, keys[head, past, :])
                    top = jnp.maximum(top, jnp.max(far, axis=1, keepdims=True))
                out = product(jnp.exp(near - top).astype(LOW), values[head, rows, :])
                if start > first:
                    out = out + product(jnp.exp(far - top).astype(LOW), values[head, past, :])
                mark = 4 + HEAD_DIM * (1 - half)
                total = out[:, mark : mark + 1]
                outs.append(out * (1.0 / total))
                high, middle, rest = three_parts(-(top + jnp.log(total)))
                marks = jnp.where(
                    lane == mark, high, jnp.where(lane == mark + 1, middle, rest)
                ).astype(LOW)
                queries[head, rows, :] = jnp.where(
                    (lane >= mark) & (lane < mark + 3), marks, query
                )
            cols = pl.ds(pl.multiple_of(pair * PAIR, PAIR), PAIR)
            attended[rows, cols] = jnp.where(upper, outs[1], outs[0]).astype(LOW)
        return carry

    lax.fori_loop(0, PAIRS, attend, 0)

    place_group = lax.broadcasted_iota(jnp.int32, (rows_all, width), 0) // GROUP
    lane_group = lax.broadcasted_iota(jnp.int32, (rows_all, width), 1) % groups
    member = jnp.where(place_group == lane_group, 1.0, 0.0).astype(LOW)
    tops = []
    for number, rows in enumerate(blocks):
        state = tok[rows, :].astype(F32) + product(attended[rows, :], w_out[...])
        hidden[rows, :] = state
        norm, _ = standard(state)
        low = (norm * gain2[...]).astype(LOW)
        second[rows, :] = low
        logits = product(low, w_wide[...])
        places = number * BLOCK + lax.broadcasted_iota(jnp.int32, (BLOCK, rows_all), 0)
        hot = jnp.where(order[...] == places, 1.0, 0.0).astype(LOW)
        inside = product(hot, member)
        logits = jnp.where(inside > 0.5, logits, NEGATIVE)
        spread[rows, :] = logits
        tops.append(jnp.max(logits, axis=0, keepdims=True))
    top = functools.reduce(jnp.maximum, tops)
    total = 0.0
    for rows in blocks:
        expo = jnp.exp(spread[rows, :] - top)
        spread[rows, :] = expo
        total = total + jnp.sum(expo, axis=0, keepdims=True)
    scale = 1.0 / total
    mixed_sum = 0.0
    pulled_sum = 0.0
    for rows in blocks:
        full = spread[rows, :] * scale
        mix[rows, :] = full
        low = full.astype(LOW)
        mixed_sum = mixed_sum + product_tn(low, second[rows, :])
        pulled_sum = pulled_sum + product_tn(low, cot[rows, :])
    mixed[...] = mixed_sum.astype(LOW)
    pulled[...] = pulled_sum.astype(LOW)
    share = EXP_DEV * groups
    for step, send in enumerate((send0, send1, send2, send3)):
        part = pl.ds(pl.multiple_of((place[0] ^ step) * share, share), share)
        send[:share, :] = mixed[part, :]
        send[share:, :] = pulled[part, :]


def expert_kernel(groups, in0, in1, in2, in3, up, down, out0, out1, out2, out3, result, pull):
    expert = pl.program_id(0)
    step = pl.program_id(1)
    share = EXP_DEV * groups
    ins = (in0, in1, in2, in3)
    outs = (out0, out1, out2, out3)
    part = pl.ds(pl.multiple_of(expert * groups, groups), groups)
    back = pl.ds(pl.multiple_of(share + expert * groups, groups), groups)
    taken = jnp.concatenate([ref[part, :] for ref in ins], axis=0)
    given = jnp.concatenate([ref[back, :] for ref in ins], axis=0)
    act, slope = gelu_parts(product(taken, up[0]))
    grad = (product_nt(given, down[0]) * slope).astype(LOW)
    forward = product(act.astype(LOW), down[0])
    backward = product_nt(grad, up[0])

    @pl.when(step == 0)
    def _():
        result[...] = forward
        pull[...] = backward

    @pl.when(step > 0)
    def _():
        result[...] += forward
        pull[...] += backward

    @pl.when(step == pl.num_programs(1) - 1)
    def _():
        for number, ref in enumerate(outs):
            own = slice(number * groups, (number + 1) * groups)
            ref[part, :] = result[own, :].astype(LOW)
            ref[back, :] = pull[own, :].astype(LOW)


def middle_kernel(
    place,
    ret0,
    ret1,
    ret2,
    ret3,
    hidden,
    cot,
    mix,
    attended,
    w_out,
    w_wide,
    gain2,
    output,
    grad_hidden,
    pulls,
    grad_out,
    grad_small,
    result,
    pull,
    second,
    inner,
    grad_attn,
):
    rows_all = hidden.shape[0]
    groups = rows_all // GROUP
    share = EXP_DEV * groups
    blocks = [pl.ds(start, BLOCK) for start in range(0, rows_all, BLOCK)]
    lane = lax.broadcasted_iota(jnp.int32, (BLOCK, PAIR), 1)
    upper = lane >= HEAD_DIM
    slot = lane % HEAD_DIM
    crossed = (lax.broadcasted_iota(jnp.int32, (PAIR, PAIR), 0) >= HEAD_DIM) != (
        lax.broadcasted_iota(jnp.int32, (PAIR, PAIR), 1) >= HEAD_DIM
    )
    crossing = jnp.where(crossed, -1.0, 0.0).astype(LOW)
    for step, ret in enumerate((ret0, ret1, ret2, ret3)):
        part = pl.ds(pl.multiple_of((place[0] ^ step) * share, share), share)
        result[part, :] = ret[:share, :]
        pull[part, :] = ret[share:, :]
    total = 0.0
    for rows in blocks:
        state = hidden[rows, :]
        norm, _ = standard(state)
        low = (norm * gain2[...]).astype(LOW)
        second[rows, :] = low
        full = mix[rows, :]
        output[rows, :] = (state + product(full.astype(LOW), result[...])).astype(LOW)
        grad_mix = product_nt(cot[rows, :], result[...]) + product_nt(low, pull[...])
        weighted = full * grad_mix
        inner[rows, :] = weighted
        total = total + jnp.sum(weighted, axis=0, keepdims=True)
    control = 0.0
    gain = 0.0
    for rows in blocks:
        full = mix[rows, :]
        grad_logits = (inner[rows, :] - full * total).astype(LOW)
        grad_second = product(full.astype(LOW), pull[...]) + product_nt(grad_logits, w_wide[...])
        control = control + product_tn(grad_logits, second[rows, :])
        norm, inverse = standard(hidden[rows, :])
        gain = gain + jnp.sum(grad_second * norm, axis=0, keepdims=True)
        grad_state = cot[rows, :].astype(F32) + standard_pull(
            norm, inverse, grad_second * gain2[...]
        )
        grad_hidden[rows, :] = grad_state
        low = grad_state.astype(LOW)
        grad_attn[rows, :] = low
        grad_att = product_nt(low, w_out[...]).astype(LOW).astype(F32)
        shared = grad_att * attended[rows, :].astype(F32)
        for pair in range(PAIRS):
            cols = slice(pair * PAIR, (pair + 1) * PAIR)
            top = shared[:, cols].astype(LOW)
            rest = (shared[:, cols] - top.astype(F32)).astype(LOW)
            delta = product(top, crossing) + product(rest, crossing)
            high, middle, last = three_parts(delta)
            marks = jnp.where(
                slot == 4,
                high,
                jnp.where(slot == 5, middle, jnp.where(slot == 6, last, 0.0)),
            )
            for half in range(2):
                mine = upper if half else ~upper
                pulls[2 * pair + half, rows, :] = jnp.where(mine, grad_att[:, cols], marks).astype(
                    LOW
                )
    grad_out[...] = product_tn(attended[...], grad_attn[...]).astype(LOW)
    experts = control.shape[0] // groups
    grad_small[:experts, :] = jnp.sum(control.reshape(experts, groups, D), axis=1)
    grad_small[experts:, :] = jnp.broadcast_to(gain, (grad_small.shape[0] - experts, D))


def pair_kernel(queries, keys, values, pulls, normed, grads, weights, grad_query):
    rows_all = queries.shape[1]
    lane = lax.broadcasted_iota(jnp.int32, (BLOCK, PAIR), 1)
    upper = lane >= HEAD_DIM
    triangle = lax.broadcasted_iota(jnp.int32, (BLOCK, BLOCK), 0) <= lax.broadcasted_iota(
        jnp.int32, (BLOCK, BLOCK), 1
    )
    started = set()
    for start in range(0, rows_all, BLOCK):
        rows = pl.ds(start, BLOCK)
        last = min(rows_all, start + BLOCK + LONGEST)
        grad_keys, grad_values = [], []
        query_parts = {}
        for half in range(2):
            key = keys[half, rows, :]
            value = values[half, rows, :]
            grad_key = 0.0
            grad_value = 0.0
            for query_start in range(start, last, BLOCK):
                part = pl.ds(query_start, BLOCK)
                query = queries[half, part, :]
                back = pulls[half, part, :]
                scores = product_nt(key, query)
                if query_start == start:
                    scores = jnp.where(triangle, scores, NEGATIVE)
                probs = jnp.exp(scores)
                grad_scores = (probs * product_nt(value, back)).astype(LOW)
                grad_value = grad_value + product(probs.astype(LOW), back)
                grad_key = grad_key + product(grad_scores, query)
                query_parts[half, query_start] = product_tn(grad_scores, key)
            grad_keys.append(grad_key)
            grad_values.append(grad_value)
        grads[rows, PAIR : 2 * PAIR] = jnp.where(upper, grad_keys[1], grad_keys[0]).astype(LOW)
        grads[rows, 2 * PAIR :] = jnp.where(upper, grad_values[1], grad_values[0]).astype(LOW)
        for query_start in range(start, last, BLOCK):
            part = pl.ds(query_start, BLOCK)
            both = jnp.where(upper, query_parts[1, query_start], query_parts[0, query_start])
            if query_start in started:
                grad_query[part, :] += both
            else:
                grad_query[part, :] = both
                started.add(query_start)
    grads[:, :PAIR] = (grad_query[...] * (HEAD_DIM ** (-0.5))).astype(LOW)
    weights[...] = product_tn(normed[...], grads[...]).astype(LOW)


def last_kernel(
    grads0, grads1, grads2, grads3, tok, grad_hidden, gain1, w_query, w_key, w_value, grad_tokens, grad_gain
):
    rows_all = tok.shape[0]
    gain = 0.0
    for start in range(0, rows_all, BLOCK):
        rows = pl.ds(start, BLOCK)
        parts = [ref[rows, :] for ref in (grads0, grads1, grads2, grads3)]
        grad_normed = 0.0
        for number, weight in enumerate((w_query, w_key, w_value)):
            cols = slice(number * PAIR, (number + 1) * PAIR)
            joined = jnp.concatenate([part[:, cols] for part in parts], axis=1)
            grad_normed = grad_normed + product_nt(joined, weight[...])
        norm, inverse = standard(tok[rows, :].astype(F32))
        gain = gain + jnp.sum(grad_normed * norm, axis=0, keepdims=True)
        grad_tokens[rows, :] = (
            grad_hidden[rows, :] + standard_pull(norm, inverse, grad_normed * gain1[...])
        ).astype(LOW)
    grad_gain[...] = jnp.broadcast_to(gain, grad_gain.shape)


def weight_kernel(groups, gathered, up, down, grad_up, grad_down):
    expert = pl.program_id(0)
    rows = gathered.shape[0] * groups
    taken = gathered[:, pl.ds(pl.multiple_of(expert * groups, groups), groups), :].reshape(rows, D)
    given = gathered[
        :, pl.ds(pl.multiple_of((EXP_DEV + expert) * groups, groups), groups), :
    ].reshape(rows, D)
    act, slope = gelu_parts(product(taken, up[0]))
    grad = (product_nt(given, down[0]) * slope).astype(LOW)
    grad_down[0] = product_tn(act.astype(LOW), given)
    grad_up[:, 0] = product_tn(taken, grad).astype(LOW).reshape(grad_up.shape[0], -1, grad.shape[1])


def vmem():
    return pl.BlockSpec(memory_space=pltpu.VMEM)


def smem():
    return pl.BlockSpec(memory_space=pltpu.SMEM)


def shape(*sizes, kind=LOW):
    return jax.ShapeDtypeStruct(sizes, kind)


def params(mib):
    return pltpu.CompilerParams(vmem_limit_bytes=mib * MIB)


def cost(flops, moved):
    return pl.CostEstimate(flops=int(flops), bytes_accessed=int(moved), transcendentals=0)


def all_reduce(part, axes, count):
    rows, cols = part.shape
    pieces = lax.all_to_all(
        part.reshape(count, rows // count, cols), axes, 0, 0, tiled=True
    )
    own = jnp.sum(pieces.astype(F32), axis=0).astype(LOW)
    spread = jnp.broadcast_to(own[None], (count, rows // count, cols))
    return lax.all_to_all(spread, axes, 0, 0, tiled=True).reshape(rows, cols)


def shards(
    tokens,
    doc_lengths,
    group_order,
    ln1_gain,
    w_query,
    w_key,
    w_value,
    w_out,
    ln2_gain,
    w_control,
    w_up,
    w_down,
    cotangent,
):
    rows = tokens.shape[0]
    hosts = lax.axis_size("expert")
    copies = lax.axis_size("dp")
    groups = rows // GROUP
    experts = hosts * EXP_DEV
    share = EXP_DEV * groups
    ff = w_up.shape[2]
    place = lax.axis_index("expert").astype(jnp.int32).reshape(1)
    gain1 = ln1_gain.reshape(1, D)
    gain2 = ln2_gain.reshape(1, D)
    w_wide = jnp.repeat(w_control, groups, axis=1)

    heads = shape(HEADS, rows, PAIR)
    with jax.named_scope("attention_and_mixing"):
        forward = pl.pallas_call(
            forward_kernel,
            in_specs=[smem()] * 2 + [vmem()] * 10,
            out_specs=[vmem()] * 11,
            out_shape=[shape(2 * share, D)] * 4
            + [
                shape(rows, D, kind=F32),
                shape(rows, experts * groups, kind=F32),
                shape(rows, D),
                heads,
                heads,
                heads,
                shape(rows, D),
            ],
            scratch_shapes=[
                pltpu.VMEM((rows, D), LOW),
                pltpu.VMEM((rows, experts * groups), F32),
                pltpu.VMEM((experts * groups, D), LOW),
                pltpu.VMEM((experts * groups, D), LOW),
            ],
            compiler_params=params(48),
            cost_estimate=cost(1e10, 2e7),
        )(
            doc_lengths,
            place,
            tokens,
            cotangent,
            group_order,
            gain1,
            w_query,
            w_key,
            w_value,
            w_out,
            gain2,
            w_wide,
        )
    sends = forward[:4]
    hidden, mix, normed, queries, keys, values, attended = forward[4:]

    def exchange(parts):
        return [parts[0]] + [
            lax.ppermute(parts[step], "expert", [(i, i ^ step) for i in range(hosts)])
            for step in range(1, hosts)
        ]

    with jax.named_scope("to_experts"):
        arrived = exchange(sends)
    with jax.named_scope("gather_for_weights"):
        gathered = lax.all_gather(
            jnp.stack(arrived), "dp", axis=0, tiled=True
        )
    with jax.named_scope("experts"):
        piece = pl.BlockSpec((2 * share, D), lambda e, f: (0, 0))
        results = pl.pallas_call(
            functools.partial(expert_kernel, groups),
            grid=(EXP_DEV, ff // FF_BLOCK),
            in_specs=[piece] * 4
            + [
                pl.BlockSpec((1, D, FF_BLOCK), lambda e, f: (e, 0, f)),
                pl.BlockSpec((1, FF_BLOCK, D), lambda e, f: (e, f, 0)),
            ],
            out_specs=[piece] * 4,
            out_shape=[shape(2 * share, D)] * 4,
            scratch_shapes=[pltpu.VMEM((hosts * groups, D), F32)] * 2,
            compiler_params=params(32),
            cost_estimate=cost(4e9, 1e7),
        )(*arrived, w_up, w_down)
    with jax.named_scope("from_experts"):
        returned = exchange(results)
    with jax.named_scope("mixing_backward"):
        output, grad_hidden, pulls, grad_out, grad_small = pl.pallas_call(
            middle_kernel,
            in_specs=[smem()] + [vmem()] * 11,
            out_specs=[vmem()] * 5,
            out_shape=[
                shape(rows, D),
                shape(rows, D, kind=F32),
                heads,
                shape(D, D),
                shape(16, D, kind=F32),
            ],
            scratch_shapes=[
                pltpu.VMEM((experts * groups, D), LOW),
                pltpu.VMEM((experts * groups, D), LOW),
                pltpu.VMEM((rows, D), LOW),
                pltpu.VMEM((rows, experts * groups), F32),
                pltpu.VMEM((rows, D), LOW),
            ],
            compiler_params=params(48),
            cost_estimate=cost(6e9, 1.5e7),
        )(place, *returned, hidden, cotangent, mix, attended, w_out, w_wide, gain2)

    axes = ("dp", "expert")
    count = copies * hosts
    with jax.named_scope("reduce_out"):
        sum_out = all_reduce(grad_out, axes, count)
    grads, sums = [], []
    for pair in range(PAIRS):
        with jax.named_scope("attention_backward"):
            half = pl.BlockSpec((2, rows, PAIR), lambda i, pair=pair: (pair, 0, 0))
            whole = pl.BlockSpec((rows, D), lambda i: (0, 0))
            grad, weights = pl.pallas_call(
                pair_kernel,
                grid=(1,),
                in_specs=[half] * 4 + [whole],
                out_specs=[
                    pl.BlockSpec((rows, 3 * PAIR), lambda i: (0, 0)),
                    pl.BlockSpec((D, 3 * PAIR), lambda i: (0, 0)),
                ],
                out_shape=[shape(rows, 3 * PAIR), shape(D, 3 * PAIR)],
                scratch_shapes=[pltpu.VMEM((rows, PAIR), F32)],
                compiler_params=params(32),
                cost_estimate=cost(5e9, 5e6),
            )(queries, keys, values, pulls, normed)
        grads.append(grad)
        if pair < PAIRS - 1:
            with jax.named_scope("reduce_pair"):
                sums.append(all_reduce(weights, axes, count))
    with jax.named_scope("norm_backward"):
        grad_tokens, grad_gain1 = pl.pallas_call(
            last_kernel,
            in_specs=[vmem()] * 10,
            out_specs=[vmem()] * 2,
            out_shape=[shape(rows, D), shape(8, D, kind=F32)],
            compiler_params=params(32),
            cost_estimate=cost(2e9, 8e6),
        )(*grads, tokens, grad_hidden, gain1, w_query, w_key, w_value)
    with jax.named_scope("reduce_last"):
        small = jnp.concatenate(
            (grad_small[: experts + 1], grad_gain1[:1], jnp.zeros((118, D), F32)), axis=0
        )
        joined = jnp.concatenate((weights, small.T.astype(LOW)), axis=1)
        sum_last = all_reduce(joined, axes, count)
    sums.append(sum_last[:, : 3 * PAIR])
    small = sum_last[:, 3 * PAIR :].astype(F32)
    with jax.named_scope("expert_weights"):
        strip = ff // copies
        mine = lax.axis_index("dp") * strip
        up_strip = lax.dynamic_slice(w_up, (0, 0, mine), (EXP_DEV, D, strip))
        down_strip = lax.dynamic_slice(w_down, (0, mine, 0), (EXP_DEV, strip, D))
        grad_up, grad_down = pl.pallas_call(
            functools.partial(weight_kernel, groups),
            grid=(EXP_DEV,),
            in_specs=[
                pl.BlockSpec((copies * hosts, 2 * share, D), lambda e: (0, 0, 0)),
                pl.BlockSpec((1, D, strip), lambda e: (e, 0, 0)),
                pl.BlockSpec((1, strip, D), lambda e: (e, 0, 0)),
            ],
            out_specs=[
                pl.BlockSpec((copies, 1, D // copies, strip), lambda e: (0, e, 0, 0)),
                pl.BlockSpec((1, strip, D), lambda e: (e, 0, 0)),
            ],
            out_shape=[
                shape(copies, EXP_DEV, D // copies, strip),
                shape(EXP_DEV, strip, D, kind=F32),
            ],
            compiler_params=params(60),
            cost_estimate=cost(3e9, 8e6),
        )(gathered, up_strip, down_strip)
        strips = lax.all_to_all(grad_up, "dp", 0, 0, tiled=True)
        grad_up = jnp.transpose(strips, (1, 2, 0, 3)).reshape(EXP_DEV, D // copies, ff).astype(F32)

    def joined_columns(number):
        cols = slice(number * PAIR, (number + 1) * PAIR)
        return jnp.concatenate([part[:, cols] for part in sums], axis=1).astype(F32)

    return (
        output,
        grad_tokens,
        small[:, experts + 1],
        joined_columns(0),
        joined_columns(1),
        joined_columns(2),
        sum_out.astype(F32),
        small[:, experts],
        small[:, :experts],
        grad_up,
        grad_down,
    )


def solution(mesh):
    return jax.shard_map(
        shards,
        mesh=mesh,
        in_specs=(
            P(("dp", "expert"), None),
            P(("dp", "expert"), None),
            P(("dp", "expert"), None),
            P(),
            P(),
            P(),
            P(),
            P(),
            P(),
            P(),
            P("expert", None, None),
            P("expert", None, None),
            P(("dp", "expert"), None),
        ),
        out_specs=(
            P(("dp", "expert"), None),
            P(("dp", "expert"), None),
            P(),
            P(),
            P(),
            P(),
            P(),
            P(),
            P(),
            P("expert", "dp", None),
            P("expert", "dp", None),
        ),
        check_vma=False,
    )
```

```python
import functools

import jax
import jax.numpy as jnp
from jax import lax
from jax.experimental import pallas as pl
from jax.experimental.pallas import tpu as pltpu
from jax.sharding import PartitionSpec as P

D = 512
HEADS = 8
HEAD_DIM = 64
PAIRS = 4
PAIR = 2 * HEAD_DIM
GROUP = 32
EXP_DEV = 2
LONGEST = 512
BLOCK = 256
FF_BLOCK = 512
EPSILON = 1e-05
NEGATIVE = -1e30
MIB = 1 << 20

F32 = jnp.float32
LOW = jnp.bfloat16


def product(left, right):
    return jnp.dot(left, right, preferred_element_type=F32)


def product_nt(left, right):
    return lax.dot_general(left, right, (((1,), (1,)), ((), ())), preferred_element_type=F32)


def product_tn(left, right):
    return lax.dot_general(left, right, (((0,), (0,)), ((), ())), preferred_element_type=F32)


def standard(values):
    center = values - jnp.mean(values, axis=-1, keepdims=True)
    inverse = lax.rsqrt(jnp.mean(center * center, axis=-1, keepdims=True) + EPSILON)
    return center * inverse, inverse


def standard_pull(norm, inverse, grad):
    return (
        grad
        - jnp.mean(grad, axis=-1, keepdims=True)
        - norm * jnp.mean(grad * norm, axis=-1, keepdims=True)
    ) * inverse


def gelu_parts(values):
    square = values * values
    tanh = jnp.tanh(0.7978845608028654 * values * (1.0 + 0.044715 * square))
    half = 0.5 + 0.5 * tanh
    slope = half + values * (0.5 - 0.5 * tanh * tanh) * (
        0.7978845608028654 + 0.10703222440890037 * square
    )
    return values * half, slope


def three_parts(values):
    high = values.astype(LOW).astype(F32)
    rest = values - high
    middle = rest.astype(LOW).astype(F32)
    return high, middle, rest - middle


def begin(copies):
    for copy in copies:
        copy.start()


def finish(copies):
    for copy in copies:
        copy.wait()


def loads(pairs, sems, first=0):
    return [
        pltpu.make_async_copy(source, target, sems.at[first + number])
        for number, (source, target) in enumerate(pairs)
    ]


def widened(w_control, width):
    experts = w_control.shape[1]
    lane = lax.broadcasted_iota(jnp.int32, (experts, width), 1) // (width // experts)
    row = lax.broadcasted_iota(jnp.int32, (experts, width), 0)
    return product(w_control[...], jnp.where(lane == row, 1.0, 0.0).astype(LOW)).astype(LOW)


def forward_kernel(
    lengths,
    place,
    order,
    gain1,
    gain2,
    w_control,
    tok_far,
    cot_far,
    w_query_far,
    w_key_far,
    w_value_far,
    w_out_far,
    send0,
    send1,
    send2,
    send3,
    hidden_far,
    mix_far,
    normed_far,
    queries_far,
    keys_far,
    values_far,
    attended_far,
    tok,
    cot,
    w_query,
    w_key,
    w_value,
    w_out,
    hidden,
    mix,
    normed,
    queries,
    keys,
    values,
    attended,
    second,
    spread,
    mixed,
    pulled,
    in_sems,
    out_sems,
):
    rows_all = tok.shape[0]
    groups = rows_all // GROUP
    width = mix.shape[1]
    ins = loads(
        [
            (tok_far, tok),
            (w_query_far, w_query),
            (w_key_far, w_key),
            (w_value_far, w_value),
            (w_out_far, w_out),
            (cot_far, cot),
        ],
        in_sems,
    )
    begin(ins)
    blocks = [pl.ds(start, BLOCK) for start in range(0, rows_all, BLOCK)]
    outs = loads(
        [(normed, normed_far), (keys, keys_far), (values, values_far), (mix, mix_far)], out_sems
    )
    state_outs = loads([(hidden.at[rows], hidden_far.at[rows]) for rows in blocks], out_sems, 4)

    def pair_outs(pair):
        first = 4 + len(blocks)
        two = pl.ds(2 * pair, 2)
        return [
            pltpu.make_async_copy(queries.at[two], queries_far.at[two], out_sems.at[first + pair])
        ]

    attended_out = pltpu.make_async_copy(
        attended, attended_far, out_sems.at[4 + len(blocks) + PAIRS]
    )
    lane = lax.broadcasted_iota(jnp.int32, (BLOCK, PAIR), 1)
    upper = lane >= HEAD_DIM
    slot = lane % HEAD_DIM
    end0 = lengths[0, 0]
    end1 = end0 + lengths[0, 1]
    end2 = end1 + lengths[0, 2]
    ones = (slot >= 4) & (slot < 7)
    finish(ins[:1])
    for number, rows in enumerate(blocks):
        norm, _ = standard(tok[rows, :].astype(F32))
        low = (norm * gain1[...]).astype(LOW)
        normed[rows, :] = low
        places = number * BLOCK + lax.broadcasted_iota(jnp.int32, (BLOCK, PAIR), 0)
        document = (
            (places >= end0).astype(jnp.int32)
            + (places >= end1).astype(jnp.int32)
            + (places >= end2).astype(jnp.int32)
        )
        same = slot == document
        key_marks = jnp.where(same | ones, 1.0, 0.0)
        value_marks = jnp.where(ones, 1.0, 0.0)
        query_marks = jnp.where((slot < 4) & ~same, NEGATIVE, 0.0)
        if number == 0:
            finish(ins[1:4])
        query = product(low, w_query[...]) * (HEAD_DIM ** (-0.5))
        key = product(low, w_key[...])
        value = product(low, w_value[...])
        for pair in range(PAIRS):
            cols = slice(pair * PAIR, (pair + 1) * PAIR)
            for half in range(2):
                mine = upper if half else ~upper
                head = 2 * pair + half
                queries[head, rows, :] = jnp.where(mine, query[:, cols], query_marks).astype(LOW)
                keys[head, rows, :] = jnp.where(mine, key[:, cols], key_marks).astype(LOW)
                values[head, rows, :] = jnp.where(mine, value[:, cols], value_marks).astype(LOW)
    begin(outs[:3])

    triangle = lax.broadcasted_iota(jnp.int32, (BLOCK, BLOCK), 1) <= lax.broadcasted_iota(
        jnp.int32, (BLOCK, BLOCK), 0
    )

    def attend(pair, carry):
        for number, rows in enumerate(blocks):
            start = number * BLOCK
            first = max(0, start - LONGEST)
            results = []
            for half in range(2):
                head = 2 * pair + half
                query = queries[head, rows, :]
                near = product_nt(query, keys[head, rows, :])
                near = jnp.where(triangle, near, NEGATIVE)
                top = jnp.max(near, axis=1, keepdims=True)
                if start > first:
                    past = pl.ds(first, start - first)
                    far = product_nt(query, keys[head, past, :])
                    top = jnp.maximum(top, jnp.max(far, axis=1, keepdims=True))
                out = product(jnp.exp(near - top).astype(LOW), values[head, rows, :])
                if start > first:
                    out = out + product(jnp.exp(far - top).astype(LOW), values[head, past, :])
                mark = 4 + HEAD_DIM * (1 - half)
                total = out[:, mark : mark + 1]
                results.append(out * (1.0 / total))
                high, middle, rest = three_parts(-(top + jnp.log(total)))
                marks = jnp.where(
                    lane == mark, high, jnp.where(lane == mark + 1, middle, rest)
                ).astype(LOW)
                queries[head, rows, :] = jnp.where(
                    (lane >= mark) & (lane < mark + 3), marks, query
                )
            cols = pl.ds(pl.multiple_of(pair * PAIR, PAIR), PAIR)
            attended[rows, cols] = jnp.where(upper, results[1], results[0]).astype(LOW)
        begin(pair_outs(pair))
        return carry

    lax.fori_loop(0, PAIRS, attend, 0)
    begin([attended_out])
    finish(ins[4:])

    place_group = lax.broadcasted_iota(jnp.int32, (rows_all, width), 0) // GROUP
    lane_group = lax.broadcasted_iota(jnp.int32, (rows_all, width), 1) % groups
    member = jnp.where(place_group == lane_group, 1.0, 0.0).astype(LOW)
    w_wide = widened(w_control, width)
    tops = []
    for number, rows in enumerate(blocks):
        state = tok[rows, :].astype(F32) + product(attended[rows, :], w_out[...])
        hidden[rows, :] = state
        begin(state_outs[number : number + 1])
        norm, _ = standard(state)
        low = (norm * gain2[...]).astype(LOW)
        second[rows, :] = low
        logits = product(low, w_wide)
        places = number * BLOCK + lax.broadcasted_iota(jnp.int32, (BLOCK, rows_all), 0)
        hot = jnp.where(order[...] == places, 1.0, 0.0).astype(LOW)
        inside = product(hot, member)
        logits = jnp.where(inside > 0.5, logits, NEGATIVE)
        spread[rows, :] = logits
        tops.append(jnp.max(logits, axis=0, keepdims=True))
    top = functools.reduce(jnp.maximum, tops)
    total = 0.0
    for rows in blocks:
        expo = jnp.exp(spread[rows, :] - top)
        spread[rows, :] = expo
        total = total + jnp.sum(expo, axis=0, keepdims=True)
    scale = 1.0 / total
    mixed_sum = 0.0
    pulled_sum = 0.0
    for rows in blocks:
        full = spread[rows, :] * scale
        mix[rows, :] = full
        low = full.astype(LOW)
        mixed_sum = mixed_sum + product_tn(low, second[rows, :])
        pulled_sum = pulled_sum + product_tn(low, cot[rows, :])
    begin(outs[3:])
    mixed[...] = mixed_sum.astype(LOW)
    pulled[...] = pulled_sum.astype(LOW)
    share = EXP_DEV * groups
    for step, send in enumerate((send0, send1, send2, send3)):
        part = pl.ds(pl.multiple_of((place[0] ^ step) * share, share), share)
        send[:share, :] = mixed[part, :]
        send[share:, :] = pulled[part, :]
    finish(outs)
    finish(state_outs)
    for pair in range(PAIRS):
        finish(pair_outs(pair))
    finish([attended_out])


def expert_kernel(groups, in0, in1, in2, in3, up, down, out0, out1, out2, out3, result, pull):
    expert = pl.program_id(0)
    step = pl.program_id(1)
    share = EXP_DEV * groups
    ins = (in0, in1, in2, in3)
    outs = (out0, out1, out2, out3)
    part = pl.ds(pl.multiple_of(expert * groups, groups), groups)
    back = pl.ds(pl.multiple_of(share + expert * groups, groups), groups)
    taken = jnp.concatenate([ref[part, :] for ref in ins], axis=0)
    given = jnp.concatenate([ref[back, :] for ref in ins], axis=0)
    act, slope = gelu_parts(product(taken, up[0]))
    grad = (product_nt(given, down[0]) * slope).astype(LOW)
    forward = product(act.astype(LOW), down[0])
    backward = product_nt(grad, up[0])

    @pl.when(step == 0)
    def _():
        result[...] = forward
        pull[...] = backward

    @pl.when(step > 0)
    def _():
        result[...] += forward
        pull[...] += backward

    @pl.when(step == pl.num_programs(1) - 1)
    def _():
        for number, ref in enumerate(outs):
            own = slice(number * groups, (number + 1) * groups)
            ref[part, :] = result[own, :].astype(LOW)
            ref[back, :] = pull[own, :].astype(LOW)


def middle_kernel(
    place,
    near,
    ret0,
    ret1,
    ret2,
    ret3,
    gain2,
    w_control,
    hidden_far,
    cot_far,
    mix_far,
    attended_far,
    w_out_far,
    output_far,
    grad_hidden_far,
    pulls_far,
    mine_out,
    other_out,
    hidden,
    cot,
    mix,
    attended,
    w_out,
    output,
    grad_hidden,
    pulls,
    result,
    pull,
    second,
    inner,
    grad_attn,
    grad_out,
    in_sems,
    out_sems,
):
    rows_all = hidden.shape[0]
    groups = rows_all // GROUP
    share = EXP_DEV * groups
    blocks = [pl.ds(start, BLOCK) for start in range(0, rows_all, BLOCK)]
    ins = loads(
        [
            (mix_far, mix),
            (hidden_far, hidden),
            (cot_far, cot),
            (w_out_far, w_out),
            (attended_far, attended),
        ],
        in_sems,
    )
    begin(ins)
    outs = loads([(output.at[rows], output_far.at[rows]) for rows in blocks], out_sems)
    state_outs = loads(
        [(grad_hidden.at[rows], grad_hidden_far.at[rows]) for rows in blocks],
        out_sems,
        len(blocks),
    )
    pull_outs = loads(
        [(pulls.at[:, rows], pulls_far.at[:, rows]) for rows in blocks],
        out_sems,
        2 * len(blocks),
    )
    lane = lax.broadcasted_iota(jnp.int32, (BLOCK, PAIR), 1)
    upper = lane >= HEAD_DIM
    slot = lane % HEAD_DIM
    crossed = (lax.broadcasted_iota(jnp.int32, (PAIR, PAIR), 0) >= HEAD_DIM) != (
        lax.broadcasted_iota(jnp.int32, (PAIR, PAIR), 1) >= HEAD_DIM
    )
    crossing = jnp.where(crossed, -1.0, 0.0).astype(LOW)
    for step, ret in enumerate((ret0, ret1, ret2, ret3)):
        part = pl.ds(pl.multiple_of((place[0] ^ step) * share, share), share)
        result[part, :] = ret[:share, :]
        pull[part, :] = ret[share:, :]
    finish(ins[:3])
    total = 0.0
    for number, rows in enumerate(blocks):
        state = hidden[rows, :]
        norm, _ = standard(state)
        low = (norm * gain2[...]).astype(LOW)
        second[rows, :] = low
        full = mix[rows, :]
        output[rows, :] = (state + product(full.astype(LOW), result[...])).astype(LOW)
        begin(outs[number : number + 1])
        grad_mix = product_nt(cot[rows, :], result[...]) + product_nt(low, pull[...])
        weighted = full * grad_mix
        inner[rows, :] = weighted
        total = total + jnp.sum(weighted, axis=0, keepdims=True)
    finish(ins[3:])
    w_wide = widened(w_control, mix.shape[1])
    control = 0.0
    gain = 0.0
    for number, rows in enumerate(blocks):
        full = mix[rows, :]
        grad_logits = (inner[rows, :] - full * total).astype(LOW)
        grad_second = product(full.astype(LOW), pull[...]) + product_nt(grad_logits, w_wide)
        control = control + product_tn(grad_logits, second[rows, :])
        norm, inverse = standard(hidden[rows, :])
        gain = gain + jnp.sum(grad_second * norm, axis=0, keepdims=True)
        grad_state = cot[rows, :].astype(F32) + standard_pull(
            norm, inverse, grad_second * gain2[...]
        )
        grad_hidden[rows, :] = grad_state
        begin(state_outs[number : number + 1])
        low = grad_state.astype(LOW)
        grad_attn[rows, :] = low
        grad_att = product_nt(low, w_out[...]).astype(LOW).astype(F32)
        shared = grad_att * attended[rows, :].astype(F32)
        for pair in range(PAIRS):
            cols = slice(pair * PAIR, (pair + 1) * PAIR)
            top = shared[:, cols].astype(LOW)
            rest = (shared[:, cols] - top.astype(F32)).astype(LOW)
            delta = product(top, crossing) + product(rest, crossing)
            high, middle, last = three_parts(delta)
            marks = jnp.where(
                slot == 4,
                high,
                jnp.where(slot == 5, middle, jnp.where(slot == 6, last, 0.0)),
            )
            for half in range(2):
                mine = upper if half else ~upper
                pulls[2 * pair + half, rows, :] = jnp.where(mine, grad_att[:, cols], marks).astype(
                    LOW
                )
        begin(pull_outs[number : number + 1])
    grad_out[:, :D] = product_tn(attended[...], grad_attn[...]).astype(LOW)
    experts = control.shape[0] // groups
    small = jnp.concatenate(
        (
            jnp.sum(control.reshape(experts, groups, D), axis=1),
            jnp.broadcast_to(gain, (PAIR - experts, D)),
        ),
        axis=0,
    )
    grad_out[:, D:] = small.T.astype(LOW)
    half = D // 2
    mine_out[...] = grad_out[pl.ds(pl.multiple_of(near[0] * half, half), half), :]
    other_out[...] = grad_out[pl.ds(pl.multiple_of((1 - near[0]) * half, half), half), :]
    finish(outs)
    finish(state_outs)
    finish(pull_outs)


def pair_kernel(
    pair_first,
    near,
    queries_far,
    keys_far,
    values_far,
    pulls_far,
    normed_far,
    grads_far,
    mine_out,
    other_out,
    queries,
    keys,
    values,
    pulls,
    normed,
    grads,
    grad_query,
    weights,
    in_sems,
    out_sems,
):
    rows_all = queries.shape[1]
    count = grads.shape[0]
    lane = lax.broadcasted_iota(jnp.int32, (BLOCK, PAIR), 1)
    upper = lane >= HEAD_DIM
    triangle = lax.broadcasted_iota(jnp.int32, (BLOCK, BLOCK), 0) <= lax.broadcasted_iota(
        jnp.int32, (BLOCK, BLOCK), 1
    )
    ins = []
    for pair in range(count):
        near_two = pl.ds(2 * pair, 2)
        far_two = pl.ds(2 * (pair_first + pair), 2)
        ins.append(
            loads(
                [
                    (far.at[far_two], close.at[near_two])
                    for far, close in (
                        (keys_far, keys),
                        (queries_far, queries),
                        (values_far, values),
                        (pulls_far, pulls),
                    )
                ],
                in_sems,
                4 * pair,
            )
        )
        begin(ins[-1])
    norm_in = pltpu.make_async_copy(normed_far, normed, in_sems.at[4 * count])
    norm_in.start()
    outs = loads([(grads.at[pair], grads_far.at[pair]) for pair in range(count)], out_sems)
    for pair in range(count):
        finish(ins[pair])
        started = set()
        for start in range(0, rows_all, BLOCK):
            rows = pl.ds(start, BLOCK)
            last = min(rows_all, start + BLOCK + LONGEST)
            grad_keys, grad_values = [], []
            query_parts = {}
            for half in range(2):
                head = 2 * pair + half
                key = keys[head, rows, :]
                value = values[head, rows, :]
                grad_key = 0.0
                grad_value = 0.0
                for query_start in range(start, last, BLOCK):
                    part = pl.ds(query_start, BLOCK)
                    query = queries[head, part, :]
                    back = pulls[head, part, :]
                    scores = product_nt(key, query)
                    if query_start == start:
                        scores = jnp.where(triangle, scores, NEGATIVE)
                    probs = jnp.exp(scores)
                    grad_scores = (probs * product_nt(value, back)).astype(LOW)
                    grad_value = grad_value + product(probs.astype(LOW), back)
                    grad_key = grad_key + product(grad_scores, query)
                    query_parts[half, query_start] = product_tn(grad_scores, key)
                grad_keys.append(grad_key)
                grad_values.append(grad_value)
            grads[pair, rows, PAIR : 2 * PAIR] = jnp.where(
                upper, grad_keys[1], grad_keys[0]
            ).astype(LOW)
            grads[pair, rows, 2 * PAIR :] = jnp.where(upper, grad_values[1], grad_values[0]).astype(
                LOW
            )
            for query_start in range(start, last, BLOCK):
                part = pl.ds(query_start, BLOCK)
                both = jnp.where(upper, query_parts[1, query_start], query_parts[0, query_start])
                if query_start in started:
                    grad_query[part, :] += both
                else:
                    grad_query[part, :] = both
                    started.add(query_start)
        grads[pair, :, :PAIR] = (grad_query[...] * (HEAD_DIM ** (-0.5))).astype(LOW)
        begin(outs[pair : pair + 1])
        if pair == 0:
            norm_in.wait()
        cols = slice(pair * 3 * PAIR, (pair + 1) * 3 * PAIR)
        weights[:, cols] = product_tn(normed[...], grads[pair]).astype(LOW)
    half = D // 2
    mine_out[...] = weights[pl.ds(pl.multiple_of(near[0] * half, half), half), :]
    other_out[...] = weights[pl.ds(pl.multiple_of((1 - near[0]) * half, half), half), :]
    finish(outs)


def last_kernel(early, late, tok, grad_hidden, gain1, w_query, w_key, w_value, grad_tokens):
    parts = [ref[pair] for ref in (early, late) for pair in range(ref.shape[0])]
    grad_normed = 0.0
    for number, weight in enumerate((w_query, w_key, w_value)):
        cols = slice(number * PAIR, (number + 1) * PAIR)
        joined = jnp.concatenate([part[:, cols] for part in parts], axis=1)
        grad_normed = grad_normed + product_nt(joined, weight[...])
    norm, inverse = standard(tok[...].astype(F32))
    grad_tokens[...] = (
        grad_hidden[...] + standard_pull(norm, inverse, grad_normed * gain1[...])
    ).astype(LOW)


def weight_kernel(expert, count, place, *refs):
    pieces = refs[:count]
    up, down = refs[count : count + 2]
    grad_up, grad_down, taken, given, held = refs[-5:]
    step = pl.program_id(0)
    share = PAIR
    groups = share // (2 * EXP_DEV)
    strip_rows, strip_ff = grad_up.shape[1], grad_down.shape[1]
    first = place[0] * strip_rows
    wide = pl.multiple_of(first // PAIR * PAIR, PAIR)
    inside = pl.ds(pl.multiple_of(first % PAIR, strip_rows), strip_rows)

    @pl.when(step == 0)
    def _():
        filled = 0
        for piece in pieces:
            for start in range(0, piece.shape[0], share):
                target = pl.ds(filled, groups)
                taken[target, :] = piece[
                    start + expert * groups : start + (expert + 1) * groups, :
                ]
                back = start + (EXP_DEV + expert) * groups
                given[target, :] = piece[back : back + groups, :]
                filled += groups

    rows_all = taken.shape[0]
    size = min(512, rows_all)
    ff_first = place[0] * strip_ff
    owner = step == ff_first // FF_BLOCK
    total = 0.0
    acts = []
    for start in range(0, rows_all, size):
        rows = pl.ds(start, size)
        act, slope = gelu_parts(product(taken[rows, :], up[0]))
        grad = (product_nt(given[rows, :], down[0]) * slope).astype(LOW)
        total = total + product_tn(taken[rows, pl.ds(wide, PAIR)], grad)
        acts.append(act.astype(LOW))
    held[:PAIR, :] = total
    grad_up[0] = held[inside, :]

    @pl.when(owner)
    def _():
        whole = 0.0
        for number, act in enumerate(acts):
            whole = whole + product_tn(act, given[pl.ds(number * size, size), :])
        held[...] = whole
        grad_down[0] = held[pl.ds(pl.multiple_of(ff_first % FF_BLOCK, strip_ff), strip_ff), :]


def assemble_kernel(
    near,
    both_own,
    both_other,
    gain1,
    w_query,
    w_key,
    w_value,
    grad_query,
    grad_key,
    grad_value,
    grad_out,
    grad_control,
    gains,
    columns,
):
    half = D // 2
    experts = grad_control.shape[1]
    own = pl.ds(pl.multiple_of(near[0] * half, half), half)
    other = pl.ds(pl.multiple_of((1 - near[0]) * half, half), half)
    for rows, both in ((own, both_own), (other, both_other)):
        grad_out[rows, :] = both[:, :D].astype(F32)
        small = both[:, D : D + PAIR].astype(F32)
        grad_control[rows, :] = small[:, :experts]
        shared = 0.0
        for number, (target, weight) in enumerate(
            ((grad_query, w_query), (grad_key, w_key), (grad_value, w_value))
        ):
            for pair in range(PAIRS):
                first = D + PAIR + (3 * pair + number) * PAIR
                part = both[:, first : first + PAIR].astype(F32)
                cols = slice(pair * PAIR, (pair + 1) * PAIR)
                target[rows, cols] = part
                shared = shared + part * weight[rows, cols].astype(F32)
        lane = lax.broadcasted_iota(jnp.int32, (half, PAIR), 1)
        columns[rows, :] = jnp.where(
            lane == 0, jnp.sum(shared, axis=1, keepdims=True), small[:, experts : experts + 1]
        )
    turned = columns[...].T[:8, :]
    row = lax.broadcasted_iota(jnp.int32, turned.shape, 0)
    gains[...] = jnp.where(row == 0, turned / gain1[...], turned)


def vmem():
    return pl.BlockSpec(memory_space=pltpu.VMEM)


def smem():
    return pl.BlockSpec(memory_space=pltpu.SMEM)


def far():
    return pl.BlockSpec(memory_space=pltpu.HBM)


def shape(*sizes, kind=LOW):
    return jax.ShapeDtypeStruct(sizes, kind)


def params(mib):
    return pltpu.CompilerParams(vmem_limit_bytes=mib * MIB)


def cost(flops, moved):
    return pl.CostEstimate(flops=int(flops), bytes_accessed=int(moved), transcendentals=0)


def ring_of(count):
    order = list(range(0, count, 2)) + list(range(count - 1, 0, -2))
    ahead = [(order[i], order[(i + 1) % count]) for i in range(count)]
    return ahead, [(target, source) for source, target in ahead]


def dma(count):
    return pltpu.SemaphoreType.DMA((count,))


def forward_call(lengths, place, order, gain1, gain2, tokens, cot, weights, w_control, experts):
    rows = tokens.shape[0]
    groups = rows // GROUP
    wide = experts * groups
    blocks = rows // BLOCK
    heads = (HEADS, rows, PAIR)
    kept = [
        ((rows, D), F32),
        ((rows, wide), F32),
        ((rows, D), LOW),
        (heads, LOW),
        (heads, LOW),
        (heads, LOW),
        ((rows, D), LOW),
    ]
    results = pl.pallas_call(
        forward_kernel,
        in_specs=[smem()] * 2 + [vmem()] * 4 + [far()] * 6,
        out_specs=[vmem()] * 4 + [far()] * 7,
        out_shape=[shape(2 * EXP_DEV * groups, D)] * 4
        + [shape(*size, kind=kind) for size, kind in kept],
        scratch_shapes=[pltpu.VMEM((rows, D), LOW)] * 2
        + [pltpu.VMEM((D, D), LOW)] * 4
        + [pltpu.VMEM(*one) for one in kept]
        + [
            pltpu.VMEM((rows, D), LOW),
            pltpu.VMEM((rows, wide), F32),
            pltpu.VMEM((wide, D), LOW),
            pltpu.VMEM((wide, D), LOW),
            dma(6),
            dma(4 + blocks + PAIRS + 1),
        ],
        compiler_params=params(52),
        cost_estimate=cost(2e10, 2e7),
    )(lengths, place, order, gain1, gain2, w_control, tokens, cot, *weights)
    return results[:4], results[4:]


def expert_call(arrived, w_up, w_down):
    size, _ = arrived[0].shape
    groups = size // (2 * EXP_DEV)
    ff = w_up.shape[2]
    piece = pl.BlockSpec((size, D), lambda e, f: (0, 0))
    return pl.pallas_call(
        functools.partial(expert_kernel, groups),
        grid=(EXP_DEV, ff // FF_BLOCK),
        in_specs=[piece] * len(arrived)
        + [
            pl.BlockSpec((1, D, FF_BLOCK), lambda e, f: (e, 0, f)),
            pl.BlockSpec((1, FF_BLOCK, D), lambda e, f: (e, f, 0)),
        ],
        out_specs=[piece] * len(arrived),
        out_shape=[shape(size, D)] * len(arrived),
        scratch_shapes=[pltpu.VMEM((len(arrived) * groups, D), F32)] * 2,
        compiler_params=params(16),
        cost_estimate=cost(5e9, 1e7),
    )(*arrived, w_up, w_down)


def middle_call(place, near, returned, gain2, w_control, hidden, cot, mix, attended, w_out):
    rows, wide = mix.shape
    blocks = rows // BLOCK
    taken = [
        ((rows, D), F32),
        ((rows, D), LOW),
        ((rows, wide), F32),
        ((rows, D), LOW),
        ((D, D), LOW),
    ]
    made = [((rows, D), LOW), ((rows, D), F32), ((HEADS, rows, PAIR), LOW)]
    part = shape(D // 2, D + PAIR)
    return pl.pallas_call(
        middle_kernel,
        in_specs=[smem()] * 2 + [vmem()] * 6 + [far()] * 5,
        out_specs=[far()] * 3 + [vmem()] * 2,
        out_shape=[shape(*size, kind=kind) for size, kind in made] + [part, part],
        scratch_shapes=[pltpu.VMEM(*one) for one in taken + made]
        + [
            pltpu.VMEM((wide, D), LOW),
            pltpu.VMEM((wide, D), LOW),
            pltpu.VMEM((rows, D), LOW),
            pltpu.VMEM((rows, wide), F32),
            pltpu.VMEM((rows, D), LOW),
            pltpu.VMEM((D, D + PAIR), LOW),
            dma(5),
            dma(3 * blocks),
        ],
        compiler_params=params(52),
        cost_estimate=cost(8e9, 1.5e7),
    )(place, near, *returned, gain2, w_control, hidden, cot, mix, attended, w_out)


def pair_call(first, near, queries, keys, values, pulls, normed):
    rows = normed.shape[0]
    half = shape(D // 2, 6 * PAIR)
    return pl.pallas_call(
        functools.partial(pair_kernel, first),
        in_specs=[smem()] + [far()] * 5,
        out_specs=[far()] + [vmem()] * 2,
        out_shape=[shape(2, rows, 3 * PAIR), half, half],
        scratch_shapes=[pltpu.VMEM((4, rows, PAIR), LOW)] * 4
        + [
            pltpu.VMEM((rows, D), LOW),
            pltpu.VMEM((2, rows, 3 * PAIR), LOW),
            pltpu.VMEM((rows, PAIR), F32),
            pltpu.VMEM((D, 6 * PAIR), LOW),
            dma(9),
            dma(2),
        ],
        compiler_params=params(52),
        cost_estimate=cost(1.4e10, 8e6),
    )(near, queries, keys, values, pulls, normed)


def weight_call(expert, copy, pieces, w_up, w_down, copies, earlier):
    ff = w_up.shape[2]
    held = sum(piece.shape[0] for piece in pieces)
    every = held // (2 * EXP_DEV)
    whole = [pl.BlockSpec(one.shape, lambda f: (0, 0)) for one in pieces]
    return pl.pallas_call(
        functools.partial(weight_kernel, expert, len(pieces)),
        grid=(ff // FF_BLOCK,),
        in_specs=[smem()]
        + whole
        + [
            pl.BlockSpec((1, D, FF_BLOCK), lambda f: (expert, 0, f)),
            pl.BlockSpec((1, FF_BLOCK, D), lambda f: (expert, f, 0)),
        ]
        + [far()] * len(earlier),
        out_specs=[
            pl.BlockSpec((1, D // copies, FF_BLOCK), lambda f: (expert, 0, f)),
            pl.BlockSpec((1, ff // copies, D), lambda f: (expert, 0, 0)),
        ],
        out_shape=[
            shape(EXP_DEV, D // copies, ff, kind=F32),
            shape(EXP_DEV, ff // copies, D, kind=F32),
        ],
        scratch_shapes=[
            pltpu.VMEM((every, D), LOW),
            pltpu.VMEM((every, D), LOW),
            pltpu.VMEM((FF_BLOCK, D), F32),
        ],
        input_output_aliases={3 + len(pieces) + i: i for i in range(len(earlier))},
        compiler_params=params(52),
        cost_estimate=cost(1e10, 8e6),
    )(copy, *pieces, w_up, w_down, *earlier)


def last_call(grads_early, grads_late, tokens, grad_hidden, gain1, weights):
    rows = tokens.shape[0]
    row_block = lambda i: (i, 0)
    fixed = lambda i: (0, 0)
    return pl.pallas_call(
        last_kernel,
        grid=(rows // BLOCK,),
        in_specs=[pl.BlockSpec((2, BLOCK, 3 * PAIR), lambda i: (0, i, 0))] * 2
        + [pl.BlockSpec((BLOCK, D), row_block)] * 2
        + [pl.BlockSpec((1, D), fixed)]
        + [pl.BlockSpec((D, D), fixed)] * 3,
        out_specs=pl.BlockSpec((BLOCK, D), row_block),
        out_shape=shape(rows, D),
        compiler_params=params(52),
        cost_estimate=cost(2e9, 8e6),
    )(grads_early, grads_late, tokens, grad_hidden, gain1, *weights)


def assemble_call(near, both_own, both_other, gain1, weights, experts):
    square = shape(D, D, kind=F32)
    return pl.pallas_call(
        assemble_kernel,
        in_specs=[smem()] + [vmem()] * 6,
        out_specs=[vmem()] * 6,
        out_shape=[square] * 4 + [shape(D, experts, kind=F32), shape(8, D, kind=F32)],
        scratch_shapes=[pltpu.VMEM((D, PAIR), F32)],
        compiler_params=params(52),
        cost_estimate=cost(1e8, 6e6),
    )(near, both_own, both_other, gain1, *weights)


def in_order(*values):
    return lax.optimization_barrier(values)


def shards(
    tokens,
    doc_lengths,
    group_order,
    ln1_gain,
    w_query,
    w_key,
    w_value,
    w_out,
    ln2_gain,
    w_control,
    w_up,
    w_down,
    cotangent,
):
    copies, far_hosts, near_hosts = (lax.axis_size(name) for name in ("dp", "far", "near"))
    hosts = far_hosts * near_hosts
    hosts_axes = ("far", "near")
    axes = ("dp", "far")
    count = copies * far_hosts
    experts = hosts * EXP_DEV
    place = lax.axis_index(hosts_axes).astype(jnp.int32).reshape(1)
    near = lax.axis_index("near").astype(jnp.int32).reshape(1)
    copy = lax.axis_index("dp").astype(jnp.int32).reshape(1)
    gain1 = ln1_gain.reshape(1, D)
    gain2 = ln2_gain.reshape(1, D)
    weights = (w_query, w_key, w_value)
    ahead, behind = ring_of(copies)
    steps_left = copies // 2 - 1
    pieces = []

    def exchange(parts):
        return [parts[0]] + [
            lax.ppermute(parts[step], hosts_axes, [(i, i ^ step) for i in range(hosts)])
            for step in range(1, hosts)
        ]

    def pass_on(ahead_part, behind_part):
        return lax.ppermute(ahead_part, "dp", ahead), lax.ppermute(behind_part, "dp", behind)

    def next_step(moving):
        nonlocal steps_left
        pieces.extend(moving)
        steps_left -= 1
        if steps_left > 0:
            return pass_on(*moving)
        half = moving[0].shape[0] // 2
        return pass_on(moving[0][:half], moving[1][half:])

    def near_swap(values):
        return lax.ppermute(values, "near", [(i, i ^ 1) for i in range(near_hosts)])

    def plus(left, right):
        return (left.astype(F32) + right.astype(F32)).astype(LOW)

    def scatter(half):
        rows, cols = half.shape
        return lax.all_to_all(half.reshape(count, rows // count, cols), axes, 0, 0, tiled=True)

    def total_of(parts):
        own = jnp.sum(parts.astype(F32), axis=0).astype(LOW)
        return jnp.broadcast_to(own[None], parts.shape)

    def spread(own):
        return lax.all_to_all(own, axes, 0, 0, tiled=True).reshape(-1, own.shape[-1])

    with jax.named_scope("attention_and_mixing"):
        sends, kept = forward_call(
            doc_lengths,
            place,
            group_order,
            gain1,
            gain2,
            tokens,
            cotangent,
            (*weights, w_out),
            w_control,
            experts,
        )
        hidden, mix, normed, queries, keys, values, attended = kept
    with jax.named_scope("to_experts"):
        arrived = exchange(sends)
    with jax.named_scope("gather_for_weights"):
        own = jnp.concatenate(arrived, axis=0)
        pieces.append(own)
        moving = pass_on(own, own)
    with jax.named_scope("experts"):
        results = expert_call(arrived, w_up, w_down)
    with jax.named_scope("from_experts"):
        returned = exchange(results)
    with jax.named_scope("gather_for_weights"):
        returned, moving = in_order(returned, moving)
        moving = next_step(moving)
    with jax.named_scope("mixing_backward"):
        output, grad_hidden, pulls, mine_out, other_out = middle_call(
            place, near, returned, gain2, w_control, hidden, cotangent, mix, attended, w_out
        )
    with jax.named_scope("gather_for_weights"):
        pulls, other_out, moving = in_order(pulls, other_out, moving)
        moving = next_step(moving)
    with jax.named_scope("reduce_early"):
        swapped_out = near_swap(other_out)
    with jax.named_scope("attention_backward"):
        grads_early, mine_early, other_early = pair_call(
            0, near, queries, keys, values, pulls, normed
        )
        mine_early, other_early, moving, swapped_out = in_order(
            mine_early, other_early, moving, swapped_out
        )
    with jax.named_scope("reduce_early"):
        swapped = near_swap(other_early)
        early = jnp.concatenate((plus(mine_out, swapped_out), plus(mine_early, swapped)), axis=1)
    with jax.named_scope("gather_for_weights"):
        early, moving, later_queries = in_order(early, moving, queries)
        early = scatter(early)
        moving = next_step(moving)
    with jax.named_scope("attention_backward"):
        grads_late, mine_late, other_late = pair_call(
            2, near, later_queries, keys, values, pulls, normed
        )
        mine_late, other_late, early, moving = in_order(mine_late, other_late, early, moving)
        while steps_left > 0:
            moving = next_step(moving)
        pieces.extend(moving)
    with jax.named_scope("reduce_late"):
        late = plus(mine_late, near_swap(other_late))
    with jax.named_scope("reduce_early"):
        early = total_of(early)
        late, early, pieces = in_order(late, early, pieces)
    with jax.named_scope("reduce_late"):
        late = scatter(late)
    with jax.named_scope("expert_weights"):
        grads_expert = weight_call(0, copy, pieces, w_up, w_down, copies, ())
        late, grads_expert = in_order(late, grads_expert)
    with jax.named_scope("reduce_late"):
        late = total_of(late)
        late, early, grads_expert, grads_late = in_order(late, early, grads_expert, grads_late)
        both = spread(jnp.concatenate((early, late), axis=2))
    with jax.named_scope("expert_weights"):
        grad_up, grad_down = weight_call(1, copy, pieces, w_up, w_down, copies, grads_expert)
    with jax.named_scope("norm_backward"):
        grad_tokens = last_call(grads_early, grads_late, tokens, grad_hidden, gain1, weights)
        both, grad_up, grad_down, grad_tokens = in_order(both, grad_up, grad_down, grad_tokens)
    with jax.named_scope("reduce_late"):
        both_other = near_swap(both)
    with jax.named_scope("assemble"):
        grad_query, grad_key, grad_value, grad_out, grad_control, gains = assemble_call(
            near, both, both_other, gain1, weights, experts
        )
    return (
        output,
        grad_tokens,
        gains[0],
        grad_query,
        grad_key,
        grad_value,
        grad_out,
        gains[1],
        grad_control,
        grad_up,
        grad_down,
    )


def solution(mesh):
    copies, hosts = mesh.shape["dp"], mesh.shape["expert"]
    finer = jax.sharding.Mesh(mesh.devices.reshape(copies, hosts // 2, 2), ("dp", "far", "near"))
    every = P(("dp", "far", "near"), None)
    expert = P(("far", "near"), None, None)
    sliced = P(("far", "near"), "dp", None)
    return jax.shard_map(
        shards,
        mesh=finer,
        in_specs=(every,) * 3 + (P(),) * 7 + (expert,) * 2 + (every,),
        out_specs=(every,) * 2 + (P(),) * 7 + (sliced,) * 2,
        check_vma=False,
    )
```

```python
import functools

import jax
import jax.numpy as jnp
from jax import lax
from jax.experimental import pallas as pl
from jax.experimental.pallas import tpu as pltpu
from jax.sharding import PartitionSpec as P

D = 512
HEADS = 8
HEAD_DIM = 64
PAIRS = 4
PAIR = 2 * HEAD_DIM
GROUP = 32
EXP_DEV = 2
LONGEST = 512
BLOCK = 256
FF_BLOCK = 512
EPSILON = 1e-05
NEGATIVE = -1e30
MIB = 1 << 20

F32 = jnp.float32
LOW = jnp.bfloat16


def product(left, right):
    return jnp.dot(left, right, preferred_element_type=F32)


def product_nt(left, right):
    return lax.dot_general(left, right, (((1,), (1,)), ((), ())), preferred_element_type=F32)


def product_tn(left, right):
    return lax.dot_general(left, right, (((0,), (0,)), ((), ())), preferred_element_type=F32)


def standard(values):
    center = values - jnp.mean(values, axis=-1, keepdims=True)
    inverse = lax.rsqrt(jnp.mean(center * center, axis=-1, keepdims=True) + EPSILON)
    return center * inverse, inverse


def standard_pull(norm, inverse, grad):
    return (
        grad
        - jnp.mean(grad, axis=-1, keepdims=True)
        - norm * jnp.mean(grad * norm, axis=-1, keepdims=True)
    ) * inverse


def gelu_parts(values):
    square = values * values
    tanh = jnp.tanh(0.7978845608028654 * values * (1.0 + 0.044715 * square))
    half = 0.5 + 0.5 * tanh
    slope = half + values * (0.5 - 0.5 * tanh * tanh) * (
        0.7978845608028654 + 0.10703222440890037 * square
    )
    return values * half, slope


def three_parts(values):
    high = values.astype(LOW).astype(F32)
    rest = values - high
    middle = rest.astype(LOW).astype(F32)
    return high, middle, rest - middle


def begin(copies):
    for copy in copies:
        copy.start()


def finish(copies):
    for copy in copies:
        copy.wait()


def loads(pairs, sems, first=0):
    return [
        pltpu.make_async_copy(source, target, sems.at[first + number])
        for number, (source, target) in enumerate(pairs)
    ]


def widened(w_control, width):
    experts = w_control.shape[0]
    lane = lax.broadcasted_iota(jnp.int32, (experts, width), 1) // (width // experts)
    row = lax.broadcasted_iota(jnp.int32, (experts, width), 0)
    return product_tn(jnp.where(lane == row, 1.0, 0.0).astype(LOW), w_control[...]).astype(LOW)


def forward_kernel(
    place,
    lengths_far,
    order_far,
    gain1_far,
    gain2_far,
    w_control_far,
    tok_far,
    cot_far,
    w_query_far,
    w_key_far,
    w_value_far,
    w_out_far,
    send0,
    send1,
    send2,
    send3,
    hidden_far,
    mix_far,
    normed_far,
    queries_far,
    keys_far,
    values_far,
    attended_far,
    lengths,
    order,
    gain1,
    gain2,
    w_control,
    tok,
    cot,
    w_query,
    w_key,
    w_value,
    w_out,
    hidden,
    mix,
    normed,
    queries,
    keys,
    values,
    attended,
    second,
    spread,
    mixed,
    pulled,
    marked,
    in_sems,
    out_sems,
):
    rows_all = tok.shape[0]
    groups = rows_all // GROUP
    width = mix.shape[1]
    ins = loads(
        [
            (tok_far, tok),
            (gain1_far, gain1),
            (lengths_far, lengths),
            (w_query_far, w_query),
            (w_key_far, w_key),
            (w_value_far, w_value),
            (w_out_far, w_out),
            (gain2_far, gain2),
            (w_control_far, w_control),
            (order_far, order),
            (cot_far, cot),
        ],
        in_sems,
    )
    begin(ins)
    blocks = [pl.ds(start, BLOCK) for start in range(0, rows_all, BLOCK)]
    outs = loads(
        [(normed, normed_far), (keys, keys_far), (values, values_far), (mix, mix_far)], out_sems
    )
    state_outs = loads([(hidden.at[rows], hidden_far.at[rows]) for rows in blocks], out_sems, 4)

    def pair_outs(pair):
        first = 4 + len(blocks)
        two = pl.ds(2 * pair, 2)
        return [
            pltpu.make_async_copy(marked.at[two], queries_far.at[two], out_sems.at[first + pair])
        ]

    attended_out = pltpu.make_async_copy(
        attended, attended_far, out_sems.at[4 + len(blocks) + PAIRS]
    )
    lane = lax.broadcasted_iota(jnp.int32, (BLOCK, PAIR), 1)
    upper = lane >= HEAD_DIM
    slot = lane % HEAD_DIM
    finish(ins[:3])
    end0 = lengths[0, 0]
    end1 = end0 + lengths[0, 1]
    end2 = end1 + lengths[0, 2]
    ones = (slot >= 4) & (slot < 7)
    for number, rows in enumerate(blocks):
        norm, _ = standard(tok[rows, :].astype(F32))
        low = (norm * gain1[...]).astype(LOW)
        normed[rows, :] = low
        places = number * BLOCK + lax.broadcasted_iota(jnp.int32, (BLOCK, PAIR), 0)
        document = (
            (places >= end0).astype(jnp.int32)
            + (places >= end1).astype(jnp.int32)
            + (places >= end2).astype(jnp.int32)
        )
        same = slot == document
        key_marks = jnp.where(same | ones, 1.0, 0.0)
        value_marks = jnp.where(ones, 1.0, 0.0)
        query_marks = jnp.where((slot < 4) & ~same, NEGATIVE, 0.0)
        if number == 0:
            finish(ins[3:6])
        query = product(low, w_query[...]) * (HEAD_DIM ** (-0.5))
        key = product(low, w_key[...])
        value = product(low, w_value[...])
        for pair in range(PAIRS):
            cols = slice(pair * PAIR, (pair + 1) * PAIR)
            for half in range(2):
                mine = upper if half else ~upper
                head = 2 * pair + half
                queries[head, rows, :] = jnp.where(mine, query[:, cols], query_marks).astype(LOW)
                keys[head, rows, :] = jnp.where(mine, key[:, cols], key_marks).astype(LOW)
                values[head, rows, :] = jnp.where(mine, value[:, cols], value_marks).astype(LOW)
    begin(outs[:3])

    triangle = lax.broadcasted_iota(jnp.int32, (BLOCK, BLOCK), 1) <= lax.broadcasted_iota(
        jnp.int32, (BLOCK, BLOCK), 0
    )

    def attend(pair, carry):
        work = [(number, half) for number in range(len(blocks)) for half in range(2)]
        results = {}

        def score(item):
            number, half = item
            start = number * BLOCK
            first = max(0, start - LONGEST)
            head = 2 * pair + half
            query = queries[head, blocks[number], :]
            near = jnp.where(triangle, product_nt(query, keys[head, blocks[number], :]), NEGATIVE)
            far = None
            if start > first:
                far = product_nt(query, keys[head, pl.ds(first, start - first), :])
            return query, near, far

        def weigh(item, scored):
            query, near, far = scored
            top = jnp.max(near, axis=1, keepdims=True)
            if far is not None:
                top = jnp.maximum(top, jnp.max(far, axis=1, keepdims=True))
                far = jnp.exp(far - top).astype(LOW)
            return query, jnp.exp(near - top).astype(LOW), far, top

        def gather(item, weighed):
            number, half = item
            query, near, far, top = weighed
            start = number * BLOCK
            first = max(0, start - LONGEST)
            head = 2 * pair + half
            rows = blocks[number]
            out = product(near, values[head, rows, :])
            if far is not None:
                out = out + product(far, values[head, pl.ds(first, start - first), :])
            mark = 4 + HEAD_DIM * (1 - half)
            total = out[:, mark : mark + 1]
            results[item] = out * (1.0 / total)
            high, middle, rest = three_parts(-(top + jnp.log(total)))
            marks = jnp.where(
                lane == mark, high, jnp.where(lane == mark + 1, middle, rest)
            ).astype(LOW)
            marked[head, rows, :] = jnp.where((lane >= mark) & (lane < mark + 3), marks, query)

        scored, weighed = {}, {}
        for index in range(len(work) + 2):
            if index < len(work):
                scored[index] = score(work[index])
            if 1 <= index <= len(work):
                weighed[index - 1] = weigh(work[index - 1], scored[index - 1])
            if index >= 2:
                gather(work[index - 2], weighed[index - 2])
        cols = pl.ds(pl.multiple_of(pair * PAIR, PAIR), PAIR)
        for number, rows in enumerate(blocks):
            attended[rows, cols] = jnp.where(upper, results[number, 1], results[number, 0]).astype(
                LOW
            )
        begin(pair_outs(pair))
        return carry

    lax.fori_loop(0, PAIRS, attend, 0)
    begin([attended_out])
    finish(ins[6:])

    place_group = lax.broadcasted_iota(jnp.int32, (rows_all, width), 0) // GROUP
    lane_group = lax.broadcasted_iota(jnp.int32, (rows_all, width), 1) % groups
    member = jnp.where(place_group == lane_group, 1.0, 0.0).astype(LOW)
    w_wide = widened(w_control, width)
    tops = []
    for number, rows in enumerate(blocks):
        state = tok[rows, :].astype(F32) + product(attended[rows, :], w_out[...])
        hidden[rows, :] = state
        begin(state_outs[number : number + 1])
        norm, _ = standard(state)
        low = (norm * gain2[...]).astype(LOW)
        second[rows, :] = low
        logits = product_nt(low, w_wide)
        places = number * BLOCK + lax.broadcasted_iota(jnp.int32, (BLOCK, rows_all), 0)
        hot = jnp.where(order[...] == places, 1.0, 0.0).astype(LOW)
        inside = product(hot, member)
        logits = jnp.where(inside > 0.5, logits, NEGATIVE)
        spread[rows, :] = logits
        tops.append(jnp.max(logits, axis=0, keepdims=True))
    top = functools.reduce(jnp.maximum, tops)
    total = 0.0
    for rows in blocks:
        expo = jnp.exp(spread[rows, :] - top)
        spread[rows, :] = expo
        total = total + jnp.sum(expo, axis=0, keepdims=True)
    scale = 1.0 / total
    mixed_sum = 0.0
    pulled_sum = 0.0
    for rows in blocks:
        full = spread[rows, :] * scale
        mix[rows, :] = full
        low = full.astype(LOW)
        mixed_sum = mixed_sum + product_tn(low, second[rows, :])
        pulled_sum = pulled_sum + product_tn(low, cot[rows, :])
    begin(outs[3:])
    mixed[...] = mixed_sum.astype(LOW)
    pulled[...] = pulled_sum.astype(LOW)
    share = EXP_DEV * groups
    for step, send in enumerate((send0, send1, send2, send3)):
        part = pl.ds(pl.multiple_of((place[0] ^ step) * share, share), share)
        send[:share, :] = mixed[part, :]
        send[share:, :] = pulled[part, :]
    finish(outs)
    finish(state_outs)
    for pair in range(PAIRS):
        finish(pair_outs(pair))
    finish([attended_out])


def expert_kernel(in0, in1, in2, in3, up_far, down_far, out0, out1, out2, out3, up, down, sems):
    groups = in0.shape[0] // (2 * EXP_DEV)
    ff = up.shape[2]
    ins = (in0, in1, in2, in3)
    outs = (out0, out1, out2, out3)
    steps = [(expert, first) for expert in range(EXP_DEV) for first in range(0, ff, FF_BLOCK)]
    copies = []
    for number, (expert, first) in enumerate(steps):
        part = pl.ds(first, FF_BLOCK)
        copies.append(
            loads(
                [
                    (up_far.at[expert, :, part], up.at[expert, :, part]),
                    (down_far.at[expert, part], down.at[expert, part]),
                ],
                sems,
                2 * number,
            )
        )
        begin(copies[-1])
    result = pull = 0.0
    for number, (expert, first) in enumerate(steps):
        part = pl.ds(first, FF_BLOCK)
        own = slice(expert * groups, (expert + 1) * groups)
        back = slice((EXP_DEV + expert) * groups, (EXP_DEV + expert + 1) * groups)
        taken = jnp.concatenate([ref[own, :] for ref in ins], axis=0)
        given = jnp.concatenate([ref[back, :] for ref in ins], axis=0)
        finish(copies[number])
        act, slope = gelu_parts(product(taken, up[expert, :, part]))
        grad = (product_nt(given, down[expert, part, :]) * slope).astype(LOW)
        result = result + product(act.astype(LOW), down[expert, part, :])
        pull = pull + product_nt(grad, up[expert, :, part])
        if first + FF_BLOCK == ff:
            for host, ref in enumerate(outs):
                rows = slice(host * groups, (host + 1) * groups)
                ref[own, :] = result[rows].astype(LOW)
                ref[back, :] = pull[rows].astype(LOW)
            result = pull = 0.0


def middle_kernel(
    place,
    near,
    ret0,
    ret1,
    ret2,
    ret3,
    gain2_far,
    w_control_far,
    hidden_far,
    cot_far,
    mix_far,
    attended_far,
    w_out_far,
    output_far,
    grad_hidden_far,
    pulls_far,
    mine_out,
    other_out,
    gain2,
    w_control,
    hidden,
    cot,
    mix,
    attended,
    w_out,
    output,
    grad_hidden,
    pulls,
    result,
    pull,
    second,
    inner,
    grad_attn,
    grad_out,
    in_sems,
    out_sems,
):
    rows_all = hidden.shape[0]
    groups = rows_all // GROUP
    share = EXP_DEV * groups
    blocks = [pl.ds(start, BLOCK) for start in range(0, rows_all, BLOCK)]
    ins = loads(
        [
            (gain2_far, gain2),
            (w_control_far, w_control),
            (mix_far, mix),
            (hidden_far, hidden),
            (cot_far, cot),
            (w_out_far, w_out),
            (attended_far, attended),
        ],
        in_sems,
    )
    begin(ins)
    outs = loads([(output.at[rows], output_far.at[rows]) for rows in blocks], out_sems)
    state_outs = loads(
        [(grad_hidden.at[rows], grad_hidden_far.at[rows]) for rows in blocks],
        out_sems,
        len(blocks),
    )
    pull_outs = loads(
        [(pulls.at[:, rows], pulls_far.at[:, rows]) for rows in blocks],
        out_sems,
        2 * len(blocks),
    )
    lane = lax.broadcasted_iota(jnp.int32, (BLOCK, PAIR), 1)
    upper = lane >= HEAD_DIM
    slot = lane % HEAD_DIM
    crossed = (lax.broadcasted_iota(jnp.int32, (PAIR, PAIR), 0) >= HEAD_DIM) != (
        lax.broadcasted_iota(jnp.int32, (PAIR, PAIR), 1) >= HEAD_DIM
    )
    crossing = jnp.where(crossed, -1.0, 0.0).astype(LOW)
    for step, ret in enumerate((ret0, ret1, ret2, ret3)):
        part = pl.ds(pl.multiple_of((place[0] ^ step) * share, share), share)
        result[part, :] = ret[:share, :]
        pull[part, :] = ret[share:, :]
    finish(ins[:5])
    total = 0.0
    for number, rows in enumerate(blocks):
        state = hidden[rows, :]
        norm, _ = standard(state)
        low = (norm * gain2[...]).astype(LOW)
        second[rows, :] = low
        full = mix[rows, :]
        output[rows, :] = (state + product(full.astype(LOW), result[...])).astype(LOW)
        begin(outs[number : number + 1])
        grad_mix = product_nt(cot[rows, :], result[...]) + product_nt(low, pull[...])
        weighted = full * grad_mix
        inner[rows, :] = weighted
        total = total + jnp.sum(weighted, axis=0, keepdims=True)
    finish(ins[5:])
    w_wide = widened(w_control, mix.shape[1])
    control = 0.0
    gain = 0.0
    for number, rows in enumerate(blocks):
        full = mix[rows, :]
        grad_logits = (inner[rows, :] - full * total).astype(LOW)
        grad_second = product(full.astype(LOW), pull[...]) + product(grad_logits, w_wide)
        control = control + product_tn(grad_logits, second[rows, :])
        norm, inverse = standard(hidden[rows, :])
        gain = gain + jnp.sum(grad_second * norm, axis=0, keepdims=True)
        grad_state = cot[rows, :].astype(F32) + standard_pull(
            norm, inverse, grad_second * gain2[...]
        )
        grad_hidden[rows, :] = grad_state
        begin(state_outs[number : number + 1])
        low = grad_state.astype(LOW)
        grad_attn[rows, :] = low
        grad_att = product_nt(low, w_out[...]).astype(LOW).astype(F32)
        shared = grad_att * attended[rows, :].astype(F32)
        for pair in range(PAIRS):
            cols = slice(pair * PAIR, (pair + 1) * PAIR)
            top = shared[:, cols].astype(LOW)
            rest = (shared[:, cols] - top.astype(F32)).astype(LOW)
            delta = product(top, crossing) + product(rest, crossing)
            high, middle, last = three_parts(delta)
            marks = jnp.where(
                slot == 4,
                high,
                jnp.where(slot == 5, middle, jnp.where(slot == 6, last, 0.0)),
            )
            for half in range(2):
                mine = upper if half else ~upper
                pulls[2 * pair + half, rows, :] = jnp.where(mine, grad_att[:, cols], marks).astype(
                    LOW
                )
        begin(pull_outs[number : number + 1])
    grad_out[:, :D] = product_tn(attended[...], grad_attn[...]).astype(LOW)
    experts = control.shape[0] // groups
    small = jnp.concatenate(
        (
            jnp.sum(control.reshape(experts, groups, D), axis=1),
            jnp.broadcast_to(gain, (PAIR - experts, D)),
        ),
        axis=0,
    )
    grad_out[:, D:] = small.T.astype(LOW)
    half = D // 2
    mine_out[...] = grad_out[pl.ds(pl.multiple_of(near[0] * half, half), half), :]
    other_out[...] = grad_out[pl.ds(pl.multiple_of((1 - near[0]) * half, half), half), :]
    finish(outs)
    finish(state_outs)
    finish(pull_outs)


def pair_kernel(
    near,
    queries_far,
    keys_far,
    values_far,
    pulls_far,
    normed_far,
    grads_far,
    mine_out,
    other_out,
    queries,
    keys,
    values,
    pulls,
    normed,
    grads,
    grad_query,
    weights,
    in_sems,
    out_sems,
):
    rows_all = normed.shape[0]
    lane = lax.broadcasted_iota(jnp.int32, (BLOCK, PAIR), 1)
    upper = lane >= HEAD_DIM
    triangle = lax.broadcasted_iota(jnp.int32, (BLOCK, BLOCK), 0) <= lax.broadcasted_iota(
        jnp.int32, (BLOCK, BLOCK), 1
    )

    def ins(pair):
        two = pl.ds(2 * pair, 2)
        return loads(
            [
                (keys_far.at[two], keys.at[two]),
                (queries_far.at[two], queries.at[two]),
                (values_far.at[two], values.at[two]),
                (pulls_far.at[two], pulls.at[two]),
            ],
            in_sems,
            4 * pair,
        )

    def outs(pair):
        return loads([(grads.at[pair], grads_far.at[pair])], out_sems, pair)

    begin(ins(0))
    norm_in = loads([(normed_far, normed)], in_sems, 4 * PAIRS)
    begin(ins(1))
    begin(norm_in)
    for pair in range(2, PAIRS):
        begin(ins(pair))

    def one_pair(pair, carry):
        finish(ins(pair))
        work = [(start, half) for start in range(0, rows_all, BLOCK) for half in range(2)]
        seen = set()
        halves = {}

        def score(item):
            start, half = item
            head = 2 * pair + half
            rows = pl.ds(start, BLOCK)
            key, value = keys[head, rows, :], values[head, rows, :]
            parts = [rows]
            if start + BLOCK < rows_all:
                after = min(rows_all, start + BLOCK + LONGEST) - (start + BLOCK)
                parts.append(pl.ds(start + BLOCK, after))
            made = []
            for number, part in enumerate(parts):
                scores = product_nt(key, queries[head, part, :])
                if number == 0:
                    scores = jnp.where(triangle, scores, NEGATIVE)
                made.append((part, scores, product_nt(value, pulls[head, part, :])))
            return key, made

        def weigh(scored):
            key, made = scored
            done = []
            for part, scores, grad_probs in made:
                probs = jnp.exp(scores)
                done.append((part, probs.astype(LOW), (probs * grad_probs).astype(LOW)))
            return key, done

        def gather(item, weighed):
            start, half = item
            head = 2 * pair + half
            key, done = weighed
            key = jnp.where(upper if half else ~upper, key, jnp.zeros_like(key))
            grad_key = 0.0
            grad_value = 0.0
            for part, probs, grad_scores in done:
                grad_value = grad_value + product(probs, pulls[head, part, :])
                grad_key = grad_key + product(grad_scores, queries[head, part, :])
                both = product_tn(grad_scores, key)
                for offset in range(0, part.size, BLOCK):
                    at = part.start + offset
                    piece = both[offset : offset + BLOCK]
                    if at in seen:
                        grad_query[pl.ds(at, BLOCK), :] += piece
                    else:
                        grad_query[pl.ds(at, BLOCK), :] = piece
                        seen.add(at)
            halves[start, half] = grad_key, grad_value
            if half == 1:
                rows = pl.ds(start, BLOCK)
                grads[pair, rows, PAIR : 2 * PAIR] = jnp.where(
                    upper, halves[start, 1][0], halves[start, 0][0]
                ).astype(LOW)
                grads[pair, rows, 2 * PAIR :] = jnp.where(
                    upper, halves[start, 1][1], halves[start, 0][1]
                ).astype(LOW)

        scored, weighed = {}, {}
        for index in range(len(work) + 2):
            if index < len(work):
                scored[index] = score(work[index])
            if 1 <= index <= len(work):
                weighed[index - 1] = weigh(scored[index - 1])
            if index >= 2:
                gather(work[index - 2], weighed[index - 2])
        grads[pair, :, :PAIR] = (grad_query[...] * (HEAD_DIM ** (-0.5))).astype(LOW)
        begin(outs(pair))

        @pl.when(pair == 0)
        def _():
            finish(norm_in)

        cols = pl.ds(pl.multiple_of(pair * 3 * PAIR, PAIR), 3 * PAIR)
        weights[:, cols] = product_tn(normed[...], grads[pair]).astype(LOW)
        return carry

    lax.fori_loop(0, PAIRS, one_pair, 0)
    half = D // 2
    mine_out[...] = weights[pl.ds(pl.multiple_of(near[0] * half, half), half), :]
    other_out[...] = weights[pl.ds(pl.multiple_of((1 - near[0]) * half, half), half), :]
    for pair in range(PAIRS):
        finish(outs(pair))


def last_kernel(grads, tok, grad_hidden, gain1, w_query, w_key, w_value, grad_tokens):
    parts = [grads[pair] for pair in range(PAIRS)]
    grad_normed = 0.0
    for number, weight in enumerate((w_query, w_key, w_value)):
        cols = slice(number * PAIR, (number + 1) * PAIR)
        joined = jnp.concatenate([part[:, cols] for part in parts], axis=1)
        grad_normed = grad_normed + product_nt(joined, weight[...])
    norm, inverse = standard(tok[...].astype(F32))
    grad_tokens[...] = (
        grad_hidden[...] + standard_pull(norm, inverse, grad_normed * gain1[...])
    ).astype(LOW)


def weight_kernel(expert, count, place, *refs):
    pieces = refs[:count]
    up, down = refs[count : count + 2]
    grad_up, grad_down, taken, given, held = refs[-5:]
    step = pl.program_id(0)
    share = PAIR
    groups = share // (2 * EXP_DEV)
    strip_rows, strip_ff = grad_up.shape[1], grad_down.shape[1]
    first = place[0] * strip_rows
    wide = pl.multiple_of(first // PAIR * PAIR, PAIR)
    inside = pl.ds(pl.multiple_of(first % PAIR, strip_rows), strip_rows)

    @pl.when(step == 0)
    def _():
        filled = 0
        for piece in pieces:
            for start in range(0, piece.shape[0], share):
                target = pl.ds(filled, groups)
                taken[target, :] = piece[
                    start + expert * groups : start + (expert + 1) * groups, :
                ]
                back = start + (EXP_DEV + expert) * groups
                given[target, :] = piece[back : back + groups, :]
                filled += groups

    rows_all = taken.shape[0]
    size = min(512, rows_all)
    ff_first = place[0] * strip_ff
    owner = step == ff_first // FF_BLOCK
    total = 0.0
    acts = []
    for start in range(0, rows_all, size):
        rows = pl.ds(start, size)
        act, slope = gelu_parts(product(taken[rows, :], up[0]))
        grad = (product_nt(given[rows, :], down[0]) * slope).astype(LOW)
        total = total + product_tn(taken[rows, pl.ds(wide, PAIR)], grad)
        acts.append(act.astype(LOW))
    held[:PAIR, :] = total
    grad_up[0] = held[inside, :]

    @pl.when(owner)
    def _():
        whole = 0.0
        for number, act in enumerate(acts):
            whole = whole + product_tn(act, given[pl.ds(number * size, size), :])
        held[...] = whole
        grad_down[0] = held[pl.ds(pl.multiple_of(ff_first % FF_BLOCK, strip_ff), strip_ff), :]


def join_kernel(mine_out, swapped_out, mine, swapped, sums):
    first = mine_out.shape[1]
    sums[:, :first] = (mine_out[...].astype(F32) + swapped_out[...].astype(F32)).astype(LOW)
    sums[:, first:] = (mine[...].astype(F32) + swapped[...].astype(F32)).astype(LOW)


def total_kernel(parts, spread):
    total = parts[0].astype(F32)
    for number in range(1, parts.shape[0]):
        total = total + parts[number].astype(F32)
    total = total.astype(LOW)
    for number in range(parts.shape[0]):
        spread[number] = total


def assemble_kernel(
    near,
    both_own,
    both_other,
    gain1_far,
    w_query_far,
    w_key_far,
    w_value_far,
    grad_query_far,
    grad_key_far,
    grad_value_far,
    grad_out_far,
    grad_control,
    grad_gain1,
    grad_gain2,
    gain1,
    weights,
    squares,
    columns,
    in_sems,
    out_sems,
):
    ins = loads(
        [
            (gain1_far, gain1),
            (w_query_far, weights.at[0]),
            (w_key_far, weights.at[1]),
            (w_value_far, weights.at[2]),
        ],
        in_sems,
    )
    begin(ins)
    half = D // 2
    experts = grad_control.shape[0]
    targets = (grad_query_far, grad_key_far, grad_value_far, grad_out_far)
    lane = lax.broadcasted_iota(jnp.int32, (half, PAIR), 1)
    outs = []
    for step, both in enumerate((both_own, both_other)):
        side = near[0] if step == 0 else 1 - near[0]
        rows = pl.ds(pl.multiple_of(side * half, half), half)
        outs.append(
            loads(
                [
                    (squares.at[number, rows], target.at[rows])
                    for number, target in enumerate(targets)
                ],
                out_sems,
                len(targets) * step,
            )
        )
        squares[3, rows, :] = both[:, :D].astype(F32)
        begin(outs[-1][3:])
        if step == 0:
            finish(ins)
        shared = 0.0
        for number in range(3):
            for pair in range(PAIRS):
                first = D + PAIR + (3 * pair + number) * PAIR
                part = both[:, first : first + PAIR].astype(F32)
                cols = slice(pair * PAIR, (pair + 1) * PAIR)
                squares[number, rows, cols] = part
                shared = shared + part * weights[number, rows, cols].astype(F32)
            begin(outs[-1][number : number + 1])
        columns[rows, :] = jnp.where(
            lane == experts + 1,
            jnp.sum(shared, axis=1, keepdims=True),
            both[:, D : D + PAIR].astype(F32),
        )
    turned = columns[...].T
    grad_control[...] = turned[:experts]
    grad_gain2[...] = turned[experts : experts + 1]
    grad_gain1[...] = turned[experts + 1 : experts + 2] / gain1[...]
    for one in outs:
        finish(one)


def vmem():
    return pl.BlockSpec(memory_space=pltpu.VMEM)


def smem():
    return pl.BlockSpec(memory_space=pltpu.SMEM)


def far():
    return pl.BlockSpec(memory_space=pltpu.HBM)


def shape(*sizes, kind=LOW):
    return jax.ShapeDtypeStruct(sizes, kind)


def params(mib):
    return pltpu.CompilerParams(vmem_limit_bytes=mib * MIB)


def cost(flops, moved):
    return pl.CostEstimate(flops=int(flops), bytes_accessed=int(moved), transcendentals=0)


def ring_of(count):
    order = list(range(0, count, 2)) + list(range(count - 1, 0, -2))
    ahead = [(order[i], order[(i + 1) % count]) for i in range(count)]
    return ahead, [(target, source) for source, target in ahead]


def dma(count):
    return pltpu.SemaphoreType.DMA((count,))


def forward_call(lengths, place, order, gain1, gain2, tokens, cot, weights, w_control, experts):
    rows = tokens.shape[0]
    groups = rows // GROUP
    wide = experts * groups
    blocks = rows // BLOCK
    heads = (HEADS, rows, PAIR)
    kept = [
        ((rows, D), F32),
        ((rows, wide), F32),
        ((rows, D), LOW),
        (heads, LOW),
        (heads, LOW),
        (heads, LOW),
        ((rows, D), LOW),
    ]
    results = pl.pallas_call(
        forward_kernel,
        in_specs=[smem()] + [far()] * 11,
        out_specs=[vmem()] * 4 + [far()] * 7,
        out_shape=[shape(2 * EXP_DEV * groups, D)] * 4
        + [shape(*size, kind=kind) for size, kind in kept],
        scratch_shapes=[
            pltpu.SMEM(lengths.shape, jnp.int32),
            pltpu.VMEM(order.shape, jnp.int32),
            pltpu.VMEM((1, D), F32),
            pltpu.VMEM((1, D), F32),
            pltpu.VMEM((experts, D), LOW),
        ]
        + [pltpu.VMEM((rows, D), LOW)] * 2
        + [pltpu.VMEM((D, D), LOW)] * 4
        + [pltpu.VMEM(*one) for one in kept]
        + [
            pltpu.VMEM((rows, D), LOW),
            pltpu.VMEM((rows, wide), F32),
            pltpu.VMEM((wide, D), LOW),
            pltpu.VMEM((wide, D), LOW),
            pltpu.VMEM(heads, LOW),
            dma(11),
            dma(4 + blocks + PAIRS + 1),
        ],
        compiler_params=params(56),
        cost_estimate=cost(2e10, 2e7),
    )(place, lengths, order, gain1, gain2, w_control, tokens, cot, *weights)
    return results[:4], results[4:]


def expert_call(arrived, w_up, w_down):
    size, _ = arrived[0].shape
    steps = EXP_DEV * w_up.shape[2] // FF_BLOCK
    return pl.pallas_call(
        expert_kernel,
        in_specs=[vmem()] * len(arrived) + [far()] * 2,
        out_specs=[vmem()] * len(arrived),
        out_shape=[shape(size, D)] * len(arrived),
        scratch_shapes=[
            pltpu.VMEM(w_up.shape, LOW),
            pltpu.VMEM(w_down.shape, LOW),
            dma(2 * steps),
        ],
        compiler_params=params(56),
        cost_estimate=cost(5e9, 1e7),
    )(*arrived, w_up, w_down)


def middle_call(place, near, returned, gain2, w_control, hidden, cot, mix, attended, w_out):
    rows, wide = mix.shape
    blocks = rows // BLOCK
    taken = [
        ((rows, D), F32),
        ((rows, D), LOW),
        ((rows, wide), F32),
        ((rows, D), LOW),
        ((D, D), LOW),
    ]
    made = [((rows, D), LOW), ((rows, D), F32), ((HEADS, rows, PAIR), LOW)]
    part = shape(D // 2, D + PAIR)
    return pl.pallas_call(
        middle_kernel,
        in_specs=[smem()] * 2 + [vmem()] * 4 + [far()] * 7,
        out_specs=[far()] * 3 + [vmem()] * 2,
        out_shape=[shape(*size, kind=kind) for size, kind in made] + [part, part],
        scratch_shapes=[pltpu.VMEM((1, D), F32), pltpu.VMEM(w_control.shape, LOW)]
        + [pltpu.VMEM(*one) for one in taken + made]
        + [
            pltpu.VMEM((wide, D), LOW),
            pltpu.VMEM((wide, D), LOW),
            pltpu.VMEM((rows, D), LOW),
            pltpu.VMEM((rows, wide), F32),
            pltpu.VMEM((rows, D), LOW),
            pltpu.VMEM((D, D + PAIR), LOW),
            dma(7),
            dma(3 * blocks),
        ],
        compiler_params=params(52),
        cost_estimate=cost(8e9, 1.5e7),
    )(place, near, *returned, gain2, w_control, hidden, cot, mix, attended, w_out)


def pair_call(near, queries, keys, values, pulls, normed):
    rows = normed.shape[0]
    half = shape(D // 2, 3 * PAIRS * PAIR)
    return pl.pallas_call(
        pair_kernel,
        in_specs=[smem()] + [far()] * 5,
        out_specs=[far()] + [vmem()] * 2,
        out_shape=[shape(PAIRS, rows, 3 * PAIR), half, half],
        scratch_shapes=[pltpu.VMEM((HEADS, rows, PAIR), LOW)] * 4
        + [
            pltpu.VMEM((rows, D), LOW),
            pltpu.VMEM((PAIRS, rows, 3 * PAIR), LOW),
            pltpu.VMEM((rows, PAIR), F32),
            pltpu.VMEM((D, 3 * PAIRS * PAIR), LOW),
            dma(4 * PAIRS + 1),
            dma(PAIRS),
        ],
        compiler_params=params(56),
        cost_estimate=cost(2e10, 1.2e7),
    )(near, queries, keys, values, pulls, normed)


def weight_call(expert, copy, pieces, w_up, w_down, copies, earlier):
    ff = w_up.shape[2]
    held = sum(piece.shape[0] for piece in pieces)
    every = held // (2 * EXP_DEV)
    whole = [pl.BlockSpec(one.shape, lambda f: (0, 0)) for one in pieces]
    return pl.pallas_call(
        functools.partial(weight_kernel, expert, len(pieces)),
        grid=(ff // FF_BLOCK,),
        in_specs=[smem()]
        + whole
        + [
            pl.BlockSpec((1, D, FF_BLOCK), lambda f: (expert, 0, f)),
            pl.BlockSpec((1, FF_BLOCK, D), lambda f: (expert, f, 0)),
        ]
        + [far()] * len(earlier),
        out_specs=[
            pl.BlockSpec((1, D // copies, FF_BLOCK), lambda f: (expert, 0, f)),
            pl.BlockSpec((1, ff // copies, D), lambda f: (expert, 0, 0)),
        ],
        out_shape=[
            shape(EXP_DEV, D // copies, ff, kind=F32),
            shape(EXP_DEV, ff // copies, D, kind=F32),
        ],
        scratch_shapes=[
            pltpu.VMEM((every, D), LOW),
            pltpu.VMEM((every, D), LOW),
            pltpu.VMEM((FF_BLOCK, D), F32),
        ],
        input_output_aliases={3 + len(pieces) + i: i for i in range(len(earlier))},
        compiler_params=params(52),
        cost_estimate=cost(1e10, 8e6),
    )(copy, *pieces, w_up, w_down, *earlier)


def last_call(grads, tokens, grad_hidden, gain1, weights):
    rows = tokens.shape[0]
    row_block = lambda i: (i, 0)
    fixed = lambda i: (0, 0)
    return pl.pallas_call(
        last_kernel,
        grid=(rows // BLOCK,),
        in_specs=[pl.BlockSpec((PAIRS, BLOCK, 3 * PAIR), lambda i: (0, i, 0))]
        + [pl.BlockSpec((BLOCK, D), row_block)] * 2
        + [pl.BlockSpec((1, D), fixed)]
        + [pl.BlockSpec((D, D), fixed)] * 3,
        out_specs=pl.BlockSpec((BLOCK, D), row_block),
        out_shape=shape(rows, D),
        compiler_params=params(52),
        cost_estimate=cost(2e9, 8e6),
    )(grads, tokens, grad_hidden, gain1, *weights)


def join_call(*parts):
    rows = parts[0].shape[0]
    return pl.pallas_call(
        join_kernel,
        in_specs=[vmem()] * 4,
        out_specs=vmem(),
        out_shape=shape(rows, parts[0].shape[1] + parts[2].shape[1]),
        compiler_params=params(16),
        cost_estimate=cost(1e6, 3e6),
    )(*parts)


def total_call(parts):
    return pl.pallas_call(
        total_kernel,
        in_specs=[vmem()],
        out_specs=vmem(),
        out_shape=shape(*parts.shape),
        compiler_params=params(16),
        cost_estimate=cost(1e6, 3e6),
    )(parts)


def assemble_call(near, both_own, both_other, gain1, weights, experts):
    square = shape(D, D, kind=F32)
    return pl.pallas_call(
        assemble_kernel,
        in_specs=[smem()] + [vmem()] * 2 + [far()] * 4,
        out_specs=[far()] * 4 + [vmem()] * 3,
        out_shape=[square] * 4 + [shape(experts, D, kind=F32)] + [shape(1, D, kind=F32)] * 2,
        scratch_shapes=[
            pltpu.VMEM((1, D), F32),
            pltpu.VMEM((3, D, D), LOW),
            pltpu.VMEM((4, D, D), F32),
            pltpu.VMEM((D, PAIR), F32),
            dma(4),
            dma(8),
        ],
        compiler_params=params(40),
        cost_estimate=cost(1e8, 6e6),
    )(near, both_own, both_other, gain1, *weights)


def in_order(*values):
    return lax.optimization_barrier(values)


def shards(
    tokens,
    doc_lengths,
    group_order,
    ln1_gain,
    w_query,
    w_key,
    w_value,
    w_out,
    ln2_gain,
    w_control,
    w_up,
    w_down,
    cotangent,
):
    copies, far_hosts, near_hosts = (lax.axis_size(name) for name in ("dp", "far", "near"))
    hosts = far_hosts * near_hosts
    hosts_axes = ("far", "near")
    axes = ("dp", "far")
    count = copies * far_hosts
    experts = hosts * EXP_DEV
    place = lax.axis_index(hosts_axes).astype(jnp.int32).reshape(1)
    near = lax.axis_index("near").astype(jnp.int32).reshape(1)
    copy = lax.axis_index("dp").astype(jnp.int32).reshape(1)
    gain1 = ln1_gain.reshape(1, D)
    gain2 = ln2_gain.reshape(1, D)
    weights = (w_query, w_key, w_value)
    w_control = w_control.T
    ahead, behind = ring_of(copies)
    steps_left = copies // 2 - 1
    pieces = []

    def exchange(parts):
        return [parts[0]] + [
            lax.ppermute(parts[step], hosts_axes, [(i, i ^ step) for i in range(hosts)])
            for step in range(1, hosts)
        ]

    def pass_on(ahead_part, behind_part):
        return lax.ppermute(ahead_part, "dp", ahead), lax.ppermute(behind_part, "dp", behind)

    def next_step(moving):
        nonlocal steps_left
        pieces.extend(moving)
        steps_left -= 1
        if steps_left > 0:
            return pass_on(*moving)
        half = moving[0].shape[0] // 2
        return pass_on(moving[0][:half], moving[1][half:])

    def near_swap(values):
        return lax.ppermute(values, "near", [(i, i ^ 1) for i in range(near_hosts)])

    def scatter(half):
        rows, cols = half.shape
        return lax.all_to_all(half.reshape(count, rows // count, cols), axes, 0, 0, tiled=True)

    def spread(own):
        return lax.all_to_all(own, axes, 0, 0, tiled=True).reshape(-1, own.shape[-1])

    with jax.named_scope("attention_and_mixing"):
        sends, kept = forward_call(
            doc_lengths,
            place,
            group_order,
            gain1,
            gain2,
            tokens,
            cotangent,
            (*weights, w_out),
            w_control,
            experts,
        )
        hidden, mix, normed, queries, keys, values, attended = kept
    with jax.named_scope("to_experts"):
        arrived = exchange(sends)
    with jax.named_scope("gather_for_weights"):
        own = jnp.concatenate(arrived, axis=0)
        pieces.append(own)
        moving = pass_on(own, own)
    with jax.named_scope("experts"):
        results = expert_call(arrived, w_up, w_down)
    with jax.named_scope("from_experts"):
        returned = exchange(results)
    with jax.named_scope("gather_for_weights"):
        moving = next_step(moving)
    with jax.named_scope("mixing_backward"):
        output, grad_hidden, pulls, mine_out, other_out = middle_call(
            place, near, returned, gain2, w_control, hidden, cotangent, mix, attended, w_out
        )
    with jax.named_scope("gather_for_weights"):
        pulls, other_out, moving = in_order(pulls, other_out, moving)
        moving = next_step(moving)
    with jax.named_scope("reduce"):
        swapped_out = near_swap(other_out)
    with jax.named_scope("attention_backward"):
        grads, mine, other = pair_call(near, queries, keys, values, pulls, normed)
        mine, other, moving, swapped_out = in_order(mine, other, moving, swapped_out)
    with jax.named_scope("gather_for_weights"):
        while steps_left > 0:
            moving = next_step(moving)
    with jax.named_scope("reduce"):
        sums = join_call(mine_out, swapped_out, mine, near_swap(other))
        sums, grads, moving = in_order(sums, grads, moving)
        pieces.extend(moving)
        sums = scatter(sums)
    with jax.named_scope("norm_backward"):
        grad_tokens = last_call(grads, tokens, grad_hidden, gain1, weights)
    with jax.named_scope("expert_weights"):
        grads_expert = weight_call(0, copy, pieces, w_up, w_down, copies, ())
        sums, grads_expert, grad_tokens = in_order(sums, grads_expert, grad_tokens)
    with jax.named_scope("reduce"):
        sums = total_call(sums)
        sums, grads_expert = in_order(sums, grads_expert)
        sums = spread(sums)
    with jax.named_scope("expert_weights"):
        grad_up, grad_down = weight_call(1, copy, pieces, w_up, w_down, copies, grads_expert)
        sums, grad_up, grad_down = in_order(sums, grad_up, grad_down)
    with jax.named_scope("reduce"):
        sums_other = near_swap(sums)
    with jax.named_scope("assemble"):
        grad_query, grad_key, grad_value, grad_out, grad_control, grad_gain1, grad_gain2 = (
            assemble_call(near, sums, sums_other, gain1, weights, experts)
        )
    return (
        output,
        grad_tokens,
        grad_gain1.reshape(D),
        grad_query,
        grad_key,
        grad_value,
        grad_out,
        grad_gain2.reshape(D),
        grad_control.T,
        grad_up,
        grad_down,
    )


def solution(mesh):
    copies, hosts = mesh.shape["dp"], mesh.shape["expert"]
    finer = jax.sharding.Mesh(mesh.devices.reshape(copies, hosts // 2, 2), ("dp", "far", "near"))
    every = P(("dp", "far", "near"), None)
    expert = P(("far", "near"), None, None)
    sliced = P(("far", "near"), "dp", None)
    return jax.shard_map(
        shards,
        mesh=finer,
        in_specs=(every,) * 3 + (P(),) * 7 + (expert,) * 2 + (every,),
        out_specs=(every,) * 2 + (P(),) * 7 + (sliced,) * 2,
        check_vma=False,
    )
```

```python
import functools

import jax
import jax.numpy as jnp
from jax import lax
from jax.experimental import pallas as pl
from jax.experimental.pallas import tpu as pltpu
from jax.sharding import PartitionSpec as P

D = 512
HEADS = 8
HEAD_DIM = 64
PAIRS = 4
PAIR = 2 * HEAD_DIM
GROUP = 32
EXP_DEV = 2
LONGEST = 512
BLOCK = 256
FF_BLOCK = 512
EPSILON = 1e-05
NEGATIVE = -1e30
MIB = 1 << 20

F32 = jnp.float32
LOW = jnp.bfloat16


def product(left, right):
    return jnp.dot(left, right, preferred_element_type=F32)


def product_nt(left, right):
    return lax.dot_general(left, right, (((1,), (1,)), ((), ())), preferred_element_type=F32)


def product_tn(left, right):
    return lax.dot_general(left, right, (((0,), (0,)), ((), ())), preferred_element_type=F32)


def standard(values):
    center = values - jnp.mean(values, axis=-1, keepdims=True)
    inverse = lax.rsqrt(jnp.mean(center * center, axis=-1, keepdims=True) + EPSILON)
    return center * inverse, inverse


def standard_pull(norm, inverse, grad):
    return (
        grad
        - jnp.mean(grad, axis=-1, keepdims=True)
        - norm * jnp.mean(grad * norm, axis=-1, keepdims=True)
    ) * inverse


def gelu_parts(values):
    square = values * values
    tanh = jnp.tanh(0.7978845608028654 * values * (1.0 + 0.044715 * square))
    half = 0.5 + 0.5 * tanh
    slope = half + values * (0.5 - 0.5 * tanh * tanh) * (
        0.7978845608028654 + 0.10703222440890037 * square
    )
    return values * half, slope


def three_parts(values):
    high = values.astype(LOW).astype(F32)
    rest = values - high
    middle = rest.astype(LOW).astype(F32)
    return high, middle, rest - middle


def begin(copies):
    for copy in copies:
        copy.start()


def finish(copies):
    for copy in copies:
        copy.wait()


def loads(pairs, sems, first=0):
    return [
        pltpu.make_async_copy(source, target, sems.at[first + number])
        for number, (source, target) in enumerate(pairs)
    ]


def widened(w_control, width):
    experts = w_control.shape[0]
    lane = lax.broadcasted_iota(jnp.int32, (experts, width), 1) // (width // experts)
    row = lax.broadcasted_iota(jnp.int32, (experts, width), 0)
    return product_tn(jnp.where(lane == row, 1.0, 0.0).astype(LOW), w_control[...]).astype(LOW)


def forward_kernel(
    place,
    lengths_far,
    order_far,
    gain1_far,
    gain2_far,
    w_control_far,
    tok_far,
    cot_far,
    w_query_far,
    w_key_far,
    w_value_far,
    w_out_far,
    send0,
    send1,
    send2,
    send3,
    hidden_far,
    mix_far,
    normed_far,
    queries_far,
    keys_far,
    values_far,
    attended_far,
    lengths,
    order,
    gain1,
    gain2,
    w_control,
    tok,
    cot,
    w_query,
    w_key,
    w_value,
    w_out,
    hidden,
    mix,
    normed,
    queries,
    keys,
    values,
    attended,
    second,
    spread,
    mixed,
    pulled,
    marked,
    in_sems,
    out_sems,
):
    rows_all = tok.shape[0]
    groups = rows_all // GROUP
    width = mix.shape[1]
    ins = loads(
        [
            (tok_far, tok),
            (gain1_far, gain1),
            (lengths_far, lengths),
            (w_query_far, w_query),
            (w_key_far, w_key),
            (w_value_far, w_value),
            (w_out_far, w_out),
            (gain2_far, gain2),
            (w_control_far, w_control),
            (order_far, order),
            (cot_far, cot),
        ],
        in_sems,
    )
    begin(ins)
    blocks = [pl.ds(start, BLOCK) for start in range(0, rows_all, BLOCK)]
    outs = loads(
        [(normed, normed_far), (keys, keys_far), (values, values_far), (mix, mix_far)], out_sems
    )
    state_outs = loads([(hidden.at[rows], hidden_far.at[rows]) for rows in blocks], out_sems, 4)

    def pair_outs(pair):
        first = 4 + len(blocks)
        two = pl.ds(2 * pair, 2)
        return [
            pltpu.make_async_copy(marked.at[two], queries_far.at[two], out_sems.at[first + pair])
        ]

    attended_out = pltpu.make_async_copy(
        attended, attended_far, out_sems.at[4 + len(blocks) + PAIRS]
    )
    lane = lax.broadcasted_iota(jnp.int32, (BLOCK, PAIR), 1)
    upper = lane >= HEAD_DIM
    slot = lane % HEAD_DIM
    finish(ins[:3])
    end0 = lengths[0, 0]
    end1 = end0 + lengths[0, 1]
    end2 = end1 + lengths[0, 2]
    ones = (slot >= 4) & (slot < 7)
    for number, rows in enumerate(blocks):
        norm, _ = standard(tok[rows, :].astype(F32))
        low = (norm * gain1[...]).astype(LOW)
        normed[rows, :] = low
        places = number * BLOCK + lax.broadcasted_iota(jnp.int32, (BLOCK, PAIR), 0)
        document = (
            (places >= end0).astype(jnp.int32)
            + (places >= end1).astype(jnp.int32)
            + (places >= end2).astype(jnp.int32)
        )
        same = slot == document
        key_marks = jnp.where(same | ones, 1.0, 0.0)
        value_marks = jnp.where(ones, 1.0, 0.0)
        query_marks = jnp.where((slot < 4) & ~same, NEGATIVE, 0.0)
        if number == 0:
            finish(ins[3:6])
        query = product(low, w_query[...]) * (HEAD_DIM ** (-0.5))
        key = product(low, w_key[...])
        value = product(low, w_value[...])
        for pair in range(PAIRS):
            cols = slice(pair * PAIR, (pair + 1) * PAIR)
            for half in range(2):
                mine = upper if half else ~upper
                head = 2 * pair + half
                queries[head, rows, :] = jnp.where(mine, query[:, cols], query_marks).astype(LOW)
                keys[head, rows, :] = jnp.where(mine, key[:, cols], key_marks).astype(LOW)
                values[head, rows, :] = jnp.where(mine, value[:, cols], value_marks).astype(LOW)
    begin(outs[:3])

    triangle = lax.broadcasted_iota(jnp.int32, (BLOCK, BLOCK), 1) <= lax.broadcasted_iota(
        jnp.int32, (BLOCK, BLOCK), 0
    )

    def attend(pair, carry):
        work = [(number, half) for number in range(len(blocks)) for half in range(2)]
        results = {}

        def score(item):
            number, half = item
            start = number * BLOCK
            first = max(0, start - LONGEST)
            head = 2 * pair + half
            query = queries[head, blocks[number], :]
            near = jnp.where(triangle, product_nt(query, keys[head, blocks[number], :]), NEGATIVE)
            far = None
            if start > first:
                far = product_nt(query, keys[head, pl.ds(first, start - first), :])
            return query, near, far

        def weigh(item, scored):
            query, near, far = scored
            top = jnp.max(near, axis=1, keepdims=True)
            if far is not None:
                top = jnp.maximum(top, jnp.max(far, axis=1, keepdims=True))
                far = jnp.exp(far - top).astype(LOW)
            return query, jnp.exp(near - top).astype(LOW), far, top

        def gather(item, weighed):
            number, half = item
            query, near, far, top = weighed
            start = number * BLOCK
            first = max(0, start - LONGEST)
            head = 2 * pair + half
            rows = blocks[number]
            out = product(near, values[head, rows, :])
            if far is not None:
                out = out + product(far, values[head, pl.ds(first, start - first), :])
            mark = 4 + HEAD_DIM * (1 - half)
            total = out[:, mark : mark + 1]
            results[item] = out * (1.0 / total)
            high, middle, rest = three_parts(-(top + jnp.log(total)))
            marks = jnp.where(
                lane == mark, high, jnp.where(lane == mark + 1, middle, rest)
            ).astype(LOW)
            marked[head, rows, :] = jnp.where((lane >= mark) & (lane < mark + 3), marks, query)

        scored, weighed = {}, {}
        for index in range(len(work) + 2):
            if index < len(work):
                scored[index] = score(work[index])
            if 1 <= index <= len(work):
                weighed[index - 1] = weigh(work[index - 1], scored[index - 1])
            if index >= 2:
                gather(work[index - 2], weighed[index - 2])
        cols = pl.ds(pl.multiple_of(pair * PAIR, PAIR), PAIR)
        for number, rows in enumerate(blocks):
            attended[rows, cols] = jnp.where(upper, results[number, 1], results[number, 0]).astype(
                LOW
            )
        begin(pair_outs(pair))
        return carry

    lax.fori_loop(0, PAIRS, attend, 0)
    begin([attended_out])
    finish(ins[6:])

    place_group = lax.broadcasted_iota(jnp.int32, (rows_all, width), 0) // GROUP
    lane_group = lax.broadcasted_iota(jnp.int32, (rows_all, width), 1) % groups
    member = jnp.where(place_group == lane_group, 1.0, 0.0).astype(LOW)
    w_wide = widened(w_control, width)
    tops = []
    for number, rows in enumerate(blocks):
        state = tok[rows, :].astype(F32) + product(attended[rows, :], w_out[...])
        hidden[rows, :] = state
        begin(state_outs[number : number + 1])
        norm, _ = standard(state)
        low = (norm * gain2[...]).astype(LOW)
        second[rows, :] = low
        logits = product_nt(low, w_wide)
        places = number * BLOCK + lax.broadcasted_iota(jnp.int32, (BLOCK, rows_all), 0)
        hot = jnp.where(order[...] == places, 1.0, 0.0).astype(LOW)
        inside = product(hot, member)
        logits = jnp.where(inside > 0.5, logits, NEGATIVE)
        spread[rows, :] = logits
        tops.append(jnp.max(logits, axis=0, keepdims=True))
    top = functools.reduce(jnp.maximum, tops)
    total = 0.0
    for rows in blocks:
        expo = jnp.exp(spread[rows, :] - top)
        spread[rows, :] = expo
        total = total + jnp.sum(expo, axis=0, keepdims=True)
    scale = 1.0 / total
    mixed_sum = 0.0
    pulled_sum = 0.0
    for rows in blocks:
        full = spread[rows, :] * scale
        mix[rows, :] = full
        low = full.astype(LOW)
        mixed_sum = mixed_sum + product_tn(low, second[rows, :])
        pulled_sum = pulled_sum + product_tn(low, cot[rows, :])
    begin(outs[3:])
    mixed[...] = mixed_sum.astype(LOW)
    pulled[...] = pulled_sum.astype(LOW)
    share = EXP_DEV * groups
    for step, send in enumerate((send0, send1, send2, send3)):
        part = pl.ds(pl.multiple_of((place[0] ^ step) * share, share), share)
        send[:share, :] = mixed[part, :]
        send[share:, :] = pulled[part, :]
    finish(outs)
    finish(state_outs)
    for pair in range(PAIRS):
        finish(pair_outs(pair))
    finish([attended_out])


def expert_kernel(in0, in1, in2, in3, up, down, out0, out1, out2, out3):
    groups = in0.shape[0] // (2 * EXP_DEV)
    ff = up.shape[2]
    ins = (in0, in1, in2, in3)
    outs = (out0, out1, out2, out3)
    steps = [(expert, first) for expert in range(EXP_DEV) for first in range(0, ff, FF_BLOCK)]
    result = pull = 0.0
    for expert, first in steps:
        part = pl.ds(first, FF_BLOCK)
        own = slice(expert * groups, (expert + 1) * groups)
        back = slice((EXP_DEV + expert) * groups, (EXP_DEV + expert + 1) * groups)
        taken = jnp.concatenate([ref[own, :] for ref in ins], axis=0)
        given = jnp.concatenate([ref[back, :] for ref in ins], axis=0)
        act, slope = gelu_parts(product(taken, up[expert, :, part]))
        grad = (product_nt(given, down[expert, part, :]) * slope).astype(LOW)
        result = result + product(act.astype(LOW), down[expert, part, :])
        pull = pull + product_nt(grad, up[expert, :, part])
        if first + FF_BLOCK == ff:
            for host, ref in enumerate(outs):
                rows = slice(host * groups, (host + 1) * groups)
                ref[own, :] = result[rows].astype(LOW)
                ref[back, :] = pull[rows].astype(LOW)
            result = pull = 0.0


def middle_kernel(
    place,
    near,
    ret0,
    ret1,
    ret2,
    ret3,
    gain2_far,
    w_control_far,
    hidden_far,
    cot_far,
    mix_far,
    attended_far,
    w_out_far,
    output_far,
    grad_hidden_far,
    pulls_far,
    mine_out,
    other_out,
    gain2,
    w_control,
    hidden,
    cot,
    mix,
    attended,
    w_out,
    output,
    grad_hidden,
    pulls,
    result,
    pull,
    second,
    inner,
    grad_attn,
    grad_out,
    in_sems,
    out_sems,
):
    rows_all = hidden.shape[0]
    groups = rows_all // GROUP
    share = EXP_DEV * groups
    blocks = [pl.ds(start, BLOCK) for start in range(0, rows_all, BLOCK)]
    ins = loads(
        [
            (gain2_far, gain2),
            (w_control_far, w_control),
            (mix_far, mix),
            (hidden_far, hidden),
            (cot_far, cot),
            (w_out_far, w_out),
            (attended_far, attended),
        ],
        in_sems,
    )
    begin(ins)
    outs = loads([(output.at[rows], output_far.at[rows]) for rows in blocks], out_sems)
    state_outs = loads(
        [(grad_hidden.at[rows], grad_hidden_far.at[rows]) for rows in blocks],
        out_sems,
        len(blocks),
    )
    pull_outs = loads(
        [(pulls.at[:, rows], pulls_far.at[:, rows]) for rows in blocks],
        out_sems,
        2 * len(blocks),
    )
    lane = lax.broadcasted_iota(jnp.int32, (BLOCK, PAIR), 1)
    upper = lane >= HEAD_DIM
    slot = lane % HEAD_DIM
    crossed = (lax.broadcasted_iota(jnp.int32, (PAIR, PAIR), 0) >= HEAD_DIM) != (
        lax.broadcasted_iota(jnp.int32, (PAIR, PAIR), 1) >= HEAD_DIM
    )
    crossing = jnp.where(crossed, -1.0, 0.0).astype(LOW)
    for step, ret in enumerate((ret0, ret1, ret2, ret3)):
        part = pl.ds(pl.multiple_of((place[0] ^ step) * share, share), share)
        result[part, :] = ret[:share, :]
        pull[part, :] = ret[share:, :]
    finish(ins[:5])
    total = 0.0
    for number, rows in enumerate(blocks):
        state = hidden[rows, :]
        norm, _ = standard(state)
        low = (norm * gain2[...]).astype(LOW)
        second[rows, :] = low
        full = mix[rows, :]
        output[rows, :] = (state + product(full.astype(LOW), result[...])).astype(LOW)
        begin(outs[number : number + 1])
        grad_mix = product_nt(cot[rows, :], result[...]) + product_nt(low, pull[...])
        weighted = full * grad_mix
        inner[rows, :] = weighted
        total = total + jnp.sum(weighted, axis=0, keepdims=True)
    finish(ins[5:])
    w_wide = widened(w_control, mix.shape[1])
    control = 0.0
    gain = 0.0
    for number, rows in enumerate(blocks):
        full = mix[rows, :]
        grad_logits = (inner[rows, :] - full * total).astype(LOW)
        grad_second = product(full.astype(LOW), pull[...]) + product(grad_logits, w_wide)
        control = control + product_tn(grad_logits, second[rows, :])
        norm, inverse = standard(hidden[rows, :])
        gain = gain + jnp.sum(grad_second * norm, axis=0, keepdims=True)
        grad_state = cot[rows, :].astype(F32) + standard_pull(
            norm, inverse, grad_second * gain2[...]
        )
        grad_hidden[rows, :] = grad_state
        begin(state_outs[number : number + 1])
        low = grad_state.astype(LOW)
        grad_attn[rows, :] = low
        grad_att = product_nt(low, w_out[...]).astype(LOW).astype(F32)
        shared = grad_att * attended[rows, :].astype(F32)
        for pair in range(PAIRS):
            cols = slice(pair * PAIR, (pair + 1) * PAIR)
            top = shared[:, cols].astype(LOW)
            rest = (shared[:, cols] - top.astype(F32)).astype(LOW)
            delta = product(top, crossing) + product(rest, crossing)
            high, middle, last = three_parts(delta)
            marks = jnp.where(
                slot == 4,
                high,
                jnp.where(slot == 5, middle, jnp.where(slot == 6, last, 0.0)),
            )
            for half in range(2):
                mine = upper if half else ~upper
                pulls[2 * pair + half, rows, :] = jnp.where(mine, grad_att[:, cols], marks).astype(
                    LOW
                )
        begin(pull_outs[number : number + 1])
    grad_out[:, :D] = product_tn(attended[...], grad_attn[...]).astype(LOW)
    experts = control.shape[0] // groups
    small = jnp.concatenate(
        (
            jnp.sum(control.reshape(experts, groups, D), axis=1),
            jnp.broadcast_to(gain, (PAIR - experts, D)),
        ),
        axis=0,
    )
    grad_out[:, D:] = small.T.astype(LOW)
    half = D // 2
    mine_out[...] = grad_out[pl.ds(pl.multiple_of(near[0] * half, half), half), :]
    other_out[...] = grad_out[pl.ds(pl.multiple_of((1 - near[0]) * half, half), half), :]
    finish(outs)
    finish(state_outs)
    finish(pull_outs)


def pair_kernel(
    near,
    queries_far,
    keys_far,
    values_far,
    pulls_far,
    normed_far,
    grads_far,
    mine_out,
    other_out,
    queries,
    keys,
    values,
    pulls,
    normed,
    grads,
    grad_query,
    weights,
    in_sems,
    out_sems,
):
    rows_all = normed.shape[0]
    lane = lax.broadcasted_iota(jnp.int32, (BLOCK, PAIR), 1)
    upper = lane >= HEAD_DIM
    triangle = lax.broadcasted_iota(jnp.int32, (BLOCK, BLOCK), 0) <= lax.broadcasted_iota(
        jnp.int32, (BLOCK, BLOCK), 1
    )

    def ins(pair):
        two = pl.ds(2 * pair, 2)
        return loads(
            [
                (keys_far.at[two], keys.at[two]),
                (queries_far.at[two], queries.at[two]),
                (values_far.at[two], values.at[two]),
                (pulls_far.at[two], pulls.at[two]),
            ],
            in_sems,
            4 * pair,
        )

    def outs(pair):
        return loads([(grads.at[pair], grads_far.at[pair])], out_sems, pair)

    begin(ins(0))
    norm_in = loads([(normed_far, normed)], in_sems, 4 * PAIRS)
    begin(ins(1))
    begin(norm_in)
    for pair in range(2, PAIRS):
        begin(ins(pair))

    def one_pair(pair, carry):
        finish(ins(pair))
        work = [(start, half) for start in range(0, rows_all, BLOCK) for half in range(2)]
        seen = set()
        halves = {}

        def score(item):
            start, half = item
            head = 2 * pair + half
            rows = pl.ds(start, BLOCK)
            key, value = keys[head, rows, :], values[head, rows, :]
            parts = [rows]
            if start + BLOCK < rows_all:
                after = min(rows_all, start + BLOCK + LONGEST) - (start + BLOCK)
                parts.append(pl.ds(start + BLOCK, after))
            made = []
            for number, part in enumerate(parts):
                scores = product_nt(key, queries[head, part, :])
                if number == 0:
                    scores = jnp.where(triangle, scores, NEGATIVE)
                made.append((part, scores, product_nt(value, pulls[head, part, :])))
            return key, made

        def weigh(scored):
            key, made = scored
            done = []
            for part, scores, grad_probs in made:
                probs = jnp.exp(scores)
                done.append((part, probs.astype(LOW), (probs * grad_probs).astype(LOW)))
            return key, done

        def gather(item, weighed):
            start, half = item
            head = 2 * pair + half
            key, done = weighed
            key = jnp.where(upper if half else ~upper, key, jnp.zeros_like(key))
            grad_key = 0.0
            grad_value = 0.0
            for part, probs, grad_scores in done:
                grad_value = grad_value + product(probs, pulls[head, part, :])
                grad_key = grad_key + product(grad_scores, queries[head, part, :])
                both = product_tn(grad_scores, key)
                for offset in range(0, part.size, BLOCK):
                    at = part.start + offset
                    piece = both[offset : offset + BLOCK]
                    if at in seen:
                        grad_query[pl.ds(at, BLOCK), :] += piece
                    else:
                        grad_query[pl.ds(at, BLOCK), :] = piece
                        seen.add(at)
            halves[start, half] = grad_key, grad_value
            if half == 1:
                rows = pl.ds(start, BLOCK)
                grads[pair, rows, PAIR : 2 * PAIR] = jnp.where(
                    upper, halves[start, 1][0], halves[start, 0][0]
                ).astype(LOW)
                grads[pair, rows, 2 * PAIR :] = jnp.where(
                    upper, halves[start, 1][1], halves[start, 0][1]
                ).astype(LOW)

        scored, weighed = {}, {}
        for index in range(len(work) + 2):
            if index < len(work):
                scored[index] = score(work[index])
            if 1 <= index <= len(work):
                weighed[index - 1] = weigh(scored[index - 1])
            if index >= 2:
                gather(work[index - 2], weighed[index - 2])
        grads[pair, :, :PAIR] = (grad_query[...] * (HEAD_DIM ** (-0.5))).astype(LOW)
        begin(outs(pair))

        @pl.when(pair == 0)
        def _():
            finish(norm_in)

        cols = pl.ds(pl.multiple_of(pair * 3 * PAIR, PAIR), 3 * PAIR)
        weights[:, cols] = product_tn(normed[...], grads[pair]).astype(LOW)
        return carry

    lax.fori_loop(0, PAIRS, one_pair, 0)
    half = D // 2
    mine_out[...] = weights[pl.ds(pl.multiple_of(near[0] * half, half), half), :]
    other_out[...] = weights[pl.ds(pl.multiple_of((1 - near[0]) * half, half), half), :]
    for pair in range(PAIRS):
        finish(outs(pair))


def last_kernel(grads, tok, grad_hidden, gain1, w_query, w_key, w_value, grad_tokens):
    parts = [grads[pair] for pair in range(PAIRS)]
    grad_normed = 0.0
    for number, weight in enumerate((w_query, w_key, w_value)):
        cols = slice(number * PAIR, (number + 1) * PAIR)
        joined = jnp.concatenate([part[:, cols] for part in parts], axis=1)
        grad_normed = grad_normed + product_nt(joined, weight[...])
    norm, inverse = standard(tok[...].astype(F32))
    grad_tokens[...] = (
        grad_hidden[...] + standard_pull(norm, inverse, grad_normed * gain1[...])
    ).astype(LOW)


def weight_kernel(expert, count, place, *refs):
    pieces = refs[:count]
    up, down = refs[count : count + 2]
    grad_up, grad_down, taken, given, held = refs[-5:]
    step = pl.program_id(0)
    share = PAIR
    groups = share // (2 * EXP_DEV)
    strip_rows, strip_ff = grad_up.shape[1], grad_down.shape[1]
    first = place[0] * strip_rows
    wide = pl.multiple_of(first // PAIR * PAIR, PAIR)
    inside = pl.ds(pl.multiple_of(first % PAIR, strip_rows), strip_rows)

    @pl.when(step == 0)
    def _():
        filled = 0
        for piece in pieces:
            for start in range(0, piece.shape[0], share):
                target = pl.ds(filled, groups)
                taken[target, :] = piece[
                    start + expert * groups : start + (expert + 1) * groups, :
                ]
                back = start + (EXP_DEV + expert) * groups
                given[target, :] = piece[back : back + groups, :]
                filled += groups

    rows_all = taken.shape[0]
    size = min(512, rows_all)
    ff_first = place[0] * strip_ff
    owner = step == ff_first // FF_BLOCK
    total = 0.0
    acts = []
    for start in range(0, rows_all, size):
        rows = pl.ds(start, size)
        act, slope = gelu_parts(product(taken[rows, :], up[0]))
        grad = (product_nt(given[rows, :], down[0]) * slope).astype(LOW)
        total = total + product_tn(taken[rows, pl.ds(wide, PAIR)], grad)
        acts.append(act.astype(LOW))
    held[:PAIR, :] = total
    grad_up[0] = held[inside, :]

    @pl.when(owner)
    def _():
        whole = 0.0
        for number, act in enumerate(acts):
            whole = whole + product_tn(act, given[pl.ds(number * size, size), :])
        held[...] = whole
        grad_down[0] = held[pl.ds(pl.multiple_of(ff_first % FF_BLOCK, strip_ff), strip_ff), :]


def join_kernel(mine_out, swapped_out, mine, swapped, sums):
    first = mine_out.shape[1]
    sums[:, :first] = (mine_out[...].astype(F32) + swapped_out[...].astype(F32)).astype(LOW)
    sums[:, first:] = (mine[...].astype(F32) + swapped[...].astype(F32)).astype(LOW)


def total_kernel(parts, spread):
    total = parts[0].astype(F32)
    for number in range(1, parts.shape[0]):
        total = total + parts[number].astype(F32)
    total = total.astype(LOW)
    for number in range(parts.shape[0]):
        spread[number] = total


def assemble_kernel(
    near,
    both_own,
    both_other,
    gain1_far,
    w_query_far,
    w_key_far,
    w_value_far,
    grad_query_far,
    grad_key_far,
    grad_value_far,
    grad_out_far,
    grad_control,
    grad_gain1,
    grad_gain2,
    gain1,
    weights,
    squares,
    columns,
    in_sems,
    out_sems,
):
    ins = loads(
        [
            (gain1_far, gain1),
            (w_query_far, weights.at[0]),
            (w_key_far, weights.at[1]),
            (w_value_far, weights.at[2]),
        ],
        in_sems,
    )
    begin(ins)
    half = D // 2
    experts = grad_control.shape[0]
    targets = (grad_query_far, grad_key_far, grad_value_far, grad_out_far)
    lane = lax.broadcasted_iota(jnp.int32, (half, PAIR), 1)
    outs = []
    for step, both in enumerate((both_own, both_other)):
        side = near[0] if step == 0 else 1 - near[0]
        rows = pl.ds(pl.multiple_of(side * half, half), half)
        outs.append(
            loads(
                [
                    (squares.at[number, rows], target.at[rows])
                    for number, target in enumerate(targets)
                ],
                out_sems,
                len(targets) * step,
            )
        )
        squares[3, rows, :] = both[:, :D].astype(F32)
        begin(outs[-1][3:])
        if step == 0:
            finish(ins)
        shared = 0.0
        for number in range(3):
            for pair in range(PAIRS):
                first = D + PAIR + (3 * pair + number) * PAIR
                part = both[:, first : first + PAIR].astype(F32)
                cols = slice(pair * PAIR, (pair + 1) * PAIR)
                squares[number, rows, cols] = part
                shared = shared + part * weights[number, rows, cols].astype(F32)
            begin(outs[-1][number : number + 1])
        columns[rows, :] = jnp.where(
            lane == experts + 1,
            jnp.sum(shared, axis=1, keepdims=True),
            both[:, D : D + PAIR].astype(F32),
        )
    turned = columns[...].T
    grad_control[...] = turned[:experts]
    grad_gain2[...] = turned[experts : experts + 1]
    grad_gain1[...] = turned[experts + 1 : experts + 2] / gain1[...]
    for one in outs:
        finish(one)


def vmem():
    return pl.BlockSpec(memory_space=pltpu.VMEM)


def smem():
    return pl.BlockSpec(memory_space=pltpu.SMEM)


def far():
    return pl.BlockSpec(memory_space=pltpu.HBM)


def shape(*sizes, kind=LOW):
    return jax.ShapeDtypeStruct(sizes, kind)


def params(mib):
    return pltpu.CompilerParams(vmem_limit_bytes=mib * MIB)


def cost(flops, moved):
    return pl.CostEstimate(flops=int(flops), bytes_accessed=int(moved), transcendentals=0)


def ring_of(count):
    order = list(range(0, count, 2)) + list(range(count - 1, 0, -2))
    ahead = [(order[i], order[(i + 1) % count]) for i in range(count)]
    return ahead, [(target, source) for source, target in ahead]


def dma(count):
    return pltpu.SemaphoreType.DMA((count,))


def forward_call(lengths, place, order, gain1, gain2, tokens, cot, weights, w_control, experts):
    rows = tokens.shape[0]
    groups = rows // GROUP
    wide = experts * groups
    blocks = rows // BLOCK
    heads = (HEADS, rows, PAIR)
    kept = [
        ((rows, D), F32),
        ((rows, wide), F32),
        ((rows, D), LOW),
        (heads, LOW),
        (heads, LOW),
        (heads, LOW),
        ((rows, D), LOW),
    ]
    results = pl.pallas_call(
        forward_kernel,
        in_specs=[smem()] + [far()] * 11,
        out_specs=[vmem()] * 4 + [far()] * 7,
        out_shape=[shape(2 * EXP_DEV * groups, D)] * 4
        + [shape(*size, kind=kind) for size, kind in kept],
        scratch_shapes=[
            pltpu.SMEM(lengths.shape, jnp.int32),
            pltpu.VMEM(order.shape, jnp.int32),
            pltpu.VMEM((1, D), F32),
            pltpu.VMEM((1, D), F32),
            pltpu.VMEM((experts, D), LOW),
        ]
        + [pltpu.VMEM((rows, D), LOW)] * 2
        + [pltpu.VMEM((D, D), LOW)] * 4
        + [pltpu.VMEM(*one) for one in kept]
        + [
            pltpu.VMEM((rows, D), LOW),
            pltpu.VMEM((rows, wide), F32),
            pltpu.VMEM((wide, D), LOW),
            pltpu.VMEM((wide, D), LOW),
            pltpu.VMEM(heads, LOW),
            dma(11),
            dma(4 + blocks + PAIRS + 1),
        ],
        compiler_params=pltpu.CompilerParams(vmem_limit_bytes=56623104),
        cost_estimate=cost(2e10, 2e7),
    )(place, lengths, order, gain1, gain2, w_control, tokens, cot, *weights)
    return results[:4], results[4:]


def expert_call(arrived, w_up, w_down):
    size, _ = arrived[0].shape
    return pl.pallas_call(
        expert_kernel,
        in_specs=[vmem()] * (len(arrived) + 2),
        out_specs=[vmem()] * len(arrived),
        out_shape=[shape(size, D)] * len(arrived),
        compiler_params=params(16),
        cost_estimate=cost(5e9, 1e7),
    )(*arrived, w_up, w_down)


def middle_call(place, near, returned, gain2, w_control, hidden, cot, mix, attended, w_out):
    rows, wide = mix.shape
    blocks = rows // BLOCK
    taken = [
        ((rows, D), F32),
        ((rows, D), LOW),
        ((rows, wide), F32),
        ((rows, D), LOW),
        ((D, D), LOW),
    ]
    made = [((rows, D), LOW), ((rows, D), F32), ((HEADS, rows, PAIR), LOW)]
    part = shape(D // 2, D + PAIR)
    return pl.pallas_call(
        middle_kernel,
        in_specs=[smem()] * 2 + [vmem()] * 4 + [far()] * 7,
        out_specs=[far()] * 3 + [vmem()] * 2,
        out_shape=[shape(*size, kind=kind) for size, kind in made] + [part, part],
        scratch_shapes=[pltpu.VMEM((1, D), F32), pltpu.VMEM(w_control.shape, LOW)]
        + [pltpu.VMEM(*one) for one in taken + made]
        + [
            pltpu.VMEM((wide, D), LOW),
            pltpu.VMEM((wide, D), LOW),
            pltpu.VMEM((rows, D), LOW),
            pltpu.VMEM((rows, wide), F32),
            pltpu.VMEM((rows, D), LOW),
            pltpu.VMEM((D, D + PAIR), LOW),
            dma(7),
            dma(3 * blocks),
        ],
        compiler_params=params(52),
        cost_estimate=cost(8e9, 1.5e7),
    )(place, near, *returned, gain2, w_control, hidden, cot, mix, attended, w_out)


def pair_call(near, queries, keys, values, pulls, normed):
    rows = normed.shape[0]
    half = shape(D // 2, 3 * PAIRS * PAIR)
    return pl.pallas_call(
        pair_kernel,
        in_specs=[smem()] + [far()] * 5,
        out_specs=[far()] + [vmem()] * 2,
        out_shape=[shape(PAIRS, rows, 3 * PAIR), half, half],
        scratch_shapes=[pltpu.VMEM((HEADS, rows, PAIR), LOW)] * 4
        + [
            pltpu.VMEM((rows, D), LOW),
            pltpu.VMEM((PAIRS, rows, 3 * PAIR), LOW),
            pltpu.VMEM((rows, PAIR), F32),
            pltpu.VMEM((D, 3 * PAIRS * PAIR), LOW),
            dma(4 * PAIRS + 1),
            dma(PAIRS),
        ],
        compiler_params=params(56),
        cost_estimate=cost(2e10, 1.2e7),
    )(near, queries, keys, values, pulls, normed)


def weight_call(expert, copy, pieces, w_up, w_down, copies, earlier):
    ff = w_up.shape[2]
    held = sum(piece.shape[0] for piece in pieces)
    every = held // (2 * EXP_DEV)
    whole = [pl.BlockSpec(one.shape, lambda f: (0, 0)) for one in pieces]
    return pl.pallas_call(
        functools.partial(weight_kernel, expert, len(pieces)),
        grid=(ff // FF_BLOCK,),
        in_specs=[smem()]
        + whole
        + [
            pl.BlockSpec((1, D, FF_BLOCK), lambda f: (expert, 0, f)),
            pl.BlockSpec((1, FF_BLOCK, D), lambda f: (expert, f, 0)),
        ]
        + [far()] * len(earlier),
        out_specs=[
            pl.BlockSpec((1, D // copies, FF_BLOCK), lambda f: (expert, 0, f)),
            pl.BlockSpec((1, ff // copies, D), lambda f: (expert, 0, 0)),
        ],
        out_shape=[
            shape(EXP_DEV, D // copies, ff, kind=F32),
            shape(EXP_DEV, ff // copies, D, kind=F32),
        ],
        scratch_shapes=[
            pltpu.VMEM((every, D), LOW),
            pltpu.VMEM((every, D), LOW),
            pltpu.VMEM((FF_BLOCK, D), F32),
        ],
        input_output_aliases={3 + len(pieces) + i: i for i in range(len(earlier))},
        compiler_params=params(52),
        cost_estimate=cost(1e10, 8e6),
    )(copy, *pieces, w_up, w_down, *earlier)


def last_call(grads, tokens, grad_hidden, gain1, weights):
    rows = tokens.shape[0]
    row_block = lambda i: (i, 0)
    fixed = lambda i: (0, 0)
    return pl.pallas_call(
        last_kernel,
        grid=(rows // BLOCK,),
        in_specs=[pl.BlockSpec((PAIRS, BLOCK, 3 * PAIR), lambda i: (0, i, 0))]
        + [pl.BlockSpec((BLOCK, D), row_block)] * 2
        + [pl.BlockSpec((1, D), fixed)]
        + [pl.BlockSpec((D, D), fixed)] * 3,
        out_specs=pl.BlockSpec((BLOCK, D), row_block),
        out_shape=shape(rows, D),
        compiler_params=params(52),
        cost_estimate=cost(2e9, 8e6),
    )(grads, tokens, grad_hidden, gain1, *weights)


def join_call(*parts):
    rows = parts[0].shape[0]
    return pl.pallas_call(
        join_kernel,
        in_specs=[vmem()] * 4,
        out_specs=vmem(),
        out_shape=shape(rows, parts[0].shape[1] + parts[2].shape[1]),
        compiler_params=params(16),
        cost_estimate=cost(1e6, 3e6),
    )(*parts)


def total_call(parts):
    return pl.pallas_call(
        total_kernel,
        in_specs=[vmem()],
        out_specs=vmem(),
        out_shape=shape(*parts.shape),
        compiler_params=params(16),
        cost_estimate=cost(1e6, 3e6),
    )(parts)


def assemble_call(near, both_own, both_other, gain1, weights, experts):
    square = shape(D, D, kind=F32)
    return pl.pallas_call(
        assemble_kernel,
        in_specs=[smem()] + [vmem()] * 2 + [far()] * 4,
        out_specs=[far()] * 4 + [vmem()] * 3,
        out_shape=[square] * 4 + [shape(experts, D, kind=F32)] + [shape(1, D, kind=F32)] * 2,
        scratch_shapes=[
            pltpu.VMEM((1, D), F32),
            pltpu.VMEM((3, D, D), LOW),
            pltpu.VMEM((4, D, D), F32),
            pltpu.VMEM((D, PAIR), F32),
            dma(4),
            dma(8),
        ],
        compiler_params=params(40),
        cost_estimate=cost(1e8, 6e6),
    )(near, both_own, both_other, gain1, *weights)


def in_order(*values):
    return lax.optimization_barrier(values)


def shards(
    tokens,
    doc_lengths,
    group_order,
    ln1_gain,
    w_query,
    w_key,
    w_value,
    w_out,
    ln2_gain,
    w_control,
    w_up,
    w_down,
    cotangent,
):
    copies, far_hosts, near_hosts = (lax.axis_size(name) for name in ("dp", "far", "near"))
    hosts = far_hosts * near_hosts
    hosts_axes = ("far", "near")
    axes = ("dp", "far")
    count = copies * far_hosts
    experts = hosts * EXP_DEV
    place = lax.axis_index(hosts_axes).astype(jnp.int32).reshape(1)
    near = lax.axis_index("near").astype(jnp.int32).reshape(1)
    copy = lax.axis_index("dp").astype(jnp.int32).reshape(1)
    gain1 = ln1_gain.reshape(1, D)
    gain2 = ln2_gain.reshape(1, D)
    weights = (w_query, w_key, w_value)
    w_control = w_control.T
    ahead, behind = ring_of(copies)
    steps_left = copies // 2 - 1
    pieces = []

    def exchange(parts):
        return [parts[0]] + [
            lax.ppermute(parts[step], hosts_axes, [(i, i ^ step) for i in range(hosts)])
            for step in range(1, hosts)
        ]

    def pass_on(ahead_part, behind_part):
        return lax.ppermute(ahead_part, "dp", ahead), lax.ppermute(behind_part, "dp", behind)

    def next_step(moving):
        nonlocal steps_left
        pieces.extend(moving)
        steps_left -= 1
        if steps_left > 0:
            return pass_on(*moving)
        half = moving[0].shape[0] // 2
        return pass_on(moving[0][:half], moving[1][half:])

    def near_swap(values):
        return lax.ppermute(values, "near", [(i, i ^ 1) for i in range(near_hosts)])

    def scatter(half):
        rows, cols = half.shape
        return lax.all_to_all(half.reshape(count, rows // count, cols), axes, 0, 0, tiled=True)

    def spread(own):
        return lax.all_to_all(own, axes, 0, 0, tiled=True).reshape(-1, own.shape[-1])

    with jax.named_scope("attention_and_mixing"):
        sends, kept = forward_call(
            doc_lengths,
            place,
            group_order,
            gain1,
            gain2,
            tokens,
            cotangent,
            (*weights, w_out),
            w_control,
            experts,
        )
        hidden, mix, normed, queries, keys, values, attended = kept
    with jax.named_scope("to_experts"):
        arrived = exchange(sends)
    with jax.named_scope("gather_for_weights"):
        own = jnp.concatenate(arrived, axis=0)
        pieces.append(own)
        moving = pass_on(own, own)
    with jax.named_scope("experts"):
        results = expert_call(arrived, w_up, w_down)
    with jax.named_scope("from_experts"):
        returned = exchange(results)
    with jax.named_scope("gather_for_weights"):
        moving = next_step(moving)
    with jax.named_scope("mixing_backward"):
        output, grad_hidden, pulls, mine_out, other_out = middle_call(
            place, near, returned, gain2, w_control, hidden, cotangent, mix, attended, w_out
        )
    with jax.named_scope("gather_for_weights"):
        pulls, other_out, moving = in_order(pulls, other_out, moving)
        moving = next_step(moving)
    with jax.named_scope("reduce"):
        swapped_out = near_swap(other_out)
    with jax.named_scope("attention_backward"):
        grads, mine, other = pair_call(near, queries, keys, values, pulls, normed)
        mine, other, moving, swapped_out = in_order(mine, other, moving, swapped_out)
    with jax.named_scope("gather_for_weights"):
        while steps_left > 0:
            moving = next_step(moving)
    with jax.named_scope("reduce"):
        sums = join_call(mine_out, swapped_out, mine, near_swap(other))
        sums, grads, moving = in_order(sums, grads, moving)
        pieces.extend(moving)
        sums = scatter(sums)
    with jax.named_scope("norm_backward"):
        grad_tokens = last_call(grads, tokens, grad_hidden, gain1, weights)
    with jax.named_scope("expert_weights"):
        grads_expert = weight_call(0, copy, pieces, w_up, w_down, copies, ())
        sums, grads_expert, grad_tokens = in_order(sums, grads_expert, grad_tokens)
    with jax.named_scope("reduce"):
        sums = total_call(sums)
        sums, grads_expert = in_order(sums, grads_expert)
        sums = spread(sums)
    with jax.named_scope("expert_weights"):
        grad_up, grad_down = weight_call(1, copy, pieces, w_up, w_down, copies, grads_expert)
        sums, grad_up, grad_down = in_order(sums, grad_up, grad_down)
    with jax.named_scope("reduce"):
        sums_other = near_swap(sums)
    with jax.named_scope("assemble"):
        grad_query, grad_key, grad_value, grad_out, grad_control, grad_gain1, grad_gain2 = (
            assemble_call(near, sums, sums_other, gain1, weights, experts)
        )
    return (
        output,
        grad_tokens,
        grad_gain1.reshape(D),
        grad_query,
        grad_key,
        grad_value,
        grad_out,
        grad_gain2.reshape(D),
        grad_control.T,
        grad_up,
        grad_down,
    )


def solution(mesh):
    copies, hosts = mesh.shape["dp"], mesh.shape["expert"]
    finer = jax.sharding.Mesh(mesh.devices.reshape(copies, hosts // 2, 2), ("dp", "far", "near"))
    every = P(("dp", "far", "near"), None)
    expert = P(("far", "near"), None, None)
    sliced = P(("far", "near"), "dp", None)
    return jax.shard_map(
        shards,
        mesh=finer,
        in_specs=(every,) * 3 + (P(),) * 7 + (expert,) * 2 + (every,),
        out_specs=(every,) * 2 + (P(),) * 7 + (sliced,) * 2,
        check_vma=False,
    )
```

```python
import functools

import jax
import jax.numpy as jnp
from jax import lax
from jax.experimental import pallas as pl
from jax.experimental.pallas import tpu as pltpu
from jax.sharding import PartitionSpec as P

D = 512
HEADS = 8
HEAD_DIM = 64
PAIRS = 4
PAIR = 2 * HEAD_DIM
GROUP = 32
EXP_DEV = 2
LONGEST = 512
BLOCK = 256
FF_BLOCK = 512
EPSILON = 1e-05
NEGATIVE = -1e30
MIB = 1 << 20

F32 = jnp.float32
LOW = jnp.bfloat16


def product(left, right):
    return jnp.dot(left, right, preferred_element_type=F32)


def product_nt(left, right):
    return lax.dot_general(left, right, (((1,), (1,)), ((), ())), preferred_element_type=F32)


def product_tn(left, right):
    return lax.dot_general(left, right, (((0,), (0,)), ((), ())), preferred_element_type=F32)


def standard(values):
    center = values - jnp.mean(values, axis=-1, keepdims=True)
    inverse = lax.rsqrt(jnp.mean(center * center, axis=-1, keepdims=True) + EPSILON)
    return center * inverse, inverse


def standard_pull(norm, inverse, grad):
    return (
        grad
        - jnp.mean(grad, axis=-1, keepdims=True)
        - norm * jnp.mean(grad * norm, axis=-1, keepdims=True)
    ) * inverse


def gelu_parts(values):
    square = values * values
    tanh = jnp.tanh(0.7978845608028654 * values * (1.0 + 0.044715 * square))
    half = 0.5 + 0.5 * tanh
    slope = half + values * (0.5 - 0.5 * tanh * tanh) * (
        0.7978845608028654 + 0.10703222440890037 * square
    )
    return values * half, slope


def three_parts(values):
    high = values.astype(LOW).astype(F32)
    rest = values - high
    middle = rest.astype(LOW).astype(F32)
    return high, middle, rest - middle


def begin(copies):
    for copy in copies:
        copy.start()


def finish(copies):
    for copy in copies:
        copy.wait()


def loads(pairs, sems, first=0):
    return [
        pltpu.make_async_copy(source, target, sems.at[first + number])
        for number, (source, target) in enumerate(pairs)
    ]


def widened(w_control, width):
    experts = w_control.shape[0]
    lane = lax.broadcasted_iota(jnp.int32, (experts, width), 1) // (width // experts)
    row = lax.broadcasted_iota(jnp.int32, (experts, width), 0)
    return product_tn(jnp.where(lane == row, 1.0, 0.0).astype(LOW), w_control[...]).astype(LOW)


def forward_kernel(
    place,
    lengths_far,
    order_far,
    gain1_far,
    gain2_far,
    w_control_far,
    tok_far,
    cot_far,
    w_query_far,
    w_key_far,
    w_value_far,
    w_out_far,
    send0,
    send1,
    send2,
    send3,
    hidden_far,
    mix_far,
    normed_far,
    queries_far,
    keys_far,
    values_far,
    attended_far,
    lengths,
    order,
    gain1,
    gain2,
    w_control,
    tok,
    cot,
    w_query,
    w_key,
    w_value,
    w_out,
    hidden,
    mix,
    normed,
    queries,
    keys,
    values,
    attended,
    second,
    spread,
    mixed,
    pulled,
    marked,
    in_sems,
    out_sems,
):
    rows_all = tok.shape[0]
    groups = rows_all // GROUP
    width = mix.shape[1]
    ins = loads(
        [
            (tok_far, tok),
            (gain1_far, gain1),
            (lengths_far, lengths),
            (w_query_far, w_query),
            (w_key_far, w_key),
            (w_value_far, w_value),
            (w_out_far, w_out),
            (gain2_far, gain2),
            (w_control_far, w_control),
            (order_far, order),
            (cot_far, cot),
        ],
        in_sems,
    )
    begin(ins)
    blocks = [pl.ds(start, BLOCK) for start in range(0, rows_all, BLOCK)]
    outs = loads(
        [(normed, normed_far), (keys, keys_far), (values, values_far), (mix, mix_far)], out_sems
    )
    state_outs = loads([(hidden.at[rows], hidden_far.at[rows]) for rows in blocks], out_sems, 4)

    def pair_outs(pair):
        first = 4 + len(blocks)
        two = pl.ds(2 * pair, 2)
        return [
            pltpu.make_async_copy(marked.at[two], queries_far.at[two], out_sems.at[first + pair])
        ]

    attended_out = pltpu.make_async_copy(
        attended, attended_far, out_sems.at[4 + len(blocks) + PAIRS]
    )
    lane = lax.broadcasted_iota(jnp.int32, (BLOCK, PAIR), 1)
    upper = lane >= HEAD_DIM
    slot = lane % HEAD_DIM
    finish(ins[:3])
    end0 = lengths[0, 0]
    end1 = end0 + lengths[0, 1]
    end2 = end1 + lengths[0, 2]
    ones = (slot >= 4) & (slot < 7)
    for number, rows in enumerate(blocks):
        norm, _ = standard(tok[rows, :].astype(F32))
        low = (norm * gain1[...]).astype(LOW)
        normed[rows, :] = low
        places = number * BLOCK + lax.broadcasted_iota(jnp.int32, (BLOCK, PAIR), 0)
        document = (
            (places >= end0).astype(jnp.int32)
            + (places >= end1).astype(jnp.int32)
            + (places >= end2).astype(jnp.int32)
        )
        same = slot == document
        key_marks = jnp.where(same | ones, 1.0, 0.0)
        value_marks = jnp.where(ones, 1.0, 0.0)
        query_marks = jnp.where((slot < 4) & ~same, NEGATIVE, 0.0)
        if number == 0:
            finish(ins[3:6])
        query = product(low, w_query[...]) * (HEAD_DIM ** (-0.5))
        key = product(low, w_key[...])
        value = product(low, w_value[...])
        for pair in range(PAIRS):
            cols = slice(pair * PAIR, (pair + 1) * PAIR)
            for half in range(2):
                mine = upper if half else ~upper
                head = 2 * pair + half
                queries[head, rows, :] = jnp.where(mine, query[:, cols], query_marks).astype(LOW)
                keys[head, rows, :] = jnp.where(mine, key[:, cols], key_marks).astype(LOW)
                values[head, rows, :] = jnp.where(mine, value[:, cols], value_marks).astype(LOW)
    begin(outs[:3])

    triangle = lax.broadcasted_iota(jnp.int32, (BLOCK, BLOCK), 1) <= lax.broadcasted_iota(
        jnp.int32, (BLOCK, BLOCK), 0
    )

    def attend(pair, carry):
        work = [(number, half) for number in range(len(blocks)) for half in range(2)]
        results = {}

        def score(item):
            number, half = item
            start = number * BLOCK
            first = max(0, start - LONGEST)
            head = 2 * pair + half
            query = queries[head, blocks[number], :]
            near = jnp.where(triangle, product_nt(query, keys[head, blocks[number], :]), NEGATIVE)
            far = None
            if start > first:
                far = product_nt(query, keys[head, pl.ds(first, start - first), :])
            return query, near, far

        def weigh(item, scored):
            query, near, far = scored
            top = jnp.max(near, axis=1, keepdims=True)
            if far is not None:
                top = jnp.maximum(top, jnp.max(far, axis=1, keepdims=True))
                far = jnp.exp(far - top).astype(LOW)
            return query, jnp.exp(near - top).astype(LOW), far, top

        def gather(item, weighed):
            number, half = item
            query, near, far, top = weighed
            start = number * BLOCK
            first = max(0, start - LONGEST)
            head = 2 * pair + half
            rows = blocks[number]
            out = product(near, values[head, rows, :])
            if far is not None:
                out = out + product(far, values[head, pl.ds(first, start - first), :])
            mark = 4 + HEAD_DIM * (1 - half)
            total = out[:, mark : mark + 1]
            results[item] = out * (1.0 / total)
            high, middle, rest = three_parts(-(top + jnp.log(total)))
            marks = jnp.where(
                lane == mark, high, jnp.where(lane == mark + 1, middle, rest)
            ).astype(LOW)
            marked[head, rows, :] = jnp.where((lane >= mark) & (lane < mark + 3), marks, query)

        scored, weighed = {}, {}
        for index in range(len(work) + 2):
            if index < len(work):
                scored[index] = score(work[index])
            if 1 <= index <= len(work):
                weighed[index - 1] = weigh(work[index - 1], scored[index - 1])
            if index >= 2:
                gather(work[index - 2], weighed[index - 2])
        cols = pl.ds(pl.multiple_of(pair * PAIR, PAIR), PAIR)
        for number, rows in enumerate(blocks):
            attended[rows, cols] = jnp.where(upper, results[number, 1], results[number, 0]).astype(
                LOW
            )
        begin(pair_outs(pair))
        return carry

    lax.fori_loop(0, PAIRS, attend, 0)
    begin([attended_out])
    finish(ins[6:])

    place_group = lax.broadcasted_iota(jnp.int32, (rows_all, width), 0) // GROUP
    lane_group = lax.broadcasted_iota(jnp.int32, (rows_all, width), 1) % groups
    member = jnp.where(place_group == lane_group, 1.0, 0.0).astype(LOW)
    w_wide = widened(w_control, width)
    tops = []
    for number, rows in enumerate(blocks):
        state = tok[rows, :].astype(F32) + product(attended[rows, :], w_out[...])
        hidden[rows, :] = state
        begin(state_outs[number : number + 1])
        norm, _ = standard(state)
        low = (norm * gain2[...]).astype(LOW)
        second[rows, :] = low
        logits = product_nt(low, w_wide)
        places = number * BLOCK + lax.broadcasted_iota(jnp.int32, (BLOCK, rows_all), 0)
        hot = jnp.where(order[...] == places, 1.0, 0.0).astype(LOW)
        inside = product(hot, member)
        logits = jnp.where(inside > 0.5, logits, NEGATIVE)
        spread[rows, :] = logits
        tops.append(jnp.max(logits, axis=0, keepdims=True))
    top = functools.reduce(jnp.maximum, tops)
    total = 0.0
    for rows in blocks:
        expo = jnp.exp(spread[rows, :] - top)
        spread[rows, :] = expo
        total = total + jnp.sum(expo, axis=0, keepdims=True)
    scale = 1.0 / total
    mixed_sum = 0.0
    pulled_sum = 0.0
    for rows in blocks:
        full = spread[rows, :] * scale
        mix[rows, :] = full
        low = full.astype(LOW)
        mixed_sum = mixed_sum + product_tn(low, second[rows, :])
        pulled_sum = pulled_sum + product_tn(low, cot[rows, :])
    begin(outs[3:])
    mixed[...] = mixed_sum.astype(LOW)
    pulled[...] = pulled_sum.astype(LOW)
    share = EXP_DEV * groups
    for step, send in enumerate((send0, send1, send2, send3)):
        part = pl.ds(pl.multiple_of((place[0] ^ step) * share, share), share)
        send[:share, :] = mixed[part, :]
        send[share:, :] = pulled[part, :]
    finish(outs)
    finish(state_outs)
    for pair in range(PAIRS):
        finish(pair_outs(pair))
    finish([attended_out])


def expert_kernel(in0, in1, in2, in3, up, down, out0, out1, out2, out3):
    groups = in0.shape[0] // (2 * EXP_DEV)
    ff = up.shape[2]
    ins = (in0, in1, in2, in3)
    outs = (out0, out1, out2, out3)
    steps = [(expert, first) for expert in range(EXP_DEV) for first in range(0, ff, FF_BLOCK)]
    result = pull = 0.0
    for expert, first in steps:
        part = pl.ds(first, FF_BLOCK)
        own = slice(expert * groups, (expert + 1) * groups)
        back = slice((EXP_DEV + expert) * groups, (EXP_DEV + expert + 1) * groups)
        taken = jnp.concatenate([ref[own, :] for ref in ins], axis=0)
        given = jnp.concatenate([ref[back, :] for ref in ins], axis=0)
        act, slope = gelu_parts(product(taken, up[expert, :, part]))
        grad = (product_nt(given, down[expert, part, :]) * slope).astype(LOW)
        result = result + product(act.astype(LOW), down[expert, part, :])
        pull = pull + product_nt(grad, up[expert, :, part])
        if first + FF_BLOCK == ff:
            for host, ref in enumerate(outs):
                rows = slice(host * groups, (host + 1) * groups)
                ref[own, :] = result[rows].astype(LOW)
                ref[back, :] = pull[rows].astype(LOW)
            result = pull = 0.0


def middle_kernel(
    place,
    near,
    ret0,
    ret1,
    ret2,
    ret3,
    gain2_far,
    w_control_far,
    hidden_far,
    cot_far,
    mix_far,
    attended_far,
    w_out_far,
    output_far,
    grad_hidden_far,
    pulls_far,
    mine_out,
    other_out,
    gain2,
    w_control,
    hidden,
    cot,
    mix,
    attended,
    w_out,
    output,
    grad_hidden,
    pulls,
    result,
    pull,
    second,
    inner,
    grad_attn,
    grad_out,
    in_sems,
    out_sems,
):
    rows_all = hidden.shape[0]
    groups = rows_all // GROUP
    share = EXP_DEV * groups
    blocks = [pl.ds(start, BLOCK) for start in range(0, rows_all, BLOCK)]
    ins = loads(
        [
            (gain2_far, gain2),
            (w_control_far, w_control),
            (mix_far, mix),
            (hidden_far, hidden),
            (cot_far, cot),
            (w_out_far, w_out),
            (attended_far, attended),
        ],
        in_sems,
    )
    begin(ins)
    outs = loads([(output.at[rows], output_far.at[rows]) for rows in blocks], out_sems)
    state_outs = loads(
        [(grad_hidden.at[rows], grad_hidden_far.at[rows]) for rows in blocks],
        out_sems,
        len(blocks),
    )
    pull_outs = loads(
        [(pulls.at[:, rows], pulls_far.at[:, rows]) for rows in blocks],
        out_sems,
        2 * len(blocks),
    )
    lane = lax.broadcasted_iota(jnp.int32, (BLOCK, PAIR), 1)
    upper = lane >= HEAD_DIM
    slot = lane % HEAD_DIM
    crossed = (lax.broadcasted_iota(jnp.int32, (PAIR, PAIR), 0) >= HEAD_DIM) != (
        lax.broadcasted_iota(jnp.int32, (PAIR, PAIR), 1) >= HEAD_DIM
    )
    crossing = jnp.where(crossed, -1.0, 0.0).astype(LOW)
    for step, ret in enumerate((ret0, ret1, ret2, ret3)):
        part = pl.ds(pl.multiple_of((place[0] ^ step) * share, share), share)
        result[part, :] = ret[:share, :]
        pull[part, :] = ret[share:, :]
    finish(ins[:5])
    total = 0.0
    for number, rows in enumerate(blocks):
        state = hidden[rows, :]
        norm, _ = standard(state)
        low = (norm * gain2[...]).astype(LOW)
        second[rows, :] = low
        full = mix[rows, :]
        output[rows, :] = (state + product(full.astype(LOW), result[...])).astype(LOW)
        begin(outs[number : number + 1])
        grad_mix = product_nt(cot[rows, :], result[...]) + product_nt(low, pull[...])
        weighted = full * grad_mix
        inner[rows, :] = weighted
        total = total + jnp.sum(weighted, axis=0, keepdims=True)
    finish(ins[5:])
    w_wide = widened(w_control, mix.shape[1])
    control = 0.0
    gain = 0.0
    for number, rows in enumerate(blocks):
        full = mix[rows, :]
        grad_logits = (inner[rows, :] - full * total).astype(LOW)
        grad_second = product(full.astype(LOW), pull[...]) + product(grad_logits, w_wide)
        control = control + product_tn(grad_logits, second[rows, :])
        norm, inverse = standard(hidden[rows, :])
        gain = gain + jnp.sum(grad_second * norm, axis=0, keepdims=True)
        grad_state = cot[rows, :].astype(F32) + standard_pull(
            norm, inverse, grad_second * gain2[...]
        )
        grad_hidden[rows, :] = grad_state
        begin(state_outs[number : number + 1])
        low = grad_state.astype(LOW)
        grad_attn[rows, :] = low
        grad_att = product_nt(low, w_out[...]).astype(LOW).astype(F32)
        shared = grad_att * attended[rows, :].astype(F32)
        for pair in range(PAIRS):
            cols = slice(pair * PAIR, (pair + 1) * PAIR)
            top = shared[:, cols].astype(LOW)
            rest = (shared[:, cols] - top.astype(F32)).astype(LOW)
            delta = product(top, crossing) + product(rest, crossing)
            high, middle, last = three_parts(delta)
            marks = jnp.where(
                slot == 4,
                high,
                jnp.where(slot == 5, middle, jnp.where(slot == 6, last, 0.0)),
            )
            for half in range(2):
                mine = upper if half else ~upper
                pulls[2 * pair + half, rows, :] = jnp.where(mine, grad_att[:, cols], marks).astype(
                    LOW
                )
        begin(pull_outs[number : number + 1])
    grad_out[:, :D] = product_tn(attended[...], grad_attn[...]).astype(LOW)
    experts = control.shape[0] // groups
    small = jnp.concatenate(
        (
            jnp.sum(control.reshape(experts, groups, D), axis=1),
            jnp.broadcast_to(gain, (PAIR - experts, D)),
        ),
        axis=0,
    )
    grad_out[:, D:] = small.T.astype(LOW)
    half = D // 2
    mine_out[...] = grad_out[pl.ds(pl.multiple_of(near[0] * half, half), half), :]
    other_out[...] = grad_out[pl.ds(pl.multiple_of((1 - near[0]) * half, half), half), :]
    finish(outs)
    finish(state_outs)
    finish(pull_outs)


def pair_kernel(
    near,
    queries_far,
    keys_far,
    values_far,
    pulls_far,
    normed_far,
    grads_far,
    mine_out,
    other_out,
    queries,
    keys,
    values,
    pulls,
    normed,
    grads,
    grad_query,
    weights,
    in_sems,
    out_sems,
):
    rows_all = normed.shape[0]
    lane = lax.broadcasted_iota(jnp.int32, (BLOCK, PAIR), 1)
    upper = lane >= HEAD_DIM
    triangle = lax.broadcasted_iota(jnp.int32, (BLOCK, BLOCK), 0) <= lax.broadcasted_iota(
        jnp.int32, (BLOCK, BLOCK), 1
    )

    def ins(pair):
        two = pl.ds(2 * pair, 2)
        return loads(
            [
                (keys_far.at[two], keys.at[two]),
                (queries_far.at[two], queries.at[two]),
                (values_far.at[two], values.at[two]),
                (pulls_far.at[two], pulls.at[two]),
            ],
            in_sems,
            4 * pair,
        )

    def outs(pair):
        return loads([(grads.at[pair], grads_far.at[pair])], out_sems, pair)

    begin(ins(0))
    norm_in = loads([(normed_far, normed)], in_sems, 4 * PAIRS)
    begin(ins(1))
    begin(norm_in)
    for pair in range(2, PAIRS):
        begin(ins(pair))

    def one_pair(pair, carry):
        finish(ins(pair))
        work = [(start, half) for start in range(0, rows_all, BLOCK) for half in range(2)]
        seen = set()
        halves = {}

        def score(item):
            start, half = item
            head = 2 * pair + half
            rows = pl.ds(start, BLOCK)
            key, value = keys[head, rows, :], values[head, rows, :]
            parts = [rows]
            if start + BLOCK < rows_all:
                after = min(rows_all, start + BLOCK + LONGEST) - (start + BLOCK)
                parts.append(pl.ds(start + BLOCK, after))
            made = []
            for number, part in enumerate(parts):
                scores = product_nt(key, queries[head, part, :])
                if number == 0:
                    scores = jnp.where(triangle, scores, NEGATIVE)
                made.append((part, scores, product_nt(value, pulls[head, part, :])))
            return key, made

        def weigh(scored):
            key, made = scored
            done = []
            for part, scores, grad_probs in made:
                probs = jnp.exp(scores)
                done.append((part, probs.astype(LOW), (probs * grad_probs).astype(LOW)))
            return key, done

        def gather(item, weighed):
            start, half = item
            head = 2 * pair + half
            key, done = weighed
            key = jnp.where(upper if half else ~upper, key, jnp.zeros_like(key))
            grad_key = 0.0
            grad_value = 0.0
            for part, probs, grad_scores in done:
                grad_value = grad_value + product(probs, pulls[head, part, :])
                grad_key = grad_key + product(grad_scores, queries[head, part, :])
                both = product_tn(grad_scores, key)
                for offset in range(0, part.size, BLOCK):
                    at = part.start + offset
                    piece = both[offset : offset + BLOCK]
                    if at in seen:
                        grad_query[pl.ds(at, BLOCK), :] += piece
                    else:
                        grad_query[pl.ds(at, BLOCK), :] = piece
                        seen.add(at)
            halves[start, half] = grad_key, grad_value
            if half == 1:
                rows = pl.ds(start, BLOCK)
                grads[pair, rows, PAIR : 2 * PAIR] = jnp.where(
                    upper, halves[start, 1][0], halves[start, 0][0]
                ).astype(LOW)
                grads[pair, rows, 2 * PAIR :] = jnp.where(
                    upper, halves[start, 1][1], halves[start, 0][1]
                ).astype(LOW)

        scored, weighed = {}, {}
        for index in range(len(work) + 2):
            if index < len(work):
                scored[index] = score(work[index])
            if 1 <= index <= len(work):
                weighed[index - 1] = weigh(scored[index - 1])
            if index >= 2:
                gather(work[index - 2], weighed[index - 2])
        grads[pair, :, :PAIR] = (grad_query[...] * (HEAD_DIM ** (-0.5))).astype(LOW)
        begin(outs(pair))

        @pl.when(pair == 0)
        def _():
            finish(norm_in)

        cols = pl.ds(pl.multiple_of(pair * 3 * PAIR, PAIR), 3 * PAIR)
        weights[:, cols] = product_tn(normed[...], grads[pair]).astype(LOW)
        return carry

    lax.fori_loop(0, PAIRS, one_pair, 0)
    half = D // 2
    mine_out[...] = weights[pl.ds(pl.multiple_of(near[0] * half, half), half), :]
    other_out[...] = weights[pl.ds(pl.multiple_of((1 - near[0]) * half, half), half), :]
    for pair in range(PAIRS):
        finish(outs(pair))


def last_kernel(grads, tok, grad_hidden, gain1, w_query, w_key, w_value, grad_tokens):
    parts = [grads[pair] for pair in range(PAIRS)]
    grad_normed = 0.0
    for number, weight in enumerate((w_query, w_key, w_value)):
        cols = slice(number * PAIR, (number + 1) * PAIR)
        joined = jnp.concatenate([part[:, cols] for part in parts], axis=1)
        grad_normed = grad_normed + product_nt(joined, weight[...])
    norm, inverse = standard(tok[...].astype(F32))
    grad_tokens[...] = (
        grad_hidden[...] + standard_pull(norm, inverse, grad_normed * gain1[...])
    ).astype(LOW)


def weight_kernel(expert, count, place, *refs):
    pieces = refs[:count]
    up, down = refs[count : count + 2]
    grad_up, grad_down, taken, given, held = refs[-5:]
    step = pl.program_id(0)
    share = PAIR
    groups = share // (2 * EXP_DEV)
    strip_rows, strip_ff = grad_up.shape[1], grad_down.shape[1]
    first = place[0] * strip_rows
    wide = pl.multiple_of(first // PAIR * PAIR, PAIR)
    inside = pl.ds(pl.multiple_of(first % PAIR, strip_rows), strip_rows)

    @pl.when(step == 0)
    def _():
        filled = 0
        for piece in pieces:
            for start in range(0, piece.shape[0], share):
                target = pl.ds(filled, groups)
                taken[target, :] = piece[
                    start + expert * groups : start + (expert + 1) * groups, :
                ]
                back = start + (EXP_DEV + expert) * groups
                given[target, :] = piece[back : back + groups, :]
                filled += groups

    rows_all = taken.shape[0]
    size = min(512, rows_all)
    ff_first = place[0] * strip_ff
    owner = step == ff_first // FF_BLOCK
    total = 0.0
    acts = []
    for start in range(0, rows_all, size):
        rows = pl.ds(start, size)
        act, slope = gelu_parts(product(taken[rows, :], up[0]))
        grad = (product_nt(given[rows, :], down[0]) * slope).astype(LOW)
        total = total + product_tn(taken[rows, pl.ds(wide, PAIR)], grad)
        acts.append(act.astype(LOW))
    held[:PAIR, :] = total
    grad_up[0] = held[inside, :]

    @pl.when(owner)
    def _():
        whole = 0.0
        for number, act in enumerate(acts):
            whole = whole + product_tn(act, given[pl.ds(number * size, size), :])
        held[...] = whole
        grad_down[0] = held[pl.ds(pl.multiple_of(ff_first % FF_BLOCK, strip_ff), strip_ff), :]


def join_kernel(mine_out, swapped_out, mine, swapped, sums):
    first = mine_out.shape[1]
    sums[:, :first] = (mine_out[...].astype(F32) + swapped_out[...].astype(F32)).astype(LOW)
    sums[:, first:] = (mine[...].astype(F32) + swapped[...].astype(F32)).astype(LOW)


def total_kernel(parts, spread):
    total = parts[0].astype(F32)
    for number in range(1, parts.shape[0]):
        total = total + parts[number].astype(F32)
    total = total.astype(LOW)
    for number in range(parts.shape[0]):
        spread[number] = total


def assemble_kernel(
    near,
    both_own,
    both_other,
    gain1_far,
    w_query_far,
    w_key_far,
    w_value_far,
    grad_query_far,
    grad_key_far,
    grad_value_far,
    grad_out_far,
    grad_control,
    grad_gain1,
    grad_gain2,
    gain1,
    weights,
    squares,
    columns,
    in_sems,
    out_sems,
):
    ins = loads(
        [
            (gain1_far, gain1),
            (w_query_far, weights.at[0]),
            (w_key_far, weights.at[1]),
            (w_value_far, weights.at[2]),
        ],
        in_sems,
    )
    begin(ins)
    half = D // 2
    experts = grad_control.shape[0]
    targets = (grad_query_far, grad_key_far, grad_value_far, grad_out_far)
    lane = lax.broadcasted_iota(jnp.int32, (half, PAIR), 1)
    outs = []
    for step, both in enumerate((both_own, both_other)):
        side = near[0] if step == 0 else 1 - near[0]
        rows = pl.ds(pl.multiple_of(side * half, half), half)
        outs.append(
            loads(
                [
                    (squares.at[number, rows], target.at[rows])
                    for number, target in enumerate(targets)
                ],
                out_sems,
                len(targets) * step,
            )
        )
        squares[3, rows, :] = both[:, :D].astype(F32)
        begin(outs[-1][3:])
        if step == 0:
            finish(ins)
        shared = 0.0
        for number in range(3):
            for pair in range(PAIRS):
                first = D + PAIR + (3 * pair + number) * PAIR
                part = both[:, first : first + PAIR].astype(F32)
                cols = slice(pair * PAIR, (pair + 1) * PAIR)
                squares[number, rows, cols] = part
                shared = shared + part * weights[number, rows, cols].astype(F32)
            begin(outs[-1][number : number + 1])
        columns[rows, :] = jnp.where(
            lane == experts + 1,
            jnp.sum(shared, axis=1, keepdims=True),
            both[:, D : D + PAIR].astype(F32),
        )
    turned = columns[...].T
    grad_control[...] = turned[:experts]
    grad_gain2[...] = turned[experts : experts + 1]
    grad_gain1[...] = turned[experts + 1 : experts + 2] / gain1[...]
    for one in outs:
        finish(one)


def vmem():
    return pl.BlockSpec(memory_space=pltpu.VMEM)


def smem():
    return pl.BlockSpec(memory_space=pltpu.SMEM)


def far():
    return pl.BlockSpec(memory_space=pltpu.HBM)


def shape(*sizes, kind=LOW):
    return jax.ShapeDtypeStruct(sizes, kind)


def params(mib):
    return pltpu.CompilerParams(vmem_limit_bytes=mib * MIB)


def cost(flops, moved):
    return pl.CostEstimate(flops=int(flops), bytes_accessed=int(moved), transcendentals=0)


def ring_of(count):
    order = list(range(0, count, 2)) + list(range(count - 1, 0, -2))
    ahead = [(order[i], order[(i + 1) % count]) for i in range(count)]
    return ahead, [(target, source) for source, target in ahead]


def dma(count):
    return pltpu.SemaphoreType.DMA((count,))


def forward_call(lengths, place, order, gain1, gain2, tokens, cot, weights, w_control, experts):
    rows = tokens.shape[0]
    groups = rows // GROUP
    wide = experts * groups
    blocks = rows // BLOCK
    heads = (HEADS, rows, PAIR)
    kept = [
        ((rows, D), F32),
        ((rows, wide), F32),
        ((rows, D), LOW),
        (heads, LOW),
        (heads, LOW),
        (heads, LOW),
        ((rows, D), LOW),
    ]
    results = pl.pallas_call(
        forward_kernel,
        in_specs=[smem()] + [far()] * 11,
        out_specs=[vmem()] * 4 + [far()] * 7,
        out_shape=[shape(2 * EXP_DEV * groups, D)] * 4
        + [shape(*size, kind=kind) for size, kind in kept],
        scratch_shapes=[
            pltpu.SMEM(lengths.shape, jnp.int32),
            pltpu.VMEM(order.shape, jnp.int32),
            pltpu.VMEM((1, D), F32),
            pltpu.VMEM((1, D), F32),
            pltpu.VMEM((experts, D), LOW),
        ]
        + [pltpu.VMEM((rows, D), LOW)] * 2
        + [pltpu.VMEM((D, D), LOW)] * 4
        + [pltpu.VMEM(*one) for one in kept]
        + [
            pltpu.VMEM((rows, D), LOW),
            pltpu.VMEM((rows, wide), F32),
            pltpu.VMEM((wide, D), LOW),
            pltpu.VMEM((wide, D), LOW),
            pltpu.VMEM(heads, LOW),
            dma(11),
            dma(4 + blocks + PAIRS + 1),
        ],
        compiler_params=pltpu.CompilerParams(vmem_limit_bytes=56623104),
        cost_estimate=cost(2e10, 2e7),
    )(place, lengths, order, gain1, gain2, w_control, tokens, cot, *weights)
    return results[:4], results[4:]


def expert_call(arrived, w_up, w_down):
    size, _ = arrived[0].shape
    return pl.pallas_call(
        expert_kernel,
        in_specs=[vmem()] * (len(arrived) + 2),
        out_specs=[vmem()] * len(arrived),
        out_shape=[shape(size, D)] * len(arrived),
        compiler_params=params(16),
        cost_estimate=cost(5e9, 1e7),
    )(*arrived, w_up, w_down)


def middle_call(place, near, returned, gain2, w_control, hidden, cot, mix, attended, w_out):
    rows, wide = mix.shape
    blocks = rows // BLOCK
    taken = [
        ((rows, D), F32),
        ((rows, D), LOW),
        ((rows, wide), F32),
        ((rows, D), LOW),
        ((D, D), LOW),
    ]
    made = [((rows, D), LOW), ((rows, D), F32), ((HEADS, rows, PAIR), LOW)]
    part = shape(D // 2, D + PAIR)
    return pl.pallas_call(
        middle_kernel,
        in_specs=[smem()] * 2 + [vmem()] * 4 + [far()] * 7,
        out_specs=[far()] * 3 + [vmem()] * 2,
        out_shape=[shape(*size, kind=kind) for size, kind in made] + [part, part],
        scratch_shapes=[pltpu.VMEM((1, D), F32), pltpu.VMEM(w_control.shape, LOW)]
        + [pltpu.VMEM(*one) for one in taken + made]
        + [
            pltpu.VMEM((wide, D), LOW),
            pltpu.VMEM((wide, D), LOW),
            pltpu.VMEM((rows, D), LOW),
            pltpu.VMEM((rows, wide), F32),
            pltpu.VMEM((rows, D), LOW),
            pltpu.VMEM((D, D + PAIR), LOW),
            dma(7),
            dma(3 * blocks),
        ],
        compiler_params=params(28),
        cost_estimate=cost(8e9, 1.5e7),
    )(place, near, *returned, gain2, w_control, hidden, cot, mix, attended, w_out)


def pair_call(near, queries, keys, values, pulls, normed):
    rows = normed.shape[0]
    half = shape(D // 2, 3 * PAIRS * PAIR)
    return pl.pallas_call(
        pair_kernel,
        in_specs=[smem()] + [far()] * 5,
        out_specs=[far()] + [vmem()] * 2,
        out_shape=[shape(PAIRS, rows, 3 * PAIR), half, half],
        scratch_shapes=[pltpu.VMEM((HEADS, rows, PAIR), LOW)] * 4
        + [
            pltpu.VMEM((rows, D), LOW),
            pltpu.VMEM((PAIRS, rows, 3 * PAIR), LOW),
            pltpu.VMEM((rows, PAIR), F32),
            pltpu.VMEM((D, 3 * PAIRS * PAIR), LOW),
            dma(4 * PAIRS + 1),
            dma(PAIRS),
        ],
        compiler_params=params(32),
        cost_estimate=cost(2e10, 1.2e7),
    )(near, queries, keys, values, pulls, normed)


def weight_call(expert, copy, pieces, w_up, w_down, copies, earlier):
    ff = w_up.shape[2]
    held = sum(piece.shape[0] for piece in pieces)
    every = held // (2 * EXP_DEV)
    whole = [pl.BlockSpec(one.shape, lambda f: (0, 0)) for one in pieces]
    return pl.pallas_call(
        functools.partial(weight_kernel, expert, len(pieces)),
        grid=(ff // FF_BLOCK,),
        in_specs=[smem()]
        + whole
        + [
            pl.BlockSpec((1, D, FF_BLOCK), lambda f: (expert, 0, f)),
            pl.BlockSpec((1, FF_BLOCK, D), lambda f: (expert, f, 0)),
        ]
        + [far()] * len(earlier),
        out_specs=[
            pl.BlockSpec((1, D // copies, FF_BLOCK), lambda f: (expert, 0, f)),
            pl.BlockSpec((1, ff // copies, D), lambda f: (expert, 0, 0)),
        ],
        out_shape=[
            shape(EXP_DEV, D // copies, ff, kind=F32),
            shape(EXP_DEV, ff // copies, D, kind=F32),
        ],
        scratch_shapes=[
            pltpu.VMEM((every, D), LOW),
            pltpu.VMEM((every, D), LOW),
            pltpu.VMEM((FF_BLOCK, D), F32),
        ],
        input_output_aliases={3 + len(pieces) + i: i for i in range(len(earlier))},
        compiler_params=params(40),
        cost_estimate=cost(1e10, 8e6),
    )(copy, *pieces, w_up, w_down, *earlier)


def last_call(grads, tokens, grad_hidden, gain1, weights):
    rows = tokens.shape[0]
    row_block = lambda i: (i, 0)
    fixed = lambda i: (0, 0)
    return pl.pallas_call(
        last_kernel,
        grid=(rows // BLOCK,),
        in_specs=[pl.BlockSpec((PAIRS, BLOCK, 3 * PAIR), lambda i: (0, i, 0))]
        + [pl.BlockSpec((BLOCK, D), row_block)] * 2
        + [pl.BlockSpec((1, D), fixed)]
        + [pl.BlockSpec((D, D), fixed)] * 3,
        out_specs=pl.BlockSpec((BLOCK, D), row_block),
        out_shape=shape(rows, D),
        compiler_params=params(32),
        cost_estimate=cost(2e9, 8e6),
    )(grads, tokens, grad_hidden, gain1, *weights)


def join_call(*parts):
    rows = parts[0].shape[0]
    return pl.pallas_call(
        join_kernel,
        in_specs=[vmem()] * 4,
        out_specs=vmem(),
        out_shape=shape(rows, parts[0].shape[1] + parts[2].shape[1]),
        compiler_params=params(16),
        cost_estimate=cost(1e6, 3e6),
    )(*parts)


def total_call(parts):
    return pl.pallas_call(
        total_kernel,
        in_specs=[vmem()],
        out_specs=vmem(),
        out_shape=shape(*parts.shape),
        compiler_params=params(16),
        cost_estimate=cost(1e6, 3e6),
    )(parts)


def assemble_call(near, both_own, both_other, gain1, weights, experts):
    square = shape(D, D, kind=F32)
    return pl.pallas_call(
        assemble_kernel,
        in_specs=[smem()] + [vmem()] * 2 + [far()] * 4,
        out_specs=[far()] * 4 + [vmem()] * 3,
        out_shape=[square] * 4 + [shape(experts, D, kind=F32)] + [shape(1, D, kind=F32)] * 2,
        scratch_shapes=[
            pltpu.VMEM((1, D), F32),
            pltpu.VMEM((3, D, D), LOW),
            pltpu.VMEM((4, D, D), F32),
            pltpu.VMEM((D, PAIR), F32),
            dma(4),
            dma(8),
        ],
        compiler_params=params(40),
        cost_estimate=cost(1e8, 6e6),
    )(near, both_own, both_other, gain1, *weights)


def in_order(*values):
    return lax.optimization_barrier(values)


def shards(
    tokens,
    doc_lengths,
    group_order,
    ln1_gain,
    w_query,
    w_key,
    w_value,
    w_out,
    ln2_gain,
    w_control,
    w_up,
    w_down,
    cotangent,
):
    copies, far_hosts, near_hosts = (lax.axis_size(name) for name in ("dp", "far", "near"))
    hosts = far_hosts * near_hosts
    hosts_axes = ("far", "near")
    axes = ("dp", "far")
    count = copies * far_hosts
    experts = hosts * EXP_DEV
    place = lax.axis_index(hosts_axes).astype(jnp.int32).reshape(1)
    near = lax.axis_index("near").astype(jnp.int32).reshape(1)
    copy = lax.axis_index("dp").astype(jnp.int32).reshape(1)
    gain1 = ln1_gain.reshape(1, D)
    gain2 = ln2_gain.reshape(1, D)
    weights = (w_query, w_key, w_value)
    w_control = w_control.T
    ahead, behind = ring_of(copies)
    steps_left = copies // 2 - 1
    pieces = []

    def exchange(parts):
        return [parts[0]] + [
            lax.ppermute(parts[step], hosts_axes, [(i, i ^ step) for i in range(hosts)])
            for step in range(1, hosts)
        ]

    def pass_on(ahead_part, behind_part):
        return lax.ppermute(ahead_part, "dp", ahead), lax.ppermute(behind_part, "dp", behind)

    def next_step(moving):
        nonlocal steps_left
        pieces.extend(moving)
        steps_left -= 1
        if steps_left > 0:
            return pass_on(*moving)
        half = moving[0].shape[0] // 2
        return pass_on(moving[0][:half], moving[1][half:])

    def near_swap(values):
        return lax.ppermute(values, "near", [(i, i ^ 1) for i in range(near_hosts)])

    def scatter(half):
        rows, cols = half.shape
        return lax.all_to_all(half.reshape(count, rows // count, cols), axes, 0, 0, tiled=True)

    def spread(own):
        return lax.all_to_all(own, axes, 0, 0, tiled=True).reshape(-1, own.shape[-1])

    with jax.named_scope("attention_and_mixing"):
        sends, kept = forward_call(
            doc_lengths,
            place,
            group_order,
            gain1,
            gain2,
            tokens,
            cotangent,
            (*weights, w_out),
            w_control,
            experts,
        )
        hidden, mix, normed, queries, keys, values, attended = kept
    with jax.named_scope("to_experts"):
        arrived = exchange(sends)
    with jax.named_scope("gather_for_weights"):
        own = jnp.concatenate(arrived, axis=0)
        pieces.append(own)
        moving = pass_on(own, own)
    with jax.named_scope("experts"):
        results = expert_call(arrived, w_up, w_down)
    with jax.named_scope("from_experts"):
        returned = exchange(results)
    with jax.named_scope("gather_for_weights"):
        moving = next_step(moving)
    with jax.named_scope("mixing_backward"):
        output, grad_hidden, pulls, mine_out, other_out = middle_call(
            place, near, returned, gain2, w_control, hidden, cotangent, mix, attended, w_out
        )
    with jax.named_scope("gather_for_weights"):
        pulls, other_out, moving = in_order(pulls, other_out, moving)
        moving = next_step(moving)
    with jax.named_scope("reduce"):
        swapped_out = near_swap(other_out)
    with jax.named_scope("attention_backward"):
        grads, mine, other = pair_call(near, queries, keys, values, pulls, normed)
        mine, other, moving, swapped_out = in_order(mine, other, moving, swapped_out)
    with jax.named_scope("gather_for_weights"):
        while steps_left > 0:
            moving = next_step(moving)
    with jax.named_scope("reduce"):
        sums = join_call(mine_out, swapped_out, mine, near_swap(other))
        sums, grads, moving = in_order(sums, grads, moving)
        pieces.extend(moving)
        sums = scatter(sums)
    with jax.named_scope("norm_backward"):
        grad_tokens = last_call(grads, tokens, grad_hidden, gain1, weights)
    with jax.named_scope("expert_weights"):
        grads_expert = weight_call(0, copy, pieces, w_up, w_down, copies, ())
        sums, grads_expert, grad_tokens = in_order(sums, grads_expert, grad_tokens)
    with jax.named_scope("reduce"):
        sums = total_call(sums)
        sums, grads_expert = in_order(sums, grads_expert)
        sums = spread(sums)
    with jax.named_scope("expert_weights"):
        grad_up, grad_down = weight_call(1, copy, pieces, w_up, w_down, copies, grads_expert)
        sums, grad_up, grad_down = in_order(sums, grad_up, grad_down)
    with jax.named_scope("reduce"):
        sums_other = near_swap(sums)
    with jax.named_scope("assemble"):
        grad_query, grad_key, grad_value, grad_out, grad_control, grad_gain1, grad_gain2 = (
            assemble_call(near, sums, sums_other, gain1, weights, experts)
        )
    return (
        output,
        grad_tokens,
        grad_gain1.reshape(D),
        grad_query,
        grad_key,
        grad_value,
        grad_out,
        grad_gain2.reshape(D),
        grad_control.T,
        grad_up,
        grad_down,
    )


def solution(mesh):
    copies, hosts = mesh.shape["dp"], mesh.shape["expert"]
    finer = jax.sharding.Mesh(mesh.devices.reshape(copies, hosts // 2, 2), ("dp", "far", "near"))
    every = P(("dp", "far", "near"), None)
    expert = P(("far", "near"), None, None)
    sliced = P(("far", "near"), "dp", None)
    return jax.shard_map(
        shards,
        mesh=finer,
        in_specs=(every,) * 3 + (P(),) * 7 + (expert,) * 2 + (every,),
        out_specs=(every,) * 2 + (P(),) * 7 + (sliced,) * 2,
        check_vma=False,
    )
```

```python
import functools

import jax
import jax.numpy as jnp
from jax import lax
from jax.experimental import pallas as pl
from jax.experimental.pallas import tpu as pltpu
from jax.sharding import PartitionSpec as P

D = 512
HEADS = 8
HEAD_DIM = 64
PAIRS = 4
PAIR = 2 * HEAD_DIM
GROUP = 32
EXP_DEV = 2
LONGEST = 512
BLOCK = 256
FF_BLOCK = 512
EPSILON = 1e-05
NEGATIVE = -1e30
MIB = 1 << 20

F32 = jnp.float32
LOW = jnp.bfloat16


def product(left, right):
    return jnp.dot(left, right, preferred_element_type=F32)


def product_nt(left, right):
    return lax.dot_general(left, right, (((1,), (1,)), ((), ())), preferred_element_type=F32)


def product_tn(left, right):
    return lax.dot_general(left, right, (((0,), (0,)), ((), ())), preferred_element_type=F32)


def standard(values):
    center = values - jnp.mean(values, axis=-1, keepdims=True)
    inverse = lax.rsqrt(jnp.mean(center * center, axis=-1, keepdims=True) + EPSILON)
    return center * inverse, inverse


def standard_pull(norm, inverse, grad):
    return (
        grad
        - jnp.mean(grad, axis=-1, keepdims=True)
        - norm * jnp.mean(grad * norm, axis=-1, keepdims=True)
    ) * inverse


def gelu_parts(values):
    square = values * values
    tanh = jnp.tanh(0.7978845608028654 * values * (1.0 + 0.044715 * square))
    half = 0.5 + 0.5 * tanh
    slope = half + values * (0.5 - 0.5 * tanh * tanh) * (
        0.7978845608028654 + 0.10703222440890037 * square
    )
    return values * half, slope


def three_parts(values):
    high = values.astype(LOW).astype(F32)
    rest = values - high
    middle = rest.astype(LOW).astype(F32)
    return high, middle, rest - middle


def begin(copies):
    for copy in copies:
        copy.start()


def finish(copies):
    for copy in copies:
        copy.wait()


def loads(pairs, sems, first=0):
    return [
        pltpu.make_async_copy(source, target, sems.at[first + number])
        for number, (source, target) in enumerate(pairs)
    ]


def widened(w_control, width):
    experts = w_control.shape[0]
    lane = lax.broadcasted_iota(jnp.int32, (experts, width), 1) // (width // experts)
    row = lax.broadcasted_iota(jnp.int32, (experts, width), 0)
    return product_tn(jnp.where(lane == row, 1.0, 0.0).astype(LOW), w_control[...]).astype(LOW)


def forward_kernel(
    place,
    lengths_far,
    order_far,
    gain1_far,
    gain2_far,
    w_control_far,
    tok_far,
    cot_far,
    w_query_far,
    w_key_far,
    w_value_far,
    w_out_far,
    send0,
    send1,
    send2,
    send3,
    hidden_far,
    mix_far,
    normed_far,
    queries_far,
    keys_far,
    values_far,
    attended_far,
    lengths,
    order,
    gain1,
    gain2,
    w_control,
    tok,
    cot,
    w_query,
    w_key,
    w_value,
    w_out,
    hidden,
    mix,
    normed,
    queries,
    keys,
    values,
    attended,
    second,
    spread,
    mixed,
    pulled,
    marked,
    in_sems,
    out_sems,
):
    rows_all = tok.shape[0]
    groups = rows_all // GROUP
    width = mix.shape[1]
    ins = loads(
        [
            (tok_far, tok),
            (gain1_far, gain1),
            (lengths_far, lengths),
            (w_query_far, w_query),
            (w_key_far, w_key),
            (w_value_far, w_value),
            (w_out_far, w_out),
            (gain2_far, gain2),
            (w_control_far, w_control),
            (order_far, order),
            (cot_far, cot),
        ],
        in_sems,
    )
    begin(ins)
    blocks = [pl.ds(start, BLOCK) for start in range(0, rows_all, BLOCK)]
    outs = loads(
        [(normed, normed_far), (keys, keys_far), (values, values_far), (mix, mix_far)], out_sems
    )
    state_outs = loads([(hidden.at[rows], hidden_far.at[rows]) for rows in blocks], out_sems, 4)

    def pair_outs(pair):
        first = 4 + len(blocks)
        two = pl.ds(2 * pair, 2)
        return [
            pltpu.make_async_copy(marked.at[two], queries_far.at[two], out_sems.at[first + pair])
        ]

    attended_out = pltpu.make_async_copy(
        attended, attended_far, out_sems.at[4 + len(blocks) + PAIRS]
    )
    lane = lax.broadcasted_iota(jnp.int32, (BLOCK, PAIR), 1)
    upper = lane >= HEAD_DIM
    slot = lane % HEAD_DIM
    finish(ins[:3])
    end0 = lengths[0, 0]
    end1 = end0 + lengths[0, 1]
    end2 = end1 + lengths[0, 2]
    ones = (slot >= 4) & (slot < 7)
    for number, rows in enumerate(blocks):
        norm, _ = standard(tok[rows, :].astype(F32))
        low = (norm * gain1[...]).astype(LOW)
        normed[rows, :] = low
        places = number * BLOCK + lax.broadcasted_iota(jnp.int32, (BLOCK, PAIR), 0)
        document = (
            (places >= end0).astype(jnp.int32)
            + (places >= end1).astype(jnp.int32)
            + (places >= end2).astype(jnp.int32)
        )
        same = slot == document
        key_marks = jnp.where(same | ones, 1.0, 0.0)
        value_marks = jnp.where(ones, 1.0, 0.0)
        query_marks = jnp.where((slot < 4) & ~same, NEGATIVE, 0.0)
        if number == 0:
            finish(ins[3:6])
        query = product(low, w_query[...]) * (HEAD_DIM ** (-0.5))
        key = product(low, w_key[...])
        value = product(low, w_value[...])
        for pair in range(PAIRS):
            cols = slice(pair * PAIR, (pair + 1) * PAIR)
            for half in range(2):
                mine = upper if half else ~upper
                head = 2 * pair + half
                queries[head, rows, :] = jnp.where(mine, query[:, cols], query_marks).astype(LOW)
                keys[head, rows, :] = jnp.where(mine, key[:, cols], key_marks).astype(LOW)
                values[head, rows, :] = jnp.where(mine, value[:, cols], value_marks).astype(LOW)
    begin(outs[:3])

    triangle = lax.broadcasted_iota(jnp.int32, (BLOCK, BLOCK), 1) <= lax.broadcasted_iota(
        jnp.int32, (BLOCK, BLOCK), 0
    )

    def attend(pair, carry):
        work = [(number, half) for number in range(len(blocks)) for half in range(2)]
        results = {}

        def score(item):
            number, half = item
            start = number * BLOCK
            first = max(0, start - LONGEST)
            head = 2 * pair + half
            query = queries[head, blocks[number], :]
            near = jnp.where(triangle, product_nt(query, keys[head, blocks[number], :]), NEGATIVE)
            far = None
            if start > first:
                far = product_nt(query, keys[head, pl.ds(first, start - first), :])
            return query, near, far

        def weigh(item, scored):
            query, near, far = scored
            top = jnp.max(near, axis=1, keepdims=True)
            if far is not None:
                top = jnp.maximum(top, jnp.max(far, axis=1, keepdims=True))
                far = jnp.exp(far - top).astype(LOW)
            return query, jnp.exp(near - top).astype(LOW), far, top

        def gather(item, weighed):
            number, half = item
            query, near, far, top = weighed
            start = number * BLOCK
            first = max(0, start - LONGEST)
            head = 2 * pair + half
            rows = blocks[number]
            out = product(near, values[head, rows, :])
            if far is not None:
                out = out + product(far, values[head, pl.ds(first, start - first), :])
            mark = 4 + HEAD_DIM * (1 - half)
            total = out[:, mark : mark + 1]
            results[item] = out * (1.0 / total)
            high, middle, rest = three_parts(-(top + jnp.log(total)))
            marks = jnp.where(
                lane == mark, high, jnp.where(lane == mark + 1, middle, rest)
            ).astype(LOW)
            marked[head, rows, :] = jnp.where((lane >= mark) & (lane < mark + 3), marks, query)

        scored, weighed = {}, {}
        for index in range(len(work) + 2):
            if index < len(work):
                scored[index] = score(work[index])
            if 1 <= index <= len(work):
                weighed[index - 1] = weigh(work[index - 1], scored[index - 1])
            if index >= 2:
                gather(work[index - 2], weighed[index - 2])
        cols = pl.ds(pl.multiple_of(pair * PAIR, PAIR), PAIR)
        for number, rows in enumerate(blocks):
            attended[rows, cols] = jnp.where(upper, results[number, 1], results[number, 0]).astype(
                LOW
            )
        begin(pair_outs(pair))
        return carry

    lax.fori_loop(0, PAIRS, attend, 0)
    begin([attended_out])
    finish(ins[6:])

    place_group = lax.broadcasted_iota(jnp.int32, (rows_all, width), 0) // GROUP
    lane_group = lax.broadcasted_iota(jnp.int32, (rows_all, width), 1) % groups
    member = jnp.where(place_group == lane_group, 1.0, 0.0).astype(LOW)
    w_wide = widened(w_control, width)
    tops = []
    for number, rows in enumerate(blocks):
        state = tok[rows, :].astype(F32) + product(attended[rows, :], w_out[...])
        hidden[rows, :] = state
        begin(state_outs[number : number + 1])
        norm, _ = standard(state)
        low = (norm * gain2[...]).astype(LOW)
        second[rows, :] = low
        logits = product_nt(low, w_wide)
        places = number * BLOCK + lax.broadcasted_iota(jnp.int32, (BLOCK, rows_all), 0)
        hot = jnp.where(order[...] == places, 1.0, 0.0).astype(LOW)
        inside = product(hot, member)
        logits = jnp.where(inside > 0.5, logits, NEGATIVE)
        spread[rows, :] = logits
        tops.append(jnp.max(logits, axis=0, keepdims=True))
    top = functools.reduce(jnp.maximum, tops)
    total = 0.0
    for rows in blocks:
        expo = jnp.exp(spread[rows, :] - top)
        spread[rows, :] = expo
        total = total + jnp.sum(expo, axis=0, keepdims=True)
    scale = 1.0 / total
    mixed_sum = 0.0
    pulled_sum = 0.0
    for rows in blocks:
        full = spread[rows, :] * scale
        mix[rows, :] = full
        low = full.astype(LOW)
        mixed_sum = mixed_sum + product_tn(low, second[rows, :])
        pulled_sum = pulled_sum + product_tn(low, cot[rows, :])
    begin(outs[3:])
    mixed[...] = mixed_sum.astype(LOW)
    pulled[...] = pulled_sum.astype(LOW)
    share = EXP_DEV * groups
    for step, send in enumerate((send0, send1, send2, send3)):
        part = pl.ds(pl.multiple_of((place[0] ^ step) * share, share), share)
        send[:share, :] = mixed[part, :]
        send[share:, :] = pulled[part, :]
    finish(outs)
    finish(state_outs)
    for pair in range(PAIRS):
        finish(pair_outs(pair))
    finish([attended_out])


def expert_kernel(in0, in1, in2, in3, up, down, out0, out1, out2, out3):
    groups = in0.shape[0] // (2 * EXP_DEV)
    ff = up.shape[2]
    ins = (in0, in1, in2, in3)
    outs = (out0, out1, out2, out3)
    steps = [(expert, first) for expert in range(EXP_DEV) for first in range(0, ff, FF_BLOCK)]
    result = pull = 0.0
    for expert, first in steps:
        part = pl.ds(first, FF_BLOCK)
        own = slice(expert * groups, (expert + 1) * groups)
        back = slice((EXP_DEV + expert) * groups, (EXP_DEV + expert + 1) * groups)
        taken = jnp.concatenate([ref[own, :] for ref in ins], axis=0)
        given = jnp.concatenate([ref[back, :] for ref in ins], axis=0)
        act, slope = gelu_parts(product(taken, up[expert, :, part]))
        grad = (product_nt(given, down[expert, part, :]) * slope).astype(LOW)
        result = result + product(act.astype(LOW), down[expert, part, :])
        pull = pull + product_nt(grad, up[expert, :, part])
        if first + FF_BLOCK == ff:
            for host, ref in enumerate(outs):
                rows = slice(host * groups, (host + 1) * groups)
                ref[own, :] = result[rows].astype(LOW)
                ref[back, :] = pull[rows].astype(LOW)
            result = pull = 0.0


def middle_kernel(
    place,
    near,
    ret0,
    ret1,
    ret2,
    ret3,
    gain2_far,
    w_control_far,
    hidden_far,
    cot_far,
    mix_far,
    attended_far,
    w_out_far,
    output_far,
    grad_hidden_far,
    pulls_far,
    mine_out,
    other_out,
    gain2,
    w_control,
    hidden,
    cot,
    mix,
    attended,
    w_out,
    output,
    grad_hidden,
    pulls,
    result,
    pull,
    second,
    inner,
    grad_attn,
    grad_out,
    in_sems,
    out_sems,
):
    rows_all = hidden.shape[0]
    groups = rows_all // GROUP
    share = EXP_DEV * groups
    blocks = [pl.ds(start, BLOCK) for start in range(0, rows_all, BLOCK)]
    ins = loads(
        [
            (gain2_far, gain2),
            (w_control_far, w_control),
            (mix_far, mix),
            (hidden_far, hidden),
            (cot_far, cot),
            (w_out_far, w_out),
            (attended_far, attended),
        ],
        in_sems,
    )
    begin(ins)
    outs = loads([(output.at[rows], output_far.at[rows]) for rows in blocks], out_sems)
    state_outs = loads(
        [(grad_hidden.at[rows], grad_hidden_far.at[rows]) for rows in blocks],
        out_sems,
        len(blocks),
    )
    pull_outs = loads(
        [(pulls.at[:, rows], pulls_far.at[:, rows]) for rows in blocks],
        out_sems,
        2 * len(blocks),
    )
    lane = lax.broadcasted_iota(jnp.int32, (BLOCK, PAIR), 1)
    upper = lane >= HEAD_DIM
    slot = lane % HEAD_DIM
    crossed = (lax.broadcasted_iota(jnp.int32, (PAIR, PAIR), 0) >= HEAD_DIM) != (
        lax.broadcasted_iota(jnp.int32, (PAIR, PAIR), 1) >= HEAD_DIM
    )
    crossing = jnp.where(crossed, -1.0, 0.0).astype(LOW)
    for step, ret in enumerate((ret0, ret1, ret2, ret3)):
        part = pl.ds(pl.multiple_of((place[0] ^ step) * share, share), share)
        result[part, :] = ret[:share, :]
        pull[part, :] = ret[share:, :]
    finish(ins[:5])
    total = 0.0
    for number, rows in enumerate(blocks):
        state = hidden[rows, :]
        norm, _ = standard(state)
        low = (norm * gain2[...]).astype(LOW)
        second[rows, :] = low
        full = mix[rows, :]
        output[rows, :] = (state + product(full.astype(LOW), result[...])).astype(LOW)
        begin(outs[number : number + 1])
        grad_mix = product_nt(cot[rows, :], result[...]) + product_nt(low, pull[...])
        weighted = full * grad_mix
        inner[rows, :] = weighted
        total = total + jnp.sum(weighted, axis=0, keepdims=True)
    finish(ins[5:])
    w_wide = widened(w_control, mix.shape[1])
    control = 0.0
    gain = 0.0
    for number, rows in enumerate(blocks):
        full = mix[rows, :]
        grad_logits = (inner[rows, :] - full * total).astype(LOW)
        grad_second = product(full.astype(LOW), pull[...]) + product(grad_logits, w_wide)
        control = control + product_tn(grad_logits, second[rows, :])
        norm, inverse = standard(hidden[rows, :])
        gain = gain + jnp.sum(grad_second * norm, axis=0, keepdims=True)
        grad_state = cot[rows, :].astype(F32) + standard_pull(
            norm, inverse, grad_second * gain2[...]
        )
        grad_hidden[rows, :] = grad_state
        begin(state_outs[number : number + 1])
        low = grad_state.astype(LOW)
        grad_attn[rows, :] = low
        grad_att = product_nt(low, w_out[...]).astype(LOW).astype(F32)
        shared = grad_att * attended[rows, :].astype(F32)
        for pair in range(PAIRS):
            cols = slice(pair * PAIR, (pair + 1) * PAIR)
            top = shared[:, cols].astype(LOW)
            rest = (shared[:, cols] - top.astype(F32)).astype(LOW)
            delta = product(top, crossing) + product(rest, crossing)
            high, middle, last = three_parts(delta)
            marks = jnp.where(
                slot == 4,
                high,
                jnp.where(slot == 5, middle, jnp.where(slot == 6, last, 0.0)),
            )
            for half in range(2):
                mine = upper if half else ~upper
                pulls[2 * pair + half, rows, :] = jnp.where(mine, grad_att[:, cols], marks).astype(
                    LOW
                )
        begin(pull_outs[number : number + 1])
    grad_out[:, :D] = product_tn(attended[...], grad_attn[...]).astype(LOW)
    experts = control.shape[0] // groups
    small = jnp.concatenate(
        (
            jnp.sum(control.reshape(experts, groups, D), axis=1),
            jnp.broadcast_to(gain, (PAIR - experts, D)),
        ),
        axis=0,
    )
    grad_out[:, D:] = small.T.astype(LOW)
    half = D // 2
    mine_out[...] = grad_out[pl.ds(pl.multiple_of(near[0] * half, half), half), :]
    other_out[...] = grad_out[pl.ds(pl.multiple_of((1 - near[0]) * half, half), half), :]
    finish(outs)
    finish(state_outs)
    finish(pull_outs)


def pair_kernel(
    near,
    queries_far,
    keys_far,
    values_far,
    pulls_far,
    normed_far,
    grads_far,
    mine_out,
    other_out,
    queries,
    keys,
    values,
    pulls,
    normed,
    grads,
    grad_query,
    weights,
    in_sems,
    out_sems,
):
    rows_all = normed.shape[0]
    lane = lax.broadcasted_iota(jnp.int32, (BLOCK, PAIR), 1)
    upper = lane >= HEAD_DIM
    triangle = lax.broadcasted_iota(jnp.int32, (BLOCK, BLOCK), 0) <= lax.broadcasted_iota(
        jnp.int32, (BLOCK, BLOCK), 1
    )

    def ins(pair):
        two = pl.ds(2 * pair, 2)
        return loads(
            [
                (keys_far.at[two], keys.at[two]),
                (queries_far.at[two], queries.at[two]),
                (values_far.at[two], values.at[two]),
                (pulls_far.at[two], pulls.at[two]),
            ],
            in_sems,
            4 * pair,
        )

    def outs(pair):
        return loads([(grads.at[pair], grads_far.at[pair])], out_sems, pair)

    begin(ins(0))
    norm_in = loads([(normed_far, normed)], in_sems, 4 * PAIRS)
    begin(ins(1))
    begin(norm_in)
    for pair in range(2, PAIRS):
        begin(ins(pair))

    def one_pair(pair, carry):
        finish(ins(pair))
        work = [(start, half) for start in range(0, rows_all, BLOCK) for half in range(2)]
        seen = set()
        halves = {}

        def score(item):
            start, half = item
            head = 2 * pair + half
            rows = pl.ds(start, BLOCK)
            key, value = keys[head, rows, :], values[head, rows, :]
            parts = [rows]
            if start + BLOCK < rows_all:
                after = min(rows_all, start + BLOCK + LONGEST) - (start + BLOCK)
                parts.append(pl.ds(start + BLOCK, after))
            made = []
            for number, part in enumerate(parts):
                scores = product_nt(key, queries[head, part, :])
                if number == 0:
                    scores = jnp.where(triangle, scores, NEGATIVE)
                made.append((part, scores, product_nt(value, pulls[head, part, :])))
            return key, made

        def weigh(scored):
            key, made = scored
            done = []
            for part, scores, grad_probs in made:
                probs = jnp.exp(scores)
                done.append((part, probs.astype(LOW), (probs * grad_probs).astype(LOW)))
            return key, done

        def gather(item, weighed):
            start, half = item
            head = 2 * pair + half
            key, done = weighed
            key = jnp.where(upper if half else ~upper, key, jnp.zeros_like(key))
            grad_key = 0.0
            grad_value = 0.0
            for part, probs, grad_scores in done:
                grad_value = grad_value + product(probs, pulls[head, part, :])
                grad_key = grad_key + product(grad_scores, queries[head, part, :])
                both = product_tn(grad_scores, key)
                for offset in range(0, part.size, BLOCK):
                    at = part.start + offset
                    piece = both[offset : offset + BLOCK]
                    if at in seen:
                        grad_query[pl.ds(at, BLOCK), :] += piece
                    else:
                        grad_query[pl.ds(at, BLOCK), :] = piece
                        seen.add(at)
            halves[start, half] = grad_key, grad_value
            if half == 1:
                rows = pl.ds(start, BLOCK)
                grads[pair, rows, PAIR : 2 * PAIR] = jnp.where(
                    upper, halves[start, 1][0], halves[start, 0][0]
                ).astype(LOW)
                grads[pair, rows, 2 * PAIR :] = jnp.where(
                    upper, halves[start, 1][1], halves[start, 0][1]
                ).astype(LOW)

        scored, weighed = {}, {}
        for index in range(len(work) + 2):
            if index < len(work):
                scored[index] = score(work[index])
            if 1 <= index <= len(work):
                weighed[index - 1] = weigh(scored[index - 1])
            if index >= 2:
                gather(work[index - 2], weighed[index - 2])
        grads[pair, :, :PAIR] = (grad_query[...] * (HEAD_DIM ** (-0.5))).astype(LOW)
        begin(outs(pair))

        @pl.when(pair == 0)
        def _():
            finish(norm_in)

        cols = pl.ds(pl.multiple_of(pair * 3 * PAIR, PAIR), 3 * PAIR)
        weights[:, cols] = product_tn(normed[...], grads[pair]).astype(LOW)
        return carry

    lax.fori_loop(0, PAIRS, one_pair, 0)
    half = D // 2
    mine_out[...] = weights[pl.ds(pl.multiple_of(near[0] * half, half), half), :]
    other_out[...] = weights[pl.ds(pl.multiple_of((1 - near[0]) * half, half), half), :]
    for pair in range(PAIRS):
        finish(outs(pair))


def last_kernel(grads, tok, grad_hidden, gain1, w_query, w_key, w_value, grad_tokens):
    parts = [grads[pair] for pair in range(PAIRS)]
    grad_normed = 0.0
    for number, weight in enumerate((w_query, w_key, w_value)):
        cols = slice(number * PAIR, (number + 1) * PAIR)
        joined = jnp.concatenate([part[:, cols] for part in parts], axis=1)
        grad_normed = grad_normed + product_nt(joined, weight[...])
    norm, inverse = standard(tok[...].astype(F32))
    grad_tokens[...] = (
        grad_hidden[...] + standard_pull(norm, inverse, grad_normed * gain1[...])
    ).astype(LOW)


def weight_kernel(expert, count, place, *refs):
    pieces = refs[:count]
    up, down = refs[count : count + 2]
    grad_up, grad_down, taken, given, held = refs[-5:]
    step = pl.program_id(0)
    share = PAIR
    groups = share // (2 * EXP_DEV)
    strip_rows, strip_ff = grad_up.shape[1], grad_down.shape[1]
    first = place[0] * strip_rows
    wide = pl.multiple_of(first // PAIR * PAIR, PAIR)
    inside = pl.ds(pl.multiple_of(first % PAIR, strip_rows), strip_rows)

    @pl.when(step == 0)
    def _():
        filled = 0
        for piece in pieces:
            for start in range(0, piece.shape[0], share):
                target = pl.ds(filled, groups)
                taken[target, :] = piece[
                    start + expert * groups : start + (expert + 1) * groups, :
                ]
                back = start + (EXP_DEV + expert) * groups
                given[target, :] = piece[back : back + groups, :]
                filled += groups

    rows_all = taken.shape[0]
    size = min(512, rows_all)
    ff_first = place[0] * strip_ff
    owner = step == ff_first // FF_BLOCK
    total = 0.0
    acts = []
    for start in range(0, rows_all, size):
        rows = pl.ds(start, size)
        act, slope = gelu_parts(product(taken[rows, :], up[0]))
        grad = (product_nt(given[rows, :], down[0]) * slope).astype(LOW)
        total = total + product_tn(taken[rows, pl.ds(wide, PAIR)], grad)
        acts.append(act.astype(LOW))
    held[:PAIR, :] = total
    grad_up[0] = held[inside, :]

    @pl.when(owner)
    def _():
        whole = 0.0
        for number, act in enumerate(acts):
            whole = whole + product_tn(act, given[pl.ds(number * size, size), :])
        held[...] = whole
        grad_down[0] = held[pl.ds(pl.multiple_of(ff_first % FF_BLOCK, strip_ff), strip_ff), :]


def join_kernel(mine_out, swapped_out, mine, swapped, sums):
    first = mine_out.shape[1]
    sums[:, :first] = (mine_out[...].astype(F32) + swapped_out[...].astype(F32)).astype(LOW)
    sums[:, first:] = (mine[...].astype(F32) + swapped[...].astype(F32)).astype(LOW)


def total_kernel(parts, spread):
    total = parts[0].astype(F32)
    for number in range(1, parts.shape[0]):
        total = total + parts[number].astype(F32)
    total = total.astype(LOW)
    for number in range(parts.shape[0]):
        spread[number] = total


def half_kernel(step, near, both, w_query_far, w_key_far, w_value_far, *refs):
    grad_query_far, grad_key_far, grad_value_far, grad_out_far, columns = refs[-9:-4]
    squares, weights, in_sems, out_sems = refs[-4:]
    half = D // 2
    side = near[0] if step == 0 else 1 - near[0]
    rows = pl.ds(pl.multiple_of(side * half, half), half)
    ins = loads(
        [
            (far_weight.at[rows], weights.at[number])
            for number, far_weight in enumerate((w_query_far, w_key_far, w_value_far))
        ],
        in_sems,
    )
    begin(ins)
    targets = (grad_query_far, grad_key_far, grad_value_far, grad_out_far)
    outs = loads(
        [(squares.at[number], target.at[rows]) for number, target in enumerate(targets)], out_sems
    )
    squares[3] = both[:, :D].astype(F32)
    begin(outs[3:])
    finish(ins)
    shared = 0.0
    for number in range(3):
        for pair in range(PAIRS):
            first = D + PAIR + (3 * pair + number) * PAIR
            part = both[:, first : first + PAIR].astype(F32)
            cols = slice(pair * PAIR, (pair + 1) * PAIR)
            squares[number, :, cols] = part
            shared = shared + part * weights[number, :, cols].astype(F32)
        begin(outs[number : number + 1])
    lane = lax.broadcasted_iota(jnp.int32, (half, PAIR), 1)
    columns[...] = jnp.where(
        lane == PAIR - 1,
        jnp.sum(shared, axis=1, keepdims=True),
        both[:, D : D + PAIR].astype(F32),
    )
    finish(outs)


def small_kernel(near, own, other, gain1, grad_control, grad_gain1, grad_gain2, columns):
    half = D // 2
    experts = grad_control.shape[0]
    for side, part in ((near[0], own), (1 - near[0], other)):
        columns[pl.ds(pl.multiple_of(side * half, half), half), :] = part[...]
    turned = columns[...].T
    grad_control[...] = turned[:experts]
    grad_gain2[...] = turned[experts : experts + 1]
    grad_gain1[...] = turned[PAIR - 1 :] / gain1[...]


def vmem():
    return pl.BlockSpec(memory_space=pltpu.VMEM)


def smem():
    return pl.BlockSpec(memory_space=pltpu.SMEM)


def far():
    return pl.BlockSpec(memory_space=pltpu.HBM)


def shape(*sizes, kind=LOW):
    return jax.ShapeDtypeStruct(sizes, kind)


def params(mib):
    return pltpu.CompilerParams(vmem_limit_bytes=mib * MIB)


def cost(flops, moved):
    return pl.CostEstimate(flops=int(flops), bytes_accessed=int(moved), transcendentals=0)


def ring_of(count):
    order = list(range(0, count, 2)) + list(range(count - 1, 0, -2))
    ahead = [(order[i], order[(i + 1) % count]) for i in range(count)]
    return ahead, [(target, source) for source, target in ahead]


def dma(count):
    return pltpu.SemaphoreType.DMA((count,))


def forward_call(lengths, place, order, gain1, gain2, tokens, cot, weights, w_control, experts):
    rows = tokens.shape[0]
    groups = rows // GROUP
    wide = experts * groups
    blocks = rows // BLOCK
    heads = (HEADS, rows, PAIR)
    kept = [
        ((rows, D), F32),
        ((rows, wide), F32),
        ((rows, D), LOW),
        (heads, LOW),
        (heads, LOW),
        (heads, LOW),
        ((rows, D), LOW),
    ]
    results = pl.pallas_call(
        forward_kernel,
        in_specs=[smem()] + [far()] * 11,
        out_specs=[vmem()] * 4 + [far()] * 7,
        out_shape=[shape(2 * EXP_DEV * groups, D)] * 4
        + [shape(*size, kind=kind) for size, kind in kept],
        scratch_shapes=[
            pltpu.SMEM(lengths.shape, jnp.int32),
            pltpu.VMEM(order.shape, jnp.int32),
            pltpu.VMEM((1, D), F32),
            pltpu.VMEM((1, D), F32),
            pltpu.VMEM((experts, D), LOW),
        ]
        + [pltpu.VMEM((rows, D), LOW)] * 2
        + [pltpu.VMEM((D, D), LOW)] * 4
        + [pltpu.VMEM(*one) for one in kept]
        + [
            pltpu.VMEM((rows, D), LOW),
            pltpu.VMEM((rows, wide), F32),
            pltpu.VMEM((wide, D), LOW),
            pltpu.VMEM((wide, D), LOW),
            pltpu.VMEM(heads, LOW),
            dma(11),
            dma(4 + blocks + PAIRS + 1),
        ],
        compiler_params=pltpu.CompilerParams(vmem_limit_bytes=56623104),
        cost_estimate=cost(2e10, 2e7),
    )(place, lengths, order, gain1, gain2, w_control, tokens, cot, *weights)
    return results[:4], results[4:]


def expert_call(arrived, w_up, w_down):
    size, _ = arrived[0].shape
    return pl.pallas_call(
        expert_kernel,
        in_specs=[vmem()] * (len(arrived) + 2),
        out_specs=[vmem()] * len(arrived),
        out_shape=[shape(size, D)] * len(arrived),
        compiler_params=params(16),
        cost_estimate=cost(5e9, 1e7),
    )(*arrived, w_up, w_down)


def middle_call(place, near, returned, gain2, w_control, hidden, cot, mix, attended, w_out):
    rows, wide = mix.shape
    blocks = rows // BLOCK
    taken = [
        ((rows, D), F32),
        ((rows, D), LOW),
        ((rows, wide), F32),
        ((rows, D), LOW),
        ((D, D), LOW),
    ]
    made = [((rows, D), LOW), ((rows, D), F32), ((HEADS, rows, PAIR), LOW)]
    part = shape(D // 2, D + PAIR)
    return pl.pallas_call(
        middle_kernel,
        in_specs=[smem()] * 2 + [vmem()] * 4 + [far()] * 7,
        out_specs=[far()] * 3 + [vmem()] * 2,
        out_shape=[shape(*size, kind=kind) for size, kind in made] + [part, part],
        scratch_shapes=[pltpu.VMEM((1, D), F32), pltpu.VMEM(w_control.shape, LOW)]
        + [pltpu.VMEM(*one) for one in taken + made]
        + [
            pltpu.VMEM((wide, D), LOW),
            pltpu.VMEM((wide, D), LOW),
            pltpu.VMEM((rows, D), LOW),
            pltpu.VMEM((rows, wide), F32),
            pltpu.VMEM((rows, D), LOW),
            pltpu.VMEM((D, D + PAIR), LOW),
            dma(7),
            dma(3 * blocks),
        ],
        compiler_params=params(28),
        cost_estimate=cost(8e9, 1.5e7),
    )(place, near, *returned, gain2, w_control, hidden, cot, mix, attended, w_out)


def pair_call(near, queries, keys, values, pulls, normed):
    rows = normed.shape[0]
    half = shape(D // 2, 3 * PAIRS * PAIR)
    return pl.pallas_call(
        pair_kernel,
        in_specs=[smem()] + [far()] * 5,
        out_specs=[far()] + [vmem()] * 2,
        out_shape=[shape(PAIRS, rows, 3 * PAIR), half, half],
        scratch_shapes=[pltpu.VMEM((HEADS, rows, PAIR), LOW)] * 4
        + [
            pltpu.VMEM((rows, D), LOW),
            pltpu.VMEM((PAIRS, rows, 3 * PAIR), LOW),
            pltpu.VMEM((rows, PAIR), F32),
            pltpu.VMEM((D, 3 * PAIRS * PAIR), LOW),
            dma(4 * PAIRS + 1),
            dma(PAIRS),
        ],
        compiler_params=params(32),
        cost_estimate=cost(2e10, 1.2e7),
    )(near, queries, keys, values, pulls, normed)


def weight_call(expert, copy, pieces, w_up, w_down, copies, earlier):
    ff = w_up.shape[2]
    held = sum(piece.shape[0] for piece in pieces)
    every = held // (2 * EXP_DEV)
    whole = [pl.BlockSpec(one.shape, lambda f: (0, 0)) for one in pieces]
    return pl.pallas_call(
        functools.partial(weight_kernel, expert, len(pieces)),
        grid=(ff // FF_BLOCK,),
        in_specs=[smem()]
        + whole
        + [
            pl.BlockSpec((1, D, FF_BLOCK), lambda f: (expert, 0, f)),
            pl.BlockSpec((1, FF_BLOCK, D), lambda f: (expert, f, 0)),
        ]
        + [far()] * len(earlier),
        out_specs=[
            pl.BlockSpec((1, D // copies, FF_BLOCK), lambda f: (expert, 0, f)),
            pl.BlockSpec((1, ff // copies, D), lambda f: (expert, 0, 0)),
        ],
        out_shape=[
            shape(EXP_DEV, D // copies, ff, kind=F32),
            shape(EXP_DEV, ff // copies, D, kind=F32),
        ],
        scratch_shapes=[
            pltpu.VMEM((every, D), LOW),
            pltpu.VMEM((every, D), LOW),
            pltpu.VMEM((FF_BLOCK, D), F32),
        ],
        input_output_aliases={3 + len(pieces) + i: i for i in range(len(earlier))},
        compiler_params=params(40),
        cost_estimate=cost(1e10, 8e6),
    )(copy, *pieces, w_up, w_down, *earlier)


def last_call(grads, tokens, grad_hidden, gain1, weights):
    rows = tokens.shape[0]
    row_block = lambda i: (i, 0)
    fixed = lambda i: (0, 0)
    return pl.pallas_call(
        last_kernel,
        grid=(rows // BLOCK,),
        in_specs=[pl.BlockSpec((PAIRS, BLOCK, 3 * PAIR), lambda i: (0, i, 0))]
        + [pl.BlockSpec((BLOCK, D), row_block)] * 2
        + [pl.BlockSpec((1, D), fixed)]
        + [pl.BlockSpec((D, D), fixed)] * 3,
        out_specs=pl.BlockSpec((BLOCK, D), row_block),
        out_shape=shape(rows, D),
        compiler_params=params(32),
        cost_estimate=cost(2e9, 8e6),
    )(grads, tokens, grad_hidden, gain1, *weights)


def join_call(*parts):
    rows = parts[0].shape[0]
    return pl.pallas_call(
        join_kernel,
        in_specs=[vmem()] * 4,
        out_specs=vmem(),
        out_shape=shape(rows, parts[0].shape[1] + parts[2].shape[1]),
        compiler_params=params(16),
        cost_estimate=cost(1e6, 3e6),
    )(*parts)


def total_call(parts):
    return pl.pallas_call(
        total_kernel,
        in_specs=[vmem()],
        out_specs=vmem(),
        out_shape=shape(*parts.shape),
        compiler_params=params(16),
        cost_estimate=cost(1e6, 3e6),
    )(parts)


def half_call(step, near, both, weights, earlier):
    square = shape(D, D, kind=F32)
    half = D // 2
    return pl.pallas_call(
        functools.partial(half_kernel, step),
        in_specs=[smem(), vmem()] + [far()] * (3 + len(earlier)),
        out_specs=[far()] * 4 + [vmem()],
        out_shape=[square] * 4 + [shape(half, PAIR, kind=F32)],
        scratch_shapes=[
            pltpu.VMEM((4, half, D), F32),
            pltpu.VMEM((3, half, D), LOW),
            dma(3),
            dma(4),
        ],
        input_output_aliases={5 + i: i for i in range(len(earlier))},
        compiler_params=params(40),
        cost_estimate=cost(1e8, 6e6),
    )(near, both, *weights, *earlier)


def small_call(near, own, other, gain1, experts):
    return pl.pallas_call(
        small_kernel,
        in_specs=[smem()] + [vmem()] * 3,
        out_specs=[vmem()] * 3,
        out_shape=[shape(experts, D, kind=F32)] + [shape(1, D, kind=F32)] * 2,
        scratch_shapes=[pltpu.VMEM((D, PAIR), F32)],
        compiler_params=params(16),
        cost_estimate=cost(1e6, 1e6),
    )(near, own, other, gain1)


def in_order(*values):
    return lax.optimization_barrier(values)


def shards(
    tokens,
    doc_lengths,
    group_order,
    ln1_gain,
    w_query,
    w_key,
    w_value,
    w_out,
    ln2_gain,
    w_control,
    w_up,
    w_down,
    cotangent,
):
    copies, far_hosts, near_hosts = (lax.axis_size(name) for name in ("dp", "far", "near"))
    hosts = far_hosts * near_hosts
    hosts_axes = ("far", "near")
    axes = ("dp", "far")
    count = copies * far_hosts
    experts = hosts * EXP_DEV
    place = lax.axis_index(hosts_axes).astype(jnp.int32).reshape(1)
    near = lax.axis_index("near").astype(jnp.int32).reshape(1)
    copy = lax.axis_index("dp").astype(jnp.int32).reshape(1)
    gain1 = ln1_gain.reshape(1, D)
    gain2 = ln2_gain.reshape(1, D)
    weights = (w_query, w_key, w_value)
    w_control = w_control.T
    ahead, behind = ring_of(copies)
    steps_left = copies // 2 - 1
    pieces = []

    def exchange(parts):
        return [parts[0]] + [
            lax.ppermute(parts[step], hosts_axes, [(i, i ^ step) for i in range(hosts)])
            for step in range(1, hosts)
        ]

    def pass_on(ahead_part, behind_part):
        return lax.ppermute(ahead_part, "dp", ahead), lax.ppermute(behind_part, "dp", behind)

    def next_step(moving):
        nonlocal steps_left
        pieces.extend(moving)
        steps_left -= 1
        if steps_left > 0:
            return pass_on(*moving)
        half = moving[0].shape[0] // 2
        return pass_on(moving[0][:half], moving[1][half:])

    def near_swap(values):
        return lax.ppermute(values, "near", [(i, i ^ 1) for i in range(near_hosts)])

    def scatter(half):
        rows, cols = half.shape
        return lax.all_to_all(half.reshape(count, rows // count, cols), axes, 0, 0, tiled=True)

    def spread(own):
        return lax.all_to_all(own, axes, 0, 0, tiled=True).reshape(-1, own.shape[-1])

    with jax.named_scope("attention_and_mixing"):
        sends, kept = forward_call(
            doc_lengths,
            place,
            group_order,
            gain1,
            gain2,
            tokens,
            cotangent,
            (*weights, w_out),
            w_control,
            experts,
        )
        hidden, mix, normed, queries, keys, values, attended = kept
    with jax.named_scope("to_experts"):
        arrived = exchange(sends)
    with jax.named_scope("gather_for_weights"):
        own = jnp.concatenate(arrived, axis=0)
        pieces.append(own)
        moving = pass_on(own, own)
    with jax.named_scope("experts"):
        results = expert_call(arrived, w_up, w_down)
    with jax.named_scope("from_experts"):
        returned = exchange(results)
    with jax.named_scope("gather_for_weights"):
        moving = next_step(moving)
    with jax.named_scope("mixing_backward"):
        output, grad_hidden, pulls, mine_out, other_out = middle_call(
            place, near, returned, gain2, w_control, hidden, cotangent, mix, attended, w_out
        )
    with jax.named_scope("gather_for_weights"):
        pulls, other_out, moving = in_order(pulls, other_out, moving)
        moving = next_step(moving)
    with jax.named_scope("reduce"):
        swapped_out = near_swap(other_out)
    with jax.named_scope("attention_backward"):
        grads, mine, other = pair_call(near, queries, keys, values, pulls, normed)
        mine, other, moving, swapped_out = in_order(mine, other, moving, swapped_out)
    with jax.named_scope("gather_for_weights"):
        while steps_left > 0:
            moving = next_step(moving)
    with jax.named_scope("reduce"):
        sums = join_call(mine_out, swapped_out, mine, near_swap(other))
        sums, grads, moving = in_order(sums, grads, moving)
        pieces.extend(moving)
        sums = scatter(sums)
    with jax.named_scope("norm_backward"):
        grad_tokens = last_call(grads, tokens, grad_hidden, gain1, weights)
    with jax.named_scope("expert_weights"):
        grads_expert = weight_call(0, copy, pieces, w_up, w_down, copies, ())
        sums, grads_expert, grad_tokens = in_order(sums, grads_expert, grad_tokens)
    with jax.named_scope("reduce"):
        sums = total_call(sums)
        sums, grads_expert = in_order(sums, grads_expert)
        sums = spread(sums)
    with jax.named_scope("expert_weights"):
        grad_up, grad_down = weight_call(1, copy, pieces, w_up, w_down, copies, grads_expert)
        sums, grad_up, grad_down = in_order(sums, grad_up, grad_down)
    with jax.named_scope("reduce"):
        sums_other = near_swap(sums)
    with jax.named_scope("assemble"):
        *squares, own_columns = half_call(0, near, sums, weights, ())
        *squares, other_columns = half_call(1, near, sums_other, weights, squares)
        grad_query, grad_key, grad_value, grad_out = squares
        grad_control, grad_gain1, grad_gain2 = small_call(
            near, own_columns, other_columns, gain1, experts
        )
    return (
        output,
        grad_tokens,
        grad_gain1.reshape(D),
        grad_query,
        grad_key,
        grad_value,
        grad_out,
        grad_gain2.reshape(D),
        grad_control.T,
        grad_up,
        grad_down,
    )


def solution(mesh):
    copies, hosts = mesh.shape["dp"], mesh.shape["expert"]
    finer = jax.sharding.Mesh(mesh.devices.reshape(copies, hosts // 2, 2), ("dp", "far", "near"))
    every = P(("dp", "far", "near"), None)
    expert = P(("far", "near"), None, None)
    sliced = P(("far", "near"), "dp", None)
    return jax.shard_map(
        shards,
        mesh=finer,
        in_specs=(every,) * 3 + (P(),) * 7 + (expert,) * 2 + (every,),
        out_specs=(every,) * 2 + (P(),) * 7 + (sliced,) * 2,
        check_vma=False,
    )
```

```python
import functools

import jax
import jax.numpy as jnp
from jax import lax
from jax.experimental import pallas as pl
from jax.experimental.pallas import tpu as pltpu
from jax.sharding import PartitionSpec as P

D = 512
HEADS = 8
HEAD_DIM = 64
PAIRS = 4
PAIR = 2 * HEAD_DIM
GROUP = 32
EXP_DEV = 2
LONGEST = 512
BLOCK = 256
FF_BLOCK = 512
EPSILON = 1e-05
NEGATIVE = -1e30
MIB = 1 << 20

F32 = jnp.float32
LOW = jnp.bfloat16


def product(left, right):
    return jnp.dot(left, right, preferred_element_type=F32)


def product_nt(left, right):
    return lax.dot_general(left, right, (((1,), (1,)), ((), ())), preferred_element_type=F32)


def product_tn(left, right):
    return lax.dot_general(left, right, (((0,), (0,)), ((), ())), preferred_element_type=F32)


def standard(values):
    center = values - jnp.mean(values, axis=-1, keepdims=True)
    inverse = lax.rsqrt(jnp.mean(center * center, axis=-1, keepdims=True) + EPSILON)
    return center * inverse, inverse


def standard_pull(norm, inverse, grad):
    return (
        grad
        - jnp.mean(grad, axis=-1, keepdims=True)
        - norm * jnp.mean(grad * norm, axis=-1, keepdims=True)
    ) * inverse


def gelu_parts(values):
    square = values * values
    tanh = jnp.tanh(0.7978845608028654 * values * (1.0 + 0.044715 * square))
    half = 0.5 + 0.5 * tanh
    slope = half + values * (0.5 - 0.5 * tanh * tanh) * (
        0.7978845608028654 + 0.10703222440890037 * square
    )
    return values * half, slope


def three_parts(values):
    high = values.astype(LOW).astype(F32)
    rest = values - high
    middle = rest.astype(LOW).astype(F32)
    return high, middle, rest - middle


def begin(copies):
    for copy in copies:
        copy.start()


def finish(copies):
    for copy in copies:
        copy.wait()


def loads(pairs, sems, first=0):
    return [
        pltpu.make_async_copy(source, target, sems.at[first + number])
        for number, (source, target) in enumerate(pairs)
    ]


def widened(w_control, width):
    experts = w_control.shape[0]
    lane = lax.broadcasted_iota(jnp.int32, (experts, width), 1) // (width // experts)
    row = lax.broadcasted_iota(jnp.int32, (experts, width), 0)
    return product_tn(jnp.where(lane == row, 1.0, 0.0).astype(LOW), w_control[...]).astype(LOW)


def forward_kernel(
    place,
    lengths_far,
    order_far,
    gain1_far,
    gain2_far,
    w_control_far,
    tok_far,
    cot_far,
    w_query_far,
    w_key_far,
    w_value_far,
    w_out_far,
    send0,
    send1,
    send2,
    send3,
    hidden_far,
    mix_far,
    normed_far,
    queries_far,
    keys_far,
    values_far,
    attended_far,
    lengths,
    order,
    gain1,
    gain2,
    w_control,
    tok,
    cot,
    w_query,
    w_key,
    w_value,
    w_out,
    hidden,
    mix,
    normed,
    queries,
    keys,
    values,
    attended,
    second,
    spread,
    mixed,
    pulled,
    marked,
    in_sems,
    out_sems,
):
    rows_all = tok.shape[0]
    groups = rows_all // GROUP
    width = mix.shape[1]
    ins = loads(
        [
            (tok_far, tok),
            (gain1_far, gain1),
            (lengths_far, lengths),
            (w_query_far, w_query),
            (w_key_far, w_key),
            (w_value_far, w_value),
            (w_out_far, w_out),
            (gain2_far, gain2),
            (w_control_far, w_control),
            (order_far, order),
            (cot_far, cot),
        ],
        in_sems,
    )
    begin(ins)
    blocks = [pl.ds(start, BLOCK) for start in range(0, rows_all, BLOCK)]
    outs = loads(
        [(normed, normed_far), (keys, keys_far), (values, values_far), (mix, mix_far)], out_sems
    )
    state_outs = loads([(hidden.at[rows], hidden_far.at[rows]) for rows in blocks], out_sems, 4)

    def pair_outs(pair):
        first = 4 + len(blocks)
        two = pl.ds(2 * pair, 2)
        return [
            pltpu.make_async_copy(marked.at[two], queries_far.at[two], out_sems.at[first + pair])
        ]

    attended_out = pltpu.make_async_copy(
        attended, attended_far, out_sems.at[4 + len(blocks) + PAIRS]
    )
    lane = lax.broadcasted_iota(jnp.int32, (BLOCK, PAIR), 1)
    upper = lane >= HEAD_DIM
    slot = lane % HEAD_DIM
    finish(ins[:3])
    end0 = lengths[0, 0]
    end1 = end0 + lengths[0, 1]
    end2 = end1 + lengths[0, 2]
    ones = (slot >= 4) & (slot < 7)
    for number, rows in enumerate(blocks):
        norm, _ = standard(tok[rows, :].astype(F32))
        low = (norm * gain1[...]).astype(LOW)
        normed[rows, :] = low
        places = number * BLOCK + lax.broadcasted_iota(jnp.int32, (BLOCK, PAIR), 0)
        document = (
            (places >= end0).astype(jnp.int32)
            + (places >= end1).astype(jnp.int32)
            + (places >= end2).astype(jnp.int32)
        )
        same = slot == document
        key_marks = jnp.where(same | ones, 1.0, 0.0)
        value_marks = jnp.where(ones, 1.0, 0.0)
        query_marks = jnp.where((slot < 4) & ~same, NEGATIVE, 0.0)
        if number == 0:
            finish(ins[3:6])
        query = product(low, w_query[...]) * (HEAD_DIM ** (-0.5))
        key = product(low, w_key[...])
        value = product(low, w_value[...])
        for pair in range(PAIRS):
            cols = slice(pair * PAIR, (pair + 1) * PAIR)
            for half in range(2):
                mine = upper if half else ~upper
                head = 2 * pair + half
                queries[head, rows, :] = jnp.where(mine, query[:, cols], query_marks).astype(LOW)
                keys[head, rows, :] = jnp.where(mine, key[:, cols], key_marks).astype(LOW)
                values[head, rows, :] = jnp.where(mine, value[:, cols], value_marks).astype(LOW)
    begin(outs[:3])

    triangle = lax.broadcasted_iota(jnp.int32, (BLOCK, BLOCK), 1) <= lax.broadcasted_iota(
        jnp.int32, (BLOCK, BLOCK), 0
    )

    def attend(pair, carry):
        work = [(number, half) for number in range(len(blocks)) for half in range(2)]
        results = {}

        def score(item):
            number, half = item
            start = number * BLOCK
            first = max(0, start - LONGEST)
            head = 2 * pair + half
            query = queries[head, blocks[number], :]
            near = jnp.where(triangle, product_nt(query, keys[head, blocks[number], :]), NEGATIVE)
            far = None
            if start > first:
                far = product_nt(query, keys[head, pl.ds(first, start - first), :])
            return query, near, far

        def weigh(item, scored):
            query, near, far = scored
            top = jnp.max(near, axis=1, keepdims=True)
            if far is not None:
                top = jnp.maximum(top, jnp.max(far, axis=1, keepdims=True))
                far = jnp.exp(far - top).astype(LOW)
            return query, jnp.exp(near - top).astype(LOW), far, top

        def gather(item, weighed):
            number, half = item
            query, near, far, top = weighed
            start = number * BLOCK
            first = max(0, start - LONGEST)
            head = 2 * pair + half
            rows = blocks[number]
            out = product(near, values[head, rows, :])
            if far is not None:
                out = out + product(far, values[head, pl.ds(first, start - first), :])
            mark = 4 + HEAD_DIM * (1 - half)
            total = out[:, mark : mark + 1]
            results[item] = out * (1.0 / total)
            high, middle, rest = three_parts(-(top + jnp.log(total)))
            marks = jnp.where(
                lane == mark, high, jnp.where(lane == mark + 1, middle, rest)
            ).astype(LOW)
            marked[head, rows, :] = jnp.where((lane >= mark) & (lane < mark + 3), marks, query)

        scored, weighed = {}, {}
        for index in range(len(work) + 2):
            if index < len(work):
                scored[index] = score(work[index])
            if 1 <= index <= len(work):
                weighed[index - 1] = weigh(work[index - 1], scored[index - 1])
            if index >= 2:
                gather(work[index - 2], weighed[index - 2])
        cols = pl.ds(pl.multiple_of(pair * PAIR, PAIR), PAIR)
        for number, rows in enumerate(blocks):
            attended[rows, cols] = jnp.where(upper, results[number, 1], results[number, 0]).astype(
                LOW
            )
        begin(pair_outs(pair))
        return carry

    lax.fori_loop(0, PAIRS, attend, 0)
    begin([attended_out])
    finish(ins[6:])

    place_group = lax.broadcasted_iota(jnp.int32, (rows_all, width), 0) // GROUP
    lane_group = lax.broadcasted_iota(jnp.int32, (rows_all, width), 1) % groups
    member = jnp.where(place_group == lane_group, 1.0, 0.0).astype(LOW)
    w_wide = widened(w_control, width)
    tops = []
    for number, rows in enumerate(blocks):
        state = tok[rows, :].astype(F32) + product(attended[rows, :], w_out[...])
        hidden[rows, :] = state
        begin(state_outs[number : number + 1])
        norm, _ = standard(state)
        low = (norm * gain2[...]).astype(LOW)
        second[rows, :] = low
        logits = product_nt(low, w_wide)
        places = number * BLOCK + lax.broadcasted_iota(jnp.int32, (BLOCK, rows_all), 0)
        hot = jnp.where(order[...] == places, 1.0, 0.0).astype(LOW)
        inside = product(hot, member)
        logits = jnp.where(inside > 0.5, logits, NEGATIVE)
        spread[rows, :] = logits
        tops.append(jnp.max(logits, axis=0, keepdims=True))
    top = functools.reduce(jnp.maximum, tops)
    total = 0.0
    for rows in blocks:
        expo = jnp.exp(spread[rows, :] - top)
        spread[rows, :] = expo
        total = total + jnp.sum(expo, axis=0, keepdims=True)
    scale = 1.0 / total
    mixed_sum = 0.0
    pulled_sum = 0.0
    for rows in blocks:
        mix[rows, :] = spread[rows, :] * scale
    begin(outs[3:])
    for rows in blocks:
        low = mix[rows, :].astype(LOW)
        mixed_sum = mixed_sum + product_tn(low, second[rows, :])
        pulled_sum = pulled_sum + product_tn(low, cot[rows, :])
    mixed[...] = mixed_sum.astype(LOW)
    pulled[...] = pulled_sum.astype(LOW)
    share = EXP_DEV * groups
    for step, send in enumerate((send0, send1, send2, send3)):
        part = pl.ds(pl.multiple_of((place[0] ^ step) * share, share), share)
        send[:share, :] = mixed[part, :]
        send[share:, :] = pulled[part, :]
    finish(outs)
    finish(state_outs)
    for pair in range(PAIRS):
        finish(pair_outs(pair))
    finish([attended_out])


def expert_kernel(in0, in1, in2, in3, up, down, out0, out1, out2, out3):
    groups = in0.shape[0] // (2 * EXP_DEV)
    ff = up.shape[2]
    ins = (in0, in1, in2, in3)
    outs = (out0, out1, out2, out3)
    steps = [(expert, first) for expert in range(EXP_DEV) for first in range(0, ff, FF_BLOCK)]
    result = pull = 0.0
    for expert, first in steps:
        part = pl.ds(first, FF_BLOCK)
        own = slice(expert * groups, (expert + 1) * groups)
        back = slice((EXP_DEV + expert) * groups, (EXP_DEV + expert + 1) * groups)
        taken = jnp.concatenate([ref[own, :] for ref in ins], axis=0)
        given = jnp.concatenate([ref[back, :] for ref in ins], axis=0)
        act, slope = gelu_parts(product(taken, up[expert, :, part]))
        grad = (product_nt(given, down[expert, part, :]) * slope).astype(LOW)
        result = result + product(act.astype(LOW), down[expert, part, :])
        pull = pull + product_nt(grad, up[expert, :, part])
        if first + FF_BLOCK == ff:
            for host, ref in enumerate(outs):
                rows = slice(host * groups, (host + 1) * groups)
                ref[own, :] = result[rows].astype(LOW)
                ref[back, :] = pull[rows].astype(LOW)
            result = pull = 0.0


def middle_kernel(
    place,
    near,
    ret0,
    ret1,
    ret2,
    ret3,
    gain2_far,
    w_control_far,
    hidden_far,
    cot_far,
    mix_far,
    attended_far,
    w_out_far,
    output_far,
    grad_hidden_far,
    pulls_far,
    mine_out,
    other_out,
    gain2,
    w_control,
    hidden,
    cot,
    mix,
    attended,
    w_out,
    output,
    grad_hidden,
    pulls,
    result,
    pull,
    second,
    inner,
    grad_attn,
    grad_out,
    in_sems,
    out_sems,
):
    rows_all = hidden.shape[0]
    groups = rows_all // GROUP
    share = EXP_DEV * groups
    blocks = [pl.ds(start, BLOCK) for start in range(0, rows_all, BLOCK)]
    ins = loads(
        [
            (gain2_far, gain2),
            (w_control_far, w_control),
            (mix_far, mix),
            (hidden_far, hidden),
            (cot_far, cot),
            (w_out_far, w_out),
            (attended_far, attended),
        ],
        in_sems,
    )
    begin(ins)
    outs = loads([(output.at[rows], output_far.at[rows]) for rows in blocks], out_sems)
    state_outs = loads(
        [(grad_hidden.at[rows], grad_hidden_far.at[rows]) for rows in blocks],
        out_sems,
        len(blocks),
    )
    pull_outs = loads(
        [(pulls.at[:, rows], pulls_far.at[:, rows]) for rows in blocks],
        out_sems,
        2 * len(blocks),
    )
    lane = lax.broadcasted_iota(jnp.int32, (BLOCK, PAIR), 1)
    upper = lane >= HEAD_DIM
    slot = lane % HEAD_DIM
    crossed = (lax.broadcasted_iota(jnp.int32, (PAIR, PAIR), 0) >= HEAD_DIM) != (
        lax.broadcasted_iota(jnp.int32, (PAIR, PAIR), 1) >= HEAD_DIM
    )
    crossing = jnp.where(crossed, -1.0, 0.0).astype(LOW)
    for step, ret in enumerate((ret0, ret1, ret2, ret3)):
        part = pl.ds(pl.multiple_of((place[0] ^ step) * share, share), share)
        result[part, :] = ret[:share, :]
        pull[part, :] = ret[share:, :]
    finish(ins[:5])
    total = 0.0
    for number, rows in enumerate(blocks):
        state = hidden[rows, :]
        norm, _ = standard(state)
        low = (norm * gain2[...]).astype(LOW)
        second[rows, :] = low
        full = mix[rows, :]
        output[rows, :] = (state + product(full.astype(LOW), result[...])).astype(LOW)
        begin(outs[number : number + 1])
        grad_mix = product_nt(cot[rows, :], result[...]) + product_nt(low, pull[...])
        weighted = full * grad_mix
        inner[rows, :] = weighted
        total = total + jnp.sum(weighted, axis=0, keepdims=True)
    finish(ins[5:])
    w_wide = widened(w_control, mix.shape[1])
    control = 0.0
    gain = 0.0
    for number, rows in enumerate(blocks):
        full = mix[rows, :]
        grad_logits = (inner[rows, :] - full * total).astype(LOW)
        grad_second = product(full.astype(LOW), pull[...]) + product(grad_logits, w_wide)
        control = control + product_tn(grad_logits, second[rows, :])
        norm, inverse = standard(hidden[rows, :])
        gain = gain + jnp.sum(grad_second * norm, axis=0, keepdims=True)
        grad_state = cot[rows, :].astype(F32) + standard_pull(
            norm, inverse, grad_second * gain2[...]
        )
        grad_hidden[rows, :] = grad_state
        begin(state_outs[number : number + 1])
        low = grad_state.astype(LOW)
        grad_attn[rows, :] = low
        grad_att = product_nt(low, w_out[...]).astype(LOW).astype(F32)
        shared = grad_att * attended[rows, :].astype(F32)
        for pair in range(PAIRS):
            cols = slice(pair * PAIR, (pair + 1) * PAIR)
            top = shared[:, cols].astype(LOW)
            rest = (shared[:, cols] - top.astype(F32)).astype(LOW)
            delta = product(top, crossing) + product(rest, crossing)
            high, middle, last = three_parts(delta)
            marks = jnp.where(
                slot == 4,
                high,
                jnp.where(slot == 5, middle, jnp.where(slot == 6, last, 0.0)),
            )
            for half in range(2):
                mine = upper if half else ~upper
                pulls[2 * pair + half, rows, :] = jnp.where(mine, grad_att[:, cols], marks).astype(
                    LOW
                )
        begin(pull_outs[number : number + 1])
    grad_out[:, :D] = product_tn(attended[...], grad_attn[...]).astype(LOW)
    experts = control.shape[0] // groups
    small = jnp.concatenate(
        (
            jnp.sum(control.reshape(experts, groups, D), axis=1),
            jnp.broadcast_to(gain, (PAIR - experts, D)),
        ),
        axis=0,
    )
    grad_out[:, D:] = small.T.astype(LOW)
    half = D // 2
    mine_out[...] = grad_out[pl.ds(pl.multiple_of(near[0] * half, half), half), :]
    other_out[...] = grad_out[pl.ds(pl.multiple_of((1 - near[0]) * half, half), half), :]
    finish(outs)
    finish(state_outs)
    finish(pull_outs)


def pair_kernel(
    near,
    queries_far,
    keys_far,
    values_far,
    pulls_far,
    normed_far,
    grads_far,
    mine_out,
    other_out,
    queries,
    keys,
    values,
    pulls,
    normed,
    grads,
    grad_query,
    weights,
    in_sems,
    out_sems,
):
    rows_all = normed.shape[0]
    lane = lax.broadcasted_iota(jnp.int32, (BLOCK, PAIR), 1)
    upper = lane >= HEAD_DIM
    triangle = lax.broadcasted_iota(jnp.int32, (BLOCK, BLOCK), 0) <= lax.broadcasted_iota(
        jnp.int32, (BLOCK, BLOCK), 1
    )

    def ins(pair):
        two = pl.ds(2 * pair, 2)
        return loads(
            [
                (keys_far.at[two], keys.at[two]),
                (queries_far.at[two], queries.at[two]),
                (values_far.at[two], values.at[two]),
                (pulls_far.at[two], pulls.at[two]),
            ],
            in_sems,
            4 * pair,
        )

    def outs(pair):
        return loads([(grads.at[pair], grads_far.at[pair])], out_sems, pair)

    begin(ins(0))
    norm_in = loads([(normed_far, normed)], in_sems, 4 * PAIRS)
    begin(ins(1))
    begin(norm_in)
    for pair in range(2, PAIRS):
        begin(ins(pair))

    def one_pair(pair, carry):
        finish(ins(pair))
        work = [(start, half) for start in range(0, rows_all, BLOCK) for half in range(2)]
        seen = set()
        halves = {}

        def score(item):
            start, half = item
            head = 2 * pair + half
            rows = pl.ds(start, BLOCK)
            key, value = keys[head, rows, :], values[head, rows, :]
            parts = [rows]
            if start + BLOCK < rows_all:
                after = min(rows_all, start + BLOCK + LONGEST) - (start + BLOCK)
                parts.append(pl.ds(start + BLOCK, after))
            made = []
            for number, part in enumerate(parts):
                scores = product_nt(key, queries[head, part, :])
                if number == 0:
                    scores = jnp.where(triangle, scores, NEGATIVE)
                made.append((part, scores, product_nt(value, pulls[head, part, :])))
            return key, made

        def weigh(scored):
            key, made = scored
            done = []
            for part, scores, grad_probs in made:
                probs = jnp.exp(scores)
                done.append((part, probs.astype(LOW), (probs * grad_probs).astype(LOW)))
            return key, done

        def gather(item, weighed):
            start, half = item
            head = 2 * pair + half
            key, done = weighed
            key = jnp.where(upper if half else ~upper, key, jnp.zeros_like(key))
            grad_key = 0.0
            grad_value = 0.0
            for part, probs, grad_scores in done:
                grad_value = grad_value + product(probs, pulls[head, part, :])
                grad_key = grad_key + product(grad_scores, queries[head, part, :])
                both = product_tn(grad_scores, key)
                for offset in range(0, part.size, BLOCK):
                    at = part.start + offset
                    piece = both[offset : offset + BLOCK]
                    if at in seen:
                        grad_query[pl.ds(at, BLOCK), :] += piece
                    else:
                        grad_query[pl.ds(at, BLOCK), :] = piece
                        seen.add(at)
            halves[start, half] = grad_key, grad_value
            if half == 1:
                rows = pl.ds(start, BLOCK)
                grads[pair, rows, PAIR : 2 * PAIR] = jnp.where(
                    upper, halves[start, 1][0], halves[start, 0][0]
                ).astype(LOW)
                grads[pair, rows, 2 * PAIR :] = jnp.where(
                    upper, halves[start, 1][1], halves[start, 0][1]
                ).astype(LOW)

        scored, weighed = {}, {}
        for index in range(len(work) + 2):
            if index < len(work):
                scored[index] = score(work[index])
            if 1 <= index <= len(work):
                weighed[index - 1] = weigh(scored[index - 1])
            if index >= 2:
                gather(work[index - 2], weighed[index - 2])
        grads[pair, :, :PAIR] = (grad_query[...] * (HEAD_DIM ** (-0.5))).astype(LOW)
        begin(outs(pair))

        @pl.when(pair == 0)
        def _():
            finish(norm_in)

        cols = pl.ds(pl.multiple_of(pair * 3 * PAIR, PAIR), 3 * PAIR)
        weights[:, cols] = product_tn(normed[...], grads[pair]).astype(LOW)
        return carry

    lax.fori_loop(0, PAIRS, one_pair, 0)
    half = D // 2
    mine_out[...] = weights[pl.ds(pl.multiple_of(near[0] * half, half), half), :]
    other_out[...] = weights[pl.ds(pl.multiple_of((1 - near[0]) * half, half), half), :]
    for pair in range(PAIRS):
        finish(outs(pair))


def last_kernel(grads, tok, grad_hidden, gain1, w_query, w_key, w_value, grad_tokens):
    parts = [grads[pair] for pair in range(PAIRS)]
    grad_normed = 0.0
    for number, weight in enumerate((w_query, w_key, w_value)):
        cols = slice(number * PAIR, (number + 1) * PAIR)
        joined = jnp.concatenate([part[:, cols] for part in parts], axis=1)
        grad_normed = grad_normed + product_nt(joined, weight[...])
    norm, inverse = standard(tok[...].astype(F32))
    grad_tokens[...] = (
        grad_hidden[...] + standard_pull(norm, inverse, grad_normed * gain1[...])
    ).astype(LOW)


def weight_kernel(expert, count, place, *refs):
    pieces = refs[:count]
    up, down = refs[count : count + 2]
    grad_up, grad_down, taken, given, held = refs[-5:]
    step = pl.program_id(0)
    share = PAIR
    groups = share // (2 * EXP_DEV)
    strip_rows, strip_ff = grad_up.shape[1], grad_down.shape[1]
    first = place[0] * strip_rows
    wide = pl.multiple_of(first // PAIR * PAIR, PAIR)
    inside = pl.ds(pl.multiple_of(first % PAIR, strip_rows), strip_rows)

    @pl.when(step == 0)
    def _():
        filled = 0
        for piece in pieces:
            for start in range(0, piece.shape[0], share):
                target = pl.ds(filled, groups)
                taken[target, :] = piece[
                    start + expert * groups : start + (expert + 1) * groups, :
                ]
                back = start + (EXP_DEV + expert) * groups
                given[target, :] = piece[back : back + groups, :]
                filled += groups

    rows_all = taken.shape[0]
    size = min(512, rows_all)
    ff_first = place[0] * strip_ff
    owner = step == ff_first // FF_BLOCK
    total = 0.0
    acts = []
    for start in range(0, rows_all, size):
        rows = pl.ds(start, size)
        act, slope = gelu_parts(product(taken[rows, :], up[0]))
        grad = (product_nt(given[rows, :], down[0]) * slope).astype(LOW)
        total = total + product_tn(taken[rows, pl.ds(wide, PAIR)], grad)
        acts.append(act.astype(LOW))
    held[:PAIR, :] = total
    grad_up[0] = held[inside, :]

    @pl.when(owner)
    def _():
        whole = 0.0
        for number, act in enumerate(acts):
            whole = whole + product_tn(act, given[pl.ds(number * size, size), :])
        held[...] = whole
        grad_down[0] = held[pl.ds(pl.multiple_of(ff_first % FF_BLOCK, strip_ff), strip_ff), :]


def join_kernel(mine_out, swapped_out, mine, swapped, sums):
    first = mine_out.shape[1]
    sums[:, :first] = (mine_out[...].astype(F32) + swapped_out[...].astype(F32)).astype(LOW)
    sums[:, first:] = (mine[...].astype(F32) + swapped[...].astype(F32)).astype(LOW)


def total_kernel(parts, spread):
    total = parts[0].astype(F32)
    for number in range(1, parts.shape[0]):
        total = total + parts[number].astype(F32)
    total = total.astype(LOW)
    for number in range(parts.shape[0]):
        spread[number] = total


def half_kernel(step, near, both, w_query_far, w_key_far, w_value_far, *refs):
    grad_query_far, grad_key_far, grad_value_far, grad_out_far, columns = refs[-9:-4]
    squares, weights, in_sems, out_sems = refs[-4:]
    half = D // 2
    side = near[0] if step == 0 else 1 - near[0]
    rows = pl.ds(pl.multiple_of(side * half, half), half)
    ins = loads(
        [
            (far_weight.at[rows], weights.at[number])
            for number, far_weight in enumerate((w_query_far, w_key_far, w_value_far))
        ],
        in_sems,
    )
    begin(ins)
    targets = (grad_query_far, grad_key_far, grad_value_far, grad_out_far)
    outs = loads(
        [(squares.at[number], target.at[rows]) for number, target in enumerate(targets)], out_sems
    )
    squares[3] = both[:, :D].astype(F32)
    begin(outs[3:])
    finish(ins)
    shared = 0.0
    for number in range(3):
        for pair in range(PAIRS):
            first = D + PAIR + (3 * pair + number) * PAIR
            part = both[:, first : first + PAIR].astype(F32)
            cols = slice(pair * PAIR, (pair + 1) * PAIR)
            squares[number, :, cols] = part
            shared = shared + part * weights[number, :, cols].astype(F32)
        begin(outs[number : number + 1])
    lane = lax.broadcasted_iota(jnp.int32, (half, PAIR), 1)
    columns[...] = jnp.where(
        lane == PAIR - 1,
        jnp.sum(shared, axis=1, keepdims=True),
        both[:, D : D + PAIR].astype(F32),
    )
    finish(outs)


def small_kernel(near, own, other, gain1, grad_control, grad_gain1, grad_gain2, columns):
    half = D // 2
    experts = grad_control.shape[0]
    for side, part in ((near[0], own), (1 - near[0], other)):
        columns[pl.ds(pl.multiple_of(side * half, half), half), :] = part[...]
    turned = columns[...].T
    grad_control[...] = turned[:experts]
    grad_gain2[...] = turned[experts : experts + 1]
    grad_gain1[...] = turned[PAIR - 1 :] / gain1[...]


def vmem():
    return pl.BlockSpec(memory_space=pltpu.VMEM)


def smem():
    return pl.BlockSpec(memory_space=pltpu.SMEM)


def far():
    return pl.BlockSpec(memory_space=pltpu.HBM)


def shape(*sizes, kind=LOW):
    return jax.ShapeDtypeStruct(sizes, kind)


def params(mib):
    return pltpu.CompilerParams(vmem_limit_bytes=mib * MIB)


def cost(flops, moved):
    return pl.CostEstimate(flops=int(flops), bytes_accessed=int(moved), transcendentals=0)


def ring_of(count):
    order = list(range(0, count, 2)) + list(range(count - 1, 0, -2))
    ahead = [(order[i], order[(i + 1) % count]) for i in range(count)]
    return ahead, [(target, source) for source, target in ahead]


def dma(count):
    return pltpu.SemaphoreType.DMA((count,))


def forward_call(lengths, place, order, gain1, gain2, tokens, cot, weights, w_control, experts):
    rows = tokens.shape[0]
    groups = rows // GROUP
    wide = experts * groups
    blocks = rows // BLOCK
    heads = (HEADS, rows, PAIR)
    kept = [
        ((rows, D), F32),
        ((rows, wide), F32),
        ((rows, D), LOW),
        (heads, LOW),
        (heads, LOW),
        (heads, LOW),
        ((rows, D), LOW),
    ]
    results = pl.pallas_call(
        forward_kernel,
        in_specs=[smem()] + [far()] * 11,
        out_specs=[vmem()] * 4 + [far()] * 7,
        out_shape=[shape(2 * EXP_DEV * groups, D)] * 4
        + [shape(*size, kind=kind) for size, kind in kept],
        scratch_shapes=[
            pltpu.SMEM(lengths.shape, jnp.int32),
            pltpu.VMEM(order.shape, jnp.int32),
            pltpu.VMEM((1, D), F32),
            pltpu.VMEM((1, D), F32),
            pltpu.VMEM((experts, D), LOW),
        ]
        + [pltpu.VMEM((rows, D), LOW)] * 2
        + [pltpu.VMEM((D, D), LOW)] * 4
        + [pltpu.VMEM(*one) for one in kept]
        + [
            pltpu.VMEM((rows, D), LOW),
            pltpu.VMEM((rows, wide), F32),
            pltpu.VMEM((wide, D), LOW),
            pltpu.VMEM((wide, D), LOW),
            pltpu.VMEM(heads, LOW),
            dma(11),
            dma(4 + blocks + PAIRS + 1),
        ],
        compiler_params=pltpu.CompilerParams(vmem_limit_bytes=56623104),
        cost_estimate=cost(2e10, 2e7),
    )(place, lengths, order, gain1, gain2, w_control, tokens, cot, *weights)
    return results[:4], results[4:]


def expert_call(arrived, w_up, w_down):
    size, _ = arrived[0].shape
    return pl.pallas_call(
        expert_kernel,
        in_specs=[vmem()] * (len(arrived) + 2),
        out_specs=[vmem()] * len(arrived),
        out_shape=[shape(size, D)] * len(arrived),
        compiler_params=params(16),
        cost_estimate=cost(5e9, 1e7),
    )(*arrived, w_up, w_down)


def middle_call(place, near, returned, gain2, w_control, hidden, cot, mix, attended, w_out):
    rows, wide = mix.shape
    blocks = rows // BLOCK
    taken = [
        ((rows, D), F32),
        ((rows, D), LOW),
        ((rows, wide), F32),
        ((rows, D), LOW),
        ((D, D), LOW),
    ]
    made = [((rows, D), LOW), ((rows, D), F32), ((HEADS, rows, PAIR), LOW)]
    part = shape(D // 2, D + PAIR)
    return pl.pallas_call(
        middle_kernel,
        in_specs=[smem()] * 2 + [vmem()] * 4 + [far()] * 7,
        out_specs=[far()] * 3 + [vmem()] * 2,
        out_shape=[shape(*size, kind=kind) for size, kind in made] + [part, part],
        scratch_shapes=[pltpu.VMEM((1, D), F32), pltpu.VMEM(w_control.shape, LOW)]
        + [pltpu.VMEM(*one) for one in taken + made]
        + [
            pltpu.VMEM((wide, D), LOW),
            pltpu.VMEM((wide, D), LOW),
            pltpu.VMEM((rows, D), LOW),
            pltpu.VMEM((rows, wide), F32),
            pltpu.VMEM((rows, D), LOW),
            pltpu.VMEM((D, D + PAIR), LOW),
            dma(7),
            dma(3 * blocks),
        ],
        compiler_params=params(28),
        cost_estimate=cost(8e9, 1.5e7),
    )(place, near, *returned, gain2, w_control, hidden, cot, mix, attended, w_out)


def pair_call(near, queries, keys, values, pulls, normed):
    rows = normed.shape[0]
    half = shape(D // 2, 3 * PAIRS * PAIR)
    return pl.pallas_call(
        pair_kernel,
        in_specs=[smem()] + [far()] * 5,
        out_specs=[far()] + [vmem()] * 2,
        out_shape=[shape(PAIRS, rows, 3 * PAIR), half, half],
        scratch_shapes=[pltpu.VMEM((HEADS, rows, PAIR), LOW)] * 4
        + [
            pltpu.VMEM((rows, D), LOW),
            pltpu.VMEM((PAIRS, rows, 3 * PAIR), LOW),
            pltpu.VMEM((rows, PAIR), F32),
            pltpu.VMEM((D, 3 * PAIRS * PAIR), LOW),
            dma(4 * PAIRS + 1),
            dma(PAIRS),
        ],
        compiler_params=params(32),
        cost_estimate=cost(2e10, 1.2e7),
    )(near, queries, keys, values, pulls, normed)


def weight_call(expert, copy, pieces, w_up, w_down, copies, earlier):
    ff = w_up.shape[2]
    held = sum(piece.shape[0] for piece in pieces)
    every = held // (2 * EXP_DEV)
    whole = [pl.BlockSpec(one.shape, lambda f: (0, 0)) for one in pieces]
    return pl.pallas_call(
        functools.partial(weight_kernel, expert, len(pieces)),
        grid=(ff // FF_BLOCK,),
        in_specs=[smem()]
        + whole
        + [
            pl.BlockSpec((1, D, FF_BLOCK), lambda f: (expert, 0, f)),
            pl.BlockSpec((1, FF_BLOCK, D), lambda f: (expert, f, 0)),
        ]
        + [far()] * len(earlier),
        out_specs=[
            pl.BlockSpec((1, D // copies, FF_BLOCK), lambda f: (expert, 0, f)),
            pl.BlockSpec((1, ff // copies, D), lambda f: (expert, 0, 0)),
        ],
        out_shape=[
            shape(EXP_DEV, D // copies, ff, kind=F32),
            shape(EXP_DEV, ff // copies, D, kind=F32),
        ],
        scratch_shapes=[
            pltpu.VMEM((every, D), LOW),
            pltpu.VMEM((every, D), LOW),
            pltpu.VMEM((FF_BLOCK, D), F32),
        ],
        input_output_aliases={3 + len(pieces) + i: i for i in range(len(earlier))},
        compiler_params=params(40),
        cost_estimate=cost(1e10, 8e6),
    )(copy, *pieces, w_up, w_down, *earlier)


def last_call(grads, tokens, grad_hidden, gain1, weights):
    rows = tokens.shape[0]
    row_block = lambda i: (i, 0)
    fixed = lambda i: (0, 0)
    return pl.pallas_call(
        last_kernel,
        grid=(rows // BLOCK,),
        in_specs=[pl.BlockSpec((PAIRS, BLOCK, 3 * PAIR), lambda i: (0, i, 0))]
        + [pl.BlockSpec((BLOCK, D), row_block)] * 2
        + [pl.BlockSpec((1, D), fixed)]
        + [pl.BlockSpec((D, D), fixed)] * 3,
        out_specs=pl.BlockSpec((BLOCK, D), row_block),
        out_shape=shape(rows, D),
        compiler_params=params(32),
        cost_estimate=cost(2e9, 8e6),
    )(grads, tokens, grad_hidden, gain1, *weights)


def join_call(*parts):
    rows = parts[0].shape[0]
    return pl.pallas_call(
        join_kernel,
        in_specs=[vmem()] * 4,
        out_specs=vmem(),
        out_shape=shape(rows, parts[0].shape[1] + parts[2].shape[1]),
        compiler_params=params(16),
        cost_estimate=cost(1e6, 3e6),
    )(*parts)


def total_call(parts):
    return pl.pallas_call(
        total_kernel,
        in_specs=[vmem()],
        out_specs=vmem(),
        out_shape=shape(*parts.shape),
        compiler_params=params(16),
        cost_estimate=cost(1e6, 3e6),
    )(parts)


def half_call(step, near, both, weights, earlier):
    square = shape(D, D, kind=F32)
    half = D // 2
    return pl.pallas_call(
        functools.partial(half_kernel, step),
        in_specs=[smem(), vmem()] + [far()] * (3 + len(earlier)),
        out_specs=[far()] * 4 + [vmem()],
        out_shape=[square] * 4 + [shape(half, PAIR, kind=F32)],
        scratch_shapes=[
            pltpu.VMEM((4, half, D), F32),
            pltpu.VMEM((3, half, D), LOW),
            dma(3),
            dma(4),
        ],
        input_output_aliases={5 + i: i for i in range(len(earlier))},
        compiler_params=params(40),
        cost_estimate=cost(1e8, 6e6),
    )(near, both, *weights, *earlier)


def small_call(near, own, other, gain1, experts):
    return pl.pallas_call(
        small_kernel,
        in_specs=[smem()] + [vmem()] * 3,
        out_specs=[vmem()] * 3,
        out_shape=[shape(experts, D, kind=F32)] + [shape(1, D, kind=F32)] * 2,
        scratch_shapes=[pltpu.VMEM((D, PAIR), F32)],
        compiler_params=params(16),
        cost_estimate=cost(1e6, 1e6),
    )(near, own, other, gain1)


def in_order(*values):
    return lax.optimization_barrier(values)


def shards(
    tokens,
    doc_lengths,
    group_order,
    ln1_gain,
    w_query,
    w_key,
    w_value,
    w_out,
    ln2_gain,
    w_control,
    w_up,
    w_down,
    cotangent,
):
    copies, far_hosts, near_hosts = (lax.axis_size(name) for name in ("dp", "far", "near"))
    hosts = far_hosts * near_hosts
    hosts_axes = ("far", "near")
    axes = ("dp", "far")
    count = copies * far_hosts
    experts = hosts * EXP_DEV
    place = lax.axis_index(hosts_axes).astype(jnp.int32).reshape(1)
    near = lax.axis_index("near").astype(jnp.int32).reshape(1)
    copy = lax.axis_index("dp").astype(jnp.int32).reshape(1)
    gain1 = ln1_gain.reshape(1, D)
    gain2 = ln2_gain.reshape(1, D)
    weights = (w_query, w_key, w_value)
    w_control = w_control.T
    ahead, behind = ring_of(copies)
    steps_left = copies // 2 - 1
    pieces = []

    def exchange(parts):
        return [parts[0]] + [
            lax.ppermute(parts[step], hosts_axes, [(i, i ^ step) for i in range(hosts)])
            for step in range(1, hosts)
        ]

    def pass_on(ahead_part, behind_part):
        return lax.ppermute(ahead_part, "dp", ahead), lax.ppermute(behind_part, "dp", behind)

    def next_step(moving):
        nonlocal steps_left
        pieces.extend(moving)
        steps_left -= 1
        if steps_left > 0:
            return pass_on(*moving)
        half = moving[0].shape[0] // 2
        return pass_on(moving[0][:half], moving[1][half:])

    def near_swap(values):
        return lax.ppermute(values, "near", [(i, i ^ 1) for i in range(near_hosts)])

    def scatter(half):
        rows, cols = half.shape
        return lax.all_to_all(half.reshape(count, rows // count, cols), axes, 0, 0, tiled=True)

    def spread(own):
        return lax.all_to_all(own, axes, 0, 0, tiled=True).reshape(-1, own.shape[-1])

    with jax.named_scope("attention_and_mixing"):
        sends, kept = forward_call(
            doc_lengths,
            place,
            group_order,
            gain1,
            gain2,
            tokens,
            cotangent,
            (*weights, w_out),
            w_control,
            experts,
        )
        hidden, mix, normed, queries, keys, values, attended = kept
    with jax.named_scope("to_experts"):
        arrived = exchange(sends)
    with jax.named_scope("gather_for_weights"):
        own = jnp.concatenate(arrived, axis=0)
        pieces.append(own)
        moving = pass_on(own, own)
    with jax.named_scope("experts"):
        results = expert_call(arrived, w_up, w_down)
    with jax.named_scope("from_experts"):
        returned = exchange(results)
    with jax.named_scope("gather_for_weights"):
        moving = next_step(moving)
    with jax.named_scope("mixing_backward"):
        output, grad_hidden, pulls, mine_out, other_out = middle_call(
            place, near, returned, gain2, w_control, hidden, cotangent, mix, attended, w_out
        )
    with jax.named_scope("gather_for_weights"):
        pulls, other_out, moving = in_order(pulls, other_out, moving)
        moving = next_step(moving)
    with jax.named_scope("reduce"):
        swapped_out = near_swap(other_out)
    with jax.named_scope("attention_backward"):
        grads, mine, other = pair_call(near, queries, keys, values, pulls, normed)
        mine, other, moving, swapped_out = in_order(mine, other, moving, swapped_out)
    with jax.named_scope("gather_for_weights"):
        while steps_left > 0:
            moving = next_step(moving)
    with jax.named_scope("reduce"):
        sums = join_call(mine_out, swapped_out, mine, near_swap(other))
        sums, grads, moving = in_order(sums, grads, moving)
        pieces.extend(moving)
        sums = scatter(sums)
    with jax.named_scope("norm_backward"):
        grad_tokens = last_call(grads, tokens, grad_hidden, gain1, weights)
    with jax.named_scope("expert_weights"):
        grads_expert = weight_call(0, copy, pieces, w_up, w_down, copies, ())
        sums, grads_expert, grad_tokens = in_order(sums, grads_expert, grad_tokens)
    with jax.named_scope("reduce"):
        sums = total_call(sums)
        sums, grads_expert = in_order(sums, grads_expert)
        sums = spread(sums)
    with jax.named_scope("expert_weights"):
        grad_up, grad_down = weight_call(1, copy, pieces, w_up, w_down, copies, grads_expert)
        sums, grad_up, grad_down = in_order(sums, grad_up, grad_down)
    with jax.named_scope("reduce"):
        sums_other = near_swap(sums)
    with jax.named_scope("assemble"):
        *squares, own_columns = half_call(0, near, sums, weights, ())
        *squares, other_columns = half_call(1, near, sums_other, weights, squares)
        grad_query, grad_key, grad_value, grad_out = squares
        grad_control, grad_gain1, grad_gain2 = small_call(
            near, own_columns, other_columns, gain1, experts
        )
    return (
        output,
        grad_tokens,
        grad_gain1.reshape(D),
        grad_query,
        grad_key,
        grad_value,
        grad_out,
        grad_gain2.reshape(D),
        grad_control.T,
        grad_up,
        grad_down,
    )


def solution(mesh):
    copies, hosts = mesh.shape["dp"], mesh.shape["expert"]
    finer = jax.sharding.Mesh(mesh.devices.reshape(copies, hosts // 2, 2), ("dp", "far", "near"))
    every = P(("dp", "far", "near"), None)
    expert = P(("far", "near"), None, None)
    sliced = P(("far", "near"), "dp", None)
    return jax.shard_map(
        shards,
        mesh=finer,
        in_specs=(every,) * 3 + (P(),) * 7 + (expert,) * 2 + (every,),
        out_specs=(every,) * 2 + (P(),) * 7 + (sliced,) * 2,
        check_vma=False,
    )
```
